32 devices in a mesh: seq: 8 (over y, x, core), mlp: 4 (over z).
Axes of the slice: x: 2, y: 2, z: 4, core: 2. Of those that a mesh axis runs over, the one named last changes fastest.
Arguments:
- tokens: bfloat16 [8, 4, 256, 1024], P('seq'), may hold values from -6 to 6
- ln_gain: float32 [1024], replicated, may hold values from 0.5 to 1.5
- ln_bias: float32 [1024], replicated, may hold values from -3 to 3
- w_query: bfloat16 [1024, 1024], P(None, 'mlp'), may hold values from -0.1875 to 0.1875
- w_key: bfloat16 [1024, 1024], P(None, 'mlp'), may hold values from -0.1875 to 0.1875
- w_value: bfloat16 [1024, 1024], P(None, 'mlp'), may hold values from -0.1875 to 0.1875
- w_attn_out: bfloat16 [1024, 1024], P('mlp'), may hold values from -6 to 6
- w_in: bfloat16 [1024, 4096], P(None, 'mlp'), may hold values from -0.1875 to 0.1875
- b_in: float32 [4096], P('mlp'), may hold values from -3 to 3
- w_mlp_out: bfloat16 [4096, 1024], P('mlp'), may hold values from -0.09375 to 0.09375
- b_out: float32 [1024], replicated, may hold values from -3 to 3
- cotangent: bfloat16 [8, 4, 256, 1024], P('seq'), may hold values from -6 to 6
Outputs:
- mixed: bfloat16 [8, 4, 256, 1024], P('seq')
- d_tokens: bfloat16 [8, 4, 256, 1024], P('seq')
- d_ln_gain: float32 [1024], replicated
- d_ln_bias: float32 [1024], replicated
- d_w_query: float32 [1024, 1024], P(None, 'mlp')
- d_w_key: float32 [1024, 1024], P(None, 'mlp')
- d_w_value: float32 [1024, 1024], P(None, 'mlp')
- d_w_attn_out: float32 [1024, 1024], P('mlp')
- d_w_in: float32 [1024, 4096], P(None, 'mlp')
- d_b_in: float32 [4096], P('mlp')
- d_w_mlp_out: float32 [4096, 1024], P('mlp')
- d_b_out: float32 [1024], replicated
The draws below stay inside these ranges and needn't reach their ends.
All inputs are finite; a program needn't handle non-finite values.
Results may differ from the reference program's by a relative error of at most 0.02.
Values may be sent and summed in bfloat16 or wider, within the bound.
No kernel may reach another device: no remote copies, remote signals or barrier semaphores. Data moves between devices by JAX's collectives and lax.ppermute only.
A program may use at most 192 MiB of HBM per device.

```python
import math
import jax
import jax.numpy as jnp
from jax import lax

D = 1024
HEADS = 16
HEAD_DIM = 64
ROT = 32
FF = 4096
TOK_DEV = 256
SEQS_DEV = 4
SHARDS = 8
LENGTH = 2048
GROUPS = 1
BLOCKS = 8
SEQS = 4


def block_scale(key, dims, pieces, least, high):
    loudness, own = 1.0, jax.random.fold_in(key, 6)
    for axis_at, blocks in pieces:
        steps = jnp.exp(jax.random.uniform(jax.random.fold_in(own, axis_at), (blocks,), jnp.float32, least / len(pieces), high / len(pieces)))
        loudness = loudness * jnp.repeat(steps, dims[axis_at] // blocks).reshape([-1 if axis == axis_at else 1 for axis in range(len(dims))])
    return loudness


def scatter_about(stream_key, extent, deviation, reach, cuts=(), kind=jnp.bfloat16):
    array = jax.random.normal(stream_key, extent, jnp.float32) * deviation
    if len(cuts) > 0:
        array = block_scale(stream_key, extent, cuts, -0.22, 0.18) * array
    return jnp.clip(array, min=-reach, max=reach).astype(kind)


def setup_inputs(seed: int = 0) -> dict:
    arg_keys = jax.random.split(jax.random.key(seed), 13)
    tokens = scatter_about(arg_keys[0], (BLOCKS, SEQS_DEV, TOK_DEV, D), 1.0, 6.0, ((0, 8),))
    ln_gain = jnp.clip(1.0 + 0.1 * jax.random.normal(arg_keys[1], (D,), jnp.float32), 0.5, 1.5)
    ln_bias = scatter_about(arg_keys[2], (D,), 0.5, 3.0, (), jnp.float32)
    w_query = scatter_about(arg_keys[3], (D, D), D ** -0.5, 0.1875, ((1, 4),))
    w_key = scatter_about(arg_keys[4], (D, D), D ** -0.5, 0.1875, ((1, 4),))
    w_value = scatter_about(arg_keys[5], (D, D), D ** -0.5, 0.1875, ((1, 4),))
    w_attn_out = scatter_about(arg_keys[6], (D, D), ((LENGTH // 8) ** 0.5 * D ** -0.5), 6.0, ((0, 4),))
    w_in = scatter_about(arg_keys[7], (D, FF), D ** -0.5, 0.1875, ((1, 4),))
    b_in = scatter_about(arg_keys[8], (FF,), 0.5, 3.0, ((0, 4),), jnp.float32)
    w_mlp_out = scatter_about(arg_keys[9], (FF, D), FF ** -0.5, 0.09375, ((0, 4),))
    b_out = scatter_about(arg_keys[10], (D,), 0.5, 3.0, (), jnp.float32)
    cotangent = scatter_about(arg_keys[11], (BLOCKS, SEQS_DEV, TOK_DEV, D), 1.0, 6.0, ((0, 8),))
    return dict(tokens=tokens, ln_gain=ln_gain, ln_bias=ln_bias, w_query=w_query, w_key=w_key, w_value=w_value, w_attn_out=w_attn_out, w_in=w_in, b_in=b_in, w_mlp_out=w_mlp_out, b_out=b_out, cotangent=cotangent)


@jax.custom_vjp
def low(v):
    return lax.optimization_barrier(v.astype(jnp.bfloat16)).astype(jnp.float32)

@jax.custom_vjp
def low_back(v):
    return v

def low_keep(v):
    return (low(v), None)

def low_pass(kept, grad):
    return (grad,)

def back_keep(v):
    return (v, None)

def back_low(kept, grad):
    return (low(grad),)
low.defvjp(low_keep, low_pass)
low_back.defvjp(back_keep, back_low)
epsilon = 1e-05
neg_big = -1e+30
highest = lax.Precision.HIGHEST

def rotary_tables(positions, model_width, head_size, rotary):
    column = jnp.arange(model_width, dtype=jnp.int32) % head_size
    pairs = (column // 2).astype(jnp.float32)
    freq = 10000.0 ** (-2.0 * pairs / rotary)
    angle = positions.astype(jnp.float32)[:, None] * freq[None, :]
    active = (column < rotary)[None, :]
    cosine = jnp.where(active, jnp.cos(angle), 1.0)
    sine_table = jnp.where(active, jnp.sin(angle), 0.0)
    row_ids = jnp.arange(model_width, dtype=jnp.int32)[:, None]
    col_ids = jnp.arange(model_width, dtype=jnp.int32)[None, :]
    inside = col_ids % head_size < rotary
    lower = inside & (col_ids % 2 == 0) & (row_ids == col_ids + 1)
    upper = inside & (col_ids % 2 == 1) & (row_ids == col_ids - 1)
    swapper = jnp.where(lower, -1.0, jnp.where(upper, 1.0, 0.0)).astype(jnp.float32)
    return (cosine, sine_table, swapper)

def attention(query_seq, keys_seq, values_seq):
    block_rows = math.gcd(LENGTH, 512)
    block_count = LENGTH // block_rows
    score_scale = HEAD_DIM ** (-0.5)
    key_pos = jnp.arange(LENGTH, dtype=jnp.int32)
    keys_heads = keys_seq.reshape(LENGTH, HEADS, HEAD_DIM)
    values_heads = values_seq.reshape(LENGTH, HEADS, HEAD_DIM)

    @jax.checkpoint
    def one_block(block_index):
        first_row = (block_index * block_rows).astype(jnp.int32)
        query_block = lax.dynamic_slice_in_dim(query_seq, first_row, block_rows, 0)
        query_block = query_block.reshape(block_rows, HEADS, HEAD_DIM)
        raw_scores = jnp.einsum('qhd,khd->hqk', query_block, keys_heads, precision=highest) * score_scale
        raw_scores = low_back(raw_scores)
        query_pos = first_row + jnp.arange(block_rows, dtype=jnp.int32)
        causal_mask = (query_pos[:, None] >= key_pos[None, :])[None]
        probs = jax.nn.softmax(jnp.where(causal_mask, raw_scores, neg_big), axis=-1)
        attended = jnp.einsum('hqk,khd->qhd', low(probs), values_heads, precision=highest)
        return attended.reshape(block_rows, D)
    blocks_out = lax.map(one_block, jnp.arange(block_count, dtype=jnp.int32))
    return blocks_out.reshape(LENGTH, D)

def layer(inputs_wide, gain, bias, w_q, w_k, w_v, w_o, w_up, inner_bias, w_down, outer_bias):
    average = lax.optimization_barrier(jnp.mean(inputs_wide, -1, keepdims=True))
    centred = inputs_wide - average
    inv_std = lax.rsqrt(lax.optimization_barrier(jnp.mean(centred * centred, -1, keepdims=True)) + epsilon)
    unit = centred * inv_std
    normed = low(unit * gain + bias)
    cosine, sine_table, swapper = rotary_tables(jnp.arange(LENGTH, dtype=jnp.int32), D, HEAD_DIM, ROT)

    def rope(vectors):
        return vectors * cosine + jnp.dot(vectors, swapper, precision=highest) * sine_table
    query = low(low_back(rope(low_back(jnp.dot(normed, w_q, precision=highest)))))
    keys = low(low_back(rope(low_back(jnp.dot(normed, w_k, precision=highest)))))
    values = low(low_back(jnp.dot(normed, w_v, precision=highest)))
    attended = low(low_back(attention(query, keys, values)))
    attn_branch = jnp.dot(attended, w_o, precision=highest)
    gate_in = low_back(jnp.dot(normed, w_up, precision=highest) + inner_bias)
    hidden = low(jax.nn.gelu(gate_in, approximate=True))
    mlp_branch = jnp.dot(hidden, w_down, precision=highest) + outer_bias
    return inputs_wide + attn_branch + mlp_branch

def to_rows(blocks):
    grouped = blocks.reshape(GROUPS, SHARDS, SEQS_DEV, TOK_DEV, D)
    return jnp.transpose(grouped, (0, 2, 1, 3, 4)).reshape(SEQS, LENGTH, D)

def to_blocks(rows):
    grouped = rows.reshape(GROUPS, SEQS_DEV, SHARDS, TOK_DEV, D)
    return jnp.transpose(grouped, (0, 2, 1, 3, 4)).reshape(BLOCKS, SEQS_DEV, TOK_DEV, D)

def reference(tokens, ln_gain, ln_bias, w_query, w_key, w_value, w_attn_out, w_in, b_in, w_mlp_out, b_out, cotangent):
    params = [a.astype(jnp.float32) for a in (ln_gain, ln_bias, w_query, w_key, w_value, w_attn_out, w_in, b_in, w_mlp_out, b_out)]
    rows_in = to_rows(tokens.astype(jnp.float32))
    rows_cot = to_rows(cotangent.astype(jnp.float32))

    def seq_step(totals, item):
        seq_in, seq_cot = item
        output, pullback = jax.vjp(layer, seq_in, *params)
        grads = pullback(seq_cot)
        totals = tuple((t + g for t, g in zip(totals, grads[1:])))
        return (totals, (output.astype(jnp.bfloat16), grads[0].astype(jnp.bfloat16)))
    start = tuple((jnp.zeros_like(p) for p in params))
    totals, (outputs, input_grads) = lax.scan(seq_step, start, (rows_in, rows_cot))
    return (to_blocks(outputs), to_blocks(input_grads), totals[0], totals[1], totals[2], totals[3], totals[4], totals[5], totals[6], totals[7], totals[8], totals[9])
```

```python
from functools import partial

import jax
import jax.numpy as jnp
from jax import lax
from jax.experimental import pallas as pl
from jax.experimental.pallas import tpu as pltpu
from jax.sharding import PartitionSpec as P

HEAD_DIM = 64
ROT = 32

epsilon = 1e-05
neg_big = -1e30
bf16 = jnp.bfloat16
f32 = jnp.float32


def passed_along(x, axis, by):
    peers = lax.axis_size(axis)
    pairs = [(i, i + by) for i in range(peers) if 0 <= i + by < peers]
    return lax.ppermute(x, axis, pairs)


def rotary_tables(positions, width):
    column = jnp.arange(width, dtype=jnp.int32) % HEAD_DIM
    pairs = (column // 2).astype(f32)
    freq = 10000.0 ** (-2.0 * pairs / ROT)
    angle = positions.astype(f32)[:, None] * freq[None, :]
    active = (column < ROT)[None, :]
    even = (column % 2 == 0)[None, :]
    cosine = jnp.where(active, jnp.cos(angle), 1.0)
    sine = jnp.where(active, jnp.sin(angle), 0.0)
    return cosine, jnp.where(even, -sine, 0.0), jnp.where(even, 0.0, sine)


def rotate(v, tables, sign):
    cosine, from_right, from_left = tables
    right = jnp.concatenate([v[..., 1:], v[..., :1]], -1)
    left = jnp.concatenate([v[..., -1:], v[..., :-1]], -1)
    return v * cosine + sign * (right * from_right + left * from_left)


def attention_kernel(x_ref, out_ref, xt, acc, sbuf, *, length, hd, tq, tk):
    xt[...] = x_ref[0].T
    acc[...] = jnp.zeros_like(acc)
    scale = hd**-0.5
    nt = (((1,), (1,)), ((), ()))
    zero = jnp.zeros((hd, tq), bf16)
    for i in range(length // tq):
        cols = slice(i * tq, (i + 1) * tq)
        span = (i + 1) * tq
        qs = (xt[0:hd, cols].astype(f32) * scale).astype(bf16)
        at = xt[3 * hd : 4 * hd, cols].astype(f32)
        zq = jnp.concatenate([zero, qs], 0)
        qz = jnp.concatenate([qs, zero], 0)
        steps = [(k0, min(k0 + tk, span)) for k0 in range(0, span, tk)]
        top = None
        for k0, k1 in steps:
            st = jnp.dot(x_ref[0, k0:k1, 0 : 2 * hd], zq, preferred_element_type=f32)
            if k1 > i * tq:
                kp = lax.broadcasted_iota(jnp.int32, st.shape, 0) + k0
                qp = lax.broadcasted_iota(jnp.int32, st.shape, 1) + i * tq
                st = jnp.where(kp <= qp, st, neg_big)
            sbuf[k0:k1, :] = st
            m = jnp.max(st, 0, keepdims=True)
            top = m if top is None else jnp.maximum(top, m)
        tot = None
        ot = None
        for k0, k1 in steps:
            e = jnp.exp(sbuf[k0:k1, :] - top)
            sbuf[k0:k1, :] = e
            s = jnp.sum(e, 0, keepdims=True)
            o = jnp.dot(xt[2 * hd : 3 * hd, k0:k1], e.astype(bf16), preferred_element_type=f32)
            tot = s if tot is None else tot + s
            ot = o if ot is None else ot + o
        r = 1.0 / tot
        ot = ot * r
        ar = (at * r).astype(bf16)
        spread = jnp.sum(ar.astype(f32) * ot, 0, keepdims=True)
        az = jnp.concatenate([ar, zero], 0)
        za = jnp.concatenate([zero, ar], 0)
        dqt = None
        for k0, k1 in steps:
            dp = jnp.dot(x_ref[0, k0:k1, 2 * hd : 4 * hd], az, preferred_element_type=f32)
            e = sbuf[k0:k1, :]
            ds = (e * (dp - spread)).astype(bf16)
            d = jnp.dot(xt[hd : 2 * hd, k0:k1], ds, preferred_element_type=f32)
            dqt = d if dqt is None else dqt + d
            acc[k0:k1, :] += lax.dot_general(ds, qz, nt, preferred_element_type=f32) + lax.dot_general(
                e.astype(bf16), za, nt, preferred_element_type=f32
            )
        both = jnp.concatenate([ot, dqt * scale], 0)
        out_ref[0, cols, 0 : 2 * hd] = both.T.astype(bf16)
    out_ref[0, :, 2 * hd : 4 * hd] = acc[...].astype(bf16)


def attention(x):
    n, length, width = x.shape
    hd = width // 4
    tq = 512 if length % 512 == 0 else 256
    tk = 512
    spec = pl.BlockSpec((1, length, width), lambda i: (i, 0, 0))
    return pl.pallas_call(
        partial(attention_kernel, length=length, hd=hd, tq=tq, tk=tk),
        grid=(n,),
        out_shape=jax.ShapeDtypeStruct(x.shape, bf16),
        in_specs=[spec],
        out_specs=spec,
        scratch_shapes=[
            pltpu.VMEM((width, length), bf16),
            pltpu.VMEM((length, 2 * hd), f32),
            pltpu.VMEM((length, tq), f32),
        ],
        compiler_params=pltpu.CompilerParams(vmem_limit_bytes=40 * 2**20),
        cost_estimate=pl.CostEstimate(
            flops=n * length * length * 4 * hd * 6, bytes_accessed=4 * n * length * width, transcendentals=n * length * length // 2
        ),
    )(x)


def exchange_attention(q, k, v, a):
    seqs, rows, inner = q.shape
    shards = lax.axis_size("seq")
    heads = inner // HEAD_DIM
    chunks = seqs * heads // shards
    wide = 4 * HEAD_DIM
    packed = jnp.stack([x.reshape(seqs, rows, heads, HEAD_DIM) for x in (q, k, v, a)], 3)
    packed = packed.reshape(seqs, rows, heads, wide).transpose(0, 2, 1, 3).reshape(chunks, shards, rows, wide)
    outs = []
    for c in range(chunks):
        mine = lax.all_to_all(packed[c], "seq", 0, 0, tiled=True)
        done = attention(mine.reshape(1, shards * rows, wide)).reshape(shards, rows, wide)
        outs.append(lax.all_to_all(done, "seq", 0, 0, tiled=True))
    back = jnp.concatenate(outs, 0).reshape(seqs, heads, rows, 4, HEAD_DIM).transpose(3, 0, 2, 1, 4)
    back = back.reshape(4, seqs, rows, inner)
    return back[0], back[1], back[2], back[3]


def ring_attention(q, k, v, a):
    seq_count, row_count, inner_width = q.shape
    score_scale = HEAD_DIM ** (-0.5)
    shard_total = lax.axis_size("seq")
    my_shard = lax.axis_index("seq")
    heads_of = lambda x: x.reshape(seq_count, row_count, inner_width // HEAD_DIM, HEAD_DIM)
    flat_of = lambda x: x.reshape(seq_count, row_count, inner_width)
    qh, gh = heads_of(q), heads_of(a)
    local = jnp.arange(row_count, dtype=jnp.int32)
    own_mask = local[:, None] >= local[None, :]
    ein = partial(jnp.einsum, preferred_element_type=f32)

    def attend_block(state, key_block, value_block, visible):
        running_max, exp_total, weighted = state
        raw = ein("sthd,suhd->shtu", qh, key_block) * score_scale
        raw = jnp.where(visible[None, None], raw, neg_big)
        new_max = jnp.maximum(running_max, jnp.max(raw, -1))
        weights = jnp.where(visible[None, None], jnp.exp(raw - new_max[..., None]), 0.0)
        shrink = jnp.exp(running_max - new_max)
        exp_total = exp_total * shrink + jnp.sum(weights, -1)
        weighted = weighted * jnp.transpose(shrink, (0, 2, 1))[..., None] + ein(
            "shtu,suhd->sthd", weights.astype(bf16), value_block
        )
        return (new_max, exp_total, weighted)

    head_count = inner_width // HEAD_DIM
    state = (
        jnp.full((seq_count, head_count, row_count), neg_big, f32),
        jnp.zeros((seq_count, head_count, row_count), f32),
        jnp.zeros(qh.shape, f32),
    )
    state = attend_block(state, heads_of(k), heads_of(v), own_mask)
    empty_stack = jnp.zeros((max(shard_total - 1, 1),) + q.shape, bf16)

    def forward_step(step, carry):
        state, near_keys, near_values, key_stack, value_stack = carry
        near_keys, near_values = passed_along((near_keys, near_values), "seq", 1)
        visible = jnp.broadcast_to(my_shard >= step, (row_count, row_count))
        state = attend_block(state, heads_of(near_keys), heads_of(near_values), visible)
        key_stack = lax.dynamic_update_index_in_dim(key_stack, near_keys, step - 1, 0)
        value_stack = lax.dynamic_update_index_in_dim(value_stack, near_values, step - 1, 0)
        return (state, near_keys, near_values, key_stack, value_stack)

    state, _, _, key_stack, value_stack = lax.fori_loop(
        1, shard_total, forward_step, (state, k, v, empty_stack, empty_stack)
    )
    running_max, exp_total, weighted = state
    log_total = running_max + jnp.log(exp_total)
    attended = weighted / jnp.transpose(exp_total, (0, 2, 1))[..., None]
    spread = jnp.transpose(jnp.sum(gh.astype(f32) * attended, -1), (0, 2, 1))

    def grads(key_block, value_block, visible):
        raw = ein("sthd,suhd->shtu", qh, key_block) * score_scale
        probs = jnp.where(visible[None, None], jnp.exp(raw - log_total[..., None]), 0.0)
        grad_probs = ein("sthd,suhd->shtu", gh, value_block)
        slopes = (probs * (grad_probs - spread[..., None])).astype(bf16)
        query_grad = ein("shtu,suhd->sthd", slopes, key_block) * score_scale
        key_grad = ein("shtu,sthd->suhd", slopes, qh) * score_scale
        value_grad = ein("shtu,sthd->suhd", probs.astype(bf16), gh)
        return query_grad, key_grad, value_grad

    d_query, d_keys, d_values = grads(heads_of(k), heads_of(v), own_mask)

    def return_step(index, carry):
        query_grad_total, travelling = carry
        step = shard_total - 1 - index
        near_keys = lax.dynamic_index_in_dim(key_stack, step - 1, 0, keepdims=False)
        near_values = lax.dynamic_index_in_dim(value_stack, step - 1, 0, keepdims=False)
        visible = jnp.broadcast_to(my_shard >= step, (row_count, row_count))
        query_grad, key_grad, value_grad = grads(heads_of(near_keys), heads_of(near_values), visible)
        joined = jnp.concatenate([flat_of(key_grad), flat_of(value_grad)], -1)
        travelling = passed_along((travelling + joined).astype(bf16), "seq", -1).astype(f32)
        return (query_grad_total + query_grad, travelling)

    start = jnp.zeros((seq_count, row_count, 2 * inner_width), f32)
    d_query, travelling = lax.fori_loop(0, shard_total - 1, return_step, (d_query, start))
    d_keys = flat_of(d_keys) + travelling[..., :inner_width]
    d_values = flat_of(d_values) + travelling[..., inner_width:]
    return tuple(x.astype(bf16) for x in (flat_of(attended), flat_of(d_query), d_keys, d_values))


def per_device(
    tokens, ln_gain, ln_bias, w_query, w_key, w_value, w_attn_out, w_in, b_in, w_mlp_out, b_out, cotangent
):
    x_low = tokens[0]
    cot = cotangent[0]
    seqs, rows, width = x_low.shape
    inner = w_query.shape[1]
    heads = inner // HEAD_DIM
    shards = lax.axis_size("seq")
    my_shard = lax.axis_index("seq")
    ein = partial(jnp.einsum, preferred_element_type=f32)
    positions = my_shard * rows + jnp.arange(rows, dtype=jnp.int32)
    tables = rotary_tables(positions, inner)
    x = x_low.astype(f32)
    centred = x - jnp.mean(x, -1, keepdims=True)
    inv_std = lax.rsqrt(jnp.mean(centred * centred, -1, keepdims=True) + epsilon)
    unit = centred * inv_std
    normed = (unit * ln_gain + ln_bias).astype(bf16)
    query = rotate(ein("std,de->ste", normed, w_query), tables, 1.0).astype(bf16)
    keys = rotate(ein("std,de->ste", normed, w_key), tables, 1.0).astype(bf16)
    values = ein("std,de->ste", normed, w_value).astype(bf16)
    d_attended = ein("std,ed->ste", cot, w_attn_out).astype(bf16)

    exchange = exchange_attention if (seqs * heads) % shards == 0 else ring_attention
    attended, d_query, d_keys, d_values = exchange(query, keys, values, d_attended)

    gate_in = ein("std,df->stf", normed, w_in) + b_in
    hidden, gelu_pull = jax.vjp(partial(jax.nn.gelu, approximate=True), gate_in)
    hidden = hidden.astype(bf16)
    d_hidden = ein("std,fd->stf", cot, w_mlp_out)
    d_gate = gelu_pull(d_hidden)[0].astype(bf16)
    d_b_in = jnp.sum(d_gate, (0, 1), dtype=f32)
    d_b_out = jnp.sum(cot, (0, 1), dtype=f32)
    d_w_mlp_out = ein("stf,std->fd", hidden, cot)
    d_w_in = ein("std,stf->df", normed, d_gate)
    mlp_part = ein("stf,fd->std", hidden, w_mlp_out)
    d_normed_mlp = ein("stf,df->std", d_gate, w_in)

    attn_part = ein("ste,ed->std", attended, w_attn_out)
    branches = lax.psum((attn_part + mlp_part).astype(bf16), "mlp").astype(f32)
    mixed = (x + branches + b_out).astype(bf16)
    d_w_attn_out = ein("ste,std->ed", attended, cot)
    d_query_pre = rotate(d_query.astype(f32), tables, -1.0).astype(bf16)
    d_key_pre = rotate(d_keys.astype(f32), tables, -1.0).astype(bf16)
    d_w_query = ein("std,ste->de", normed, d_query_pre)
    d_w_key = ein("std,ste->de", normed, d_key_pre)
    d_w_value = ein("std,ste->de", normed, d_values)
    d_normed_part = d_normed_mlp + ein("ste,de->std", d_query_pre, w_query)
    d_normed_part = d_normed_part + ein("ste,de->std", d_key_pre, w_key)
    d_normed_part = d_normed_part + ein("ste,de->std", d_values, w_value)
    d_normed = lax.psum(d_normed_part.astype(bf16), "mlp").astype(f32)
    d_gain = jnp.sum(d_normed * unit, (0, 1))
    d_bias = jnp.sum(d_normed, (0, 1))
    d_unit = d_normed * ln_gain
    d_inputs = inv_std * (
        d_unit - jnp.mean(d_unit, -1, keepdims=True) - unit * jnp.mean(d_unit * unit, -1, keepdims=True)
    )
    d_tokens = (cot.astype(f32) + d_inputs).astype(bf16)

    def total(v):
        return lax.psum(v.astype(bf16), "seq").astype(f32)

    return (
        mixed[None],
        d_tokens[None],
        total(d_gain),
        total(d_bias),
        total(d_w_query),
        total(d_w_key),
        total(d_w_value),
        total(d_w_attn_out),
        total(d_w_in),
        total(d_b_in),
        total(d_w_mlp_out),
        total(d_b_out),
    )


def solution(mesh):
    rows, whole = P("seq", None, None, None), P()
    cols, down = P(None, "mlp"), P("mlp", None)
    return jax.shard_map(
        per_device,
        mesh=mesh,
        in_specs=(rows, whole, whole, cols, cols, cols, down, cols, P("mlp"), down, whole, rows),
        out_specs=(rows, rows, whole, whole, cols, cols, cols, down, cols, P("mlp"), down, whole),
        check_vma=False,
    )
```

```python
from functools import partial

import jax
import jax.numpy as jnp
import numpy as np
from jax import lax
from jax.experimental import pallas as pl
from jax.experimental.pallas import tpu as pltpu
from jax.sharding import PartitionSpec as P

HEAD_DIM = 64
ROT = 32

epsilon = 1e-05
neg_big = -1e30
bf16 = jnp.bfloat16
f32 = jnp.float32


def passed_along(x, axis, by):
    peers = lax.axis_size(axis)
    pairs = [(i, i + by) for i in range(peers) if 0 <= i + by < peers]
    return lax.ppermute(x, axis, pairs)


def rotary_tables(positions, width):
    column = jnp.arange(width, dtype=jnp.int32) % HEAD_DIM
    pairs = (column // 2).astype(f32)
    freq = 10000.0 ** (-2.0 * pairs / ROT)
    angle = positions.astype(f32)[:, None] * freq[None, :]
    active = (column < ROT)[None, :]
    even = (column % 2 == 0)[None, :]
    cosine = jnp.where(active, jnp.cos(angle), 1.0)
    sine = jnp.where(active, jnp.sin(angle), 0.0)
    return cosine, jnp.where(even, -sine, 0.0), jnp.where(even, 0.0, sine)


def rotate(v, tables, sign):
    cosine, from_right, from_left = tables
    right = jnp.concatenate([v[..., 1:], v[..., :1]], -1)
    left = jnp.concatenate([v[..., -1:], v[..., :-1]], -1)
    return v * cosine + sign * (right * from_right + left * from_left)


def attention_kernel(x_ref, out_ref, xt, acc, sbuf, *, length, hd, tq, tk):
    xt[...] = x_ref[0].T
    acc[...] = jnp.zeros_like(acc)
    scale = hd**-0.5
    nt = (((1,), (1,)), ((), ()))
    zero = jnp.zeros((hd, tq), bf16)
    for i in range(length // tq):
        cols = slice(i * tq, (i + 1) * tq)
        span = (i + 1) * tq
        qs = (xt[0:hd, cols].astype(f32) * scale).astype(bf16)
        at = xt[3 * hd : 4 * hd, cols].astype(f32)
        zq = jnp.concatenate([zero, qs], 0)
        qz = jnp.concatenate([qs, zero], 0)
        steps = [(k0, min(k0 + tk, span)) for k0 in range(0, span, tk)]
        top = None
        for k0, k1 in steps:
            st = jnp.dot(x_ref[0, k0:k1, 0 : 2 * hd], zq, preferred_element_type=f32)
            if k1 > i * tq:
                kp = lax.broadcasted_iota(jnp.int32, st.shape, 0) + k0
                qp = lax.broadcasted_iota(jnp.int32, st.shape, 1) + i * tq
                st = jnp.where(kp <= qp, st, neg_big)
            sbuf[k0:k1, :] = st
            m = jnp.max(st, 0, keepdims=True)
            top = m if top is None else jnp.maximum(top, m)
        tot = None
        ot = None
        for k0, k1 in steps:
            e = jnp.exp(sbuf[k0:k1, :] - top)
            sbuf[k0:k1, :] = e
            s = jnp.sum(e, 0, keepdims=True)
            o = jnp.dot(xt[2 * hd : 3 * hd, k0:k1], e.astype(bf16), preferred_element_type=f32)
            tot = s if tot is None else tot + s
            ot = o if ot is None else ot + o
        r = 1.0 / tot
        ot = ot * r
        ar = (at * r).astype(bf16)
        spread = jnp.sum(ar.astype(f32) * ot, 0, keepdims=True)
        az = jnp.concatenate([ar, zero], 0)
        za = jnp.concatenate([zero, ar], 0)
        dqt = None
        for k0, k1 in steps:
            dp = jnp.dot(x_ref[0, k0:k1, 2 * hd : 4 * hd], az, preferred_element_type=f32)
            e = sbuf[k0:k1, :]
            ds = (e * (dp - spread)).astype(bf16)
            d = jnp.dot(xt[hd : 2 * hd, k0:k1], ds, preferred_element_type=f32)
            dqt = d if dqt is None else dqt + d
            acc[k0:k1, :] += lax.dot_general(ds, qz, nt, preferred_element_type=f32) + lax.dot_general(
                e.astype(bf16), za, nt, preferred_element_type=f32
            )
        both = jnp.concatenate([ot, dqt * scale], 0)
        out_ref[0, cols, 0 : 2 * hd] = both.T.astype(bf16)
    out_ref[0, :, 2 * hd : 4 * hd] = acc[...].astype(bf16)


def attention(x, after=()):
    n, length, width = x.shape
    hd = width // 4
    tq = 512 if length % 512 == 0 else 256
    spec = pl.BlockSpec((1, length, width), lambda i: (i, 0, 0))
    return call(
        partial(attention_kernel, length=length, hd=hd, tq=tq, tk=512),
        (n,),
        (x,),
        [spec],
        spec,
        shape_of(*x.shape),
        7,
        after,
        scratch=[pltpu.VMEM((width, length), bf16), pltpu.VMEM((length, 2 * hd), f32), pltpu.VMEM((length, tq), f32)],
        vmem=32,
        pinned=0,
    )


def ring_attention(q, k, v, a):
    seq_count, row_count, inner_width = q.shape
    score_scale = HEAD_DIM ** (-0.5)
    shard_total = lax.axis_size("seq")
    my_shard = lax.axis_index("seq")
    heads_of = lambda x: x.reshape(seq_count, row_count, inner_width // HEAD_DIM, HEAD_DIM)
    flat_of = lambda x: x.reshape(seq_count, row_count, inner_width)
    qh, gh = heads_of(q), heads_of(a)
    local = jnp.arange(row_count, dtype=jnp.int32)
    own_mask = local[:, None] >= local[None, :]
    ein = partial(jnp.einsum, preferred_element_type=f32)

    def attend_block(state, key_block, value_block, visible):
        running_max, exp_total, weighted = state
        raw = ein("sthd,suhd->shtu", qh, key_block) * score_scale
        raw = jnp.where(visible[None, None], raw, neg_big)
        new_max = jnp.maximum(running_max, jnp.max(raw, -1))
        weights = jnp.where(visible[None, None], jnp.exp(raw - new_max[..., None]), 0.0)
        shrink = jnp.exp(running_max - new_max)
        exp_total = exp_total * shrink + jnp.sum(weights, -1)
        weighted = weighted * jnp.transpose(shrink, (0, 2, 1))[..., None] + ein(
            "shtu,suhd->sthd", weights.astype(bf16), value_block
        )
        return (new_max, exp_total, weighted)

    head_count = inner_width // HEAD_DIM
    state = (
        jnp.full((seq_count, head_count, row_count), neg_big, f32),
        jnp.zeros((seq_count, head_count, row_count), f32),
        jnp.zeros(qh.shape, f32),
    )
    state = attend_block(state, heads_of(k), heads_of(v), own_mask)
    empty_stack = jnp.zeros((max(shard_total - 1, 1),) + q.shape, bf16)

    def forward_step(step, carry):
        state, near_keys, near_values, key_stack, value_stack = carry
        near_keys, near_values = passed_along((near_keys, near_values), "seq", 1)
        visible = jnp.broadcast_to(my_shard >= step, (row_count, row_count))
        state = attend_block(state, heads_of(near_keys), heads_of(near_values), visible)
        key_stack = lax.dynamic_update_index_in_dim(key_stack, near_keys, step - 1, 0)
        value_stack = lax.dynamic_update_index_in_dim(value_stack, near_values, step - 1, 0)
        return (state, near_keys, near_values, key_stack, value_stack)

    state, _, _, key_stack, value_stack = lax.fori_loop(
        1, shard_total, forward_step, (state, k, v, empty_stack, empty_stack)
    )
    running_max, exp_total, weighted = state
    log_total = running_max + jnp.log(exp_total)
    attended = weighted / jnp.transpose(exp_total, (0, 2, 1))[..., None]
    spread = jnp.transpose(jnp.sum(gh.astype(f32) * attended, -1), (0, 2, 1))

    def grads(key_block, value_block, visible):
        raw = ein("sthd,suhd->shtu", qh, key_block) * score_scale
        probs = jnp.where(visible[None, None], jnp.exp(raw - log_total[..., None]), 0.0)
        grad_probs = ein("sthd,suhd->shtu", gh, value_block)
        slopes = (probs * (grad_probs - spread[..., None])).astype(bf16)
        query_grad = ein("shtu,suhd->sthd", slopes, key_block) * score_scale
        key_grad = ein("shtu,sthd->suhd", slopes, qh) * score_scale
        value_grad = ein("shtu,sthd->suhd", probs.astype(bf16), gh)
        return query_grad, key_grad, value_grad

    d_query, d_keys, d_values = grads(heads_of(k), heads_of(v), own_mask)

    def return_step(index, carry):
        query_grad_total, travelling = carry
        step = shard_total - 1 - index
        near_keys = lax.dynamic_index_in_dim(key_stack, step - 1, 0, keepdims=False)
        near_values = lax.dynamic_index_in_dim(value_stack, step - 1, 0, keepdims=False)
        visible = jnp.broadcast_to(my_shard >= step, (row_count, row_count))
        query_grad, key_grad, value_grad = grads(heads_of(near_keys), heads_of(near_values), visible)
        joined = jnp.concatenate([flat_of(key_grad), flat_of(value_grad)], -1)
        travelling = passed_along((travelling + joined).astype(bf16), "seq", -1).astype(f32)
        return (query_grad_total + query_grad, travelling)

    start = jnp.zeros((seq_count, row_count, 2 * inner_width), f32)
    d_query, travelling = lax.fori_loop(0, shard_total - 1, return_step, (d_query, start))
    d_keys = flat_of(d_keys) + travelling[..., :inner_width]
    d_values = flat_of(d_values) + travelling[..., inner_width:]
    return tuple(x.astype(bf16) for x in (flat_of(attended), flat_of(d_query), d_keys, d_values))


def by_ring(
    tokens, ln_gain, ln_bias, w_query, w_key, w_value, w_attn_out, w_in, b_in, w_mlp_out, b_out, cotangent
):
    x_low = tokens[0]
    cot = cotangent[0]
    seqs, rows, width = x_low.shape
    inner = w_query.shape[1]
    my_shard = lax.axis_index("seq")
    ein = partial(jnp.einsum, preferred_element_type=f32)
    positions = my_shard * rows + jnp.arange(rows, dtype=jnp.int32)
    tables = rotary_tables(positions, inner)
    x = x_low.astype(f32)
    centred = x - jnp.mean(x, -1, keepdims=True)
    inv_std = lax.rsqrt(jnp.mean(centred * centred, -1, keepdims=True) + epsilon)
    unit = centred * inv_std
    normed = (unit * ln_gain + ln_bias).astype(bf16)
    query = rotate(ein("std,de->ste", normed, w_query), tables, 1.0).astype(bf16)
    keys = rotate(ein("std,de->ste", normed, w_key), tables, 1.0).astype(bf16)
    values = ein("std,de->ste", normed, w_value).astype(bf16)
    d_attended = ein("std,ed->ste", cot, w_attn_out).astype(bf16)

    attended, d_query, d_keys, d_values = ring_attention(query, keys, values, d_attended)

    gate_in = ein("std,df->stf", normed, w_in) + b_in
    hidden, gelu_pull = jax.vjp(partial(jax.nn.gelu, approximate=True), gate_in)
    hidden = hidden.astype(bf16)
    d_hidden = ein("std,fd->stf", cot, w_mlp_out)
    d_gate = gelu_pull(d_hidden)[0].astype(bf16)
    d_b_in = jnp.sum(d_gate, (0, 1), dtype=f32)
    d_b_out = jnp.sum(cot, (0, 1), dtype=f32)
    d_w_mlp_out = ein("stf,std->fd", hidden, cot)
    d_w_in = ein("std,stf->df", normed, d_gate)
    mlp_part = ein("stf,fd->std", hidden, w_mlp_out)
    d_normed_mlp = ein("stf,df->std", d_gate, w_in)

    attn_part = ein("ste,ed->std", attended, w_attn_out)
    branches = lax.psum((attn_part + mlp_part).astype(bf16), "mlp").astype(f32)
    mixed = (x + branches + b_out).astype(bf16)
    d_w_attn_out = ein("ste,std->ed", attended, cot)
    d_query_pre = rotate(d_query.astype(f32), tables, -1.0).astype(bf16)
    d_key_pre = rotate(d_keys.astype(f32), tables, -1.0).astype(bf16)
    d_w_query = ein("std,ste->de", normed, d_query_pre)
    d_w_key = ein("std,ste->de", normed, d_key_pre)
    d_w_value = ein("std,ste->de", normed, d_values)
    d_normed_part = d_normed_mlp + ein("ste,de->std", d_query_pre, w_query)
    d_normed_part = d_normed_part + ein("ste,de->std", d_key_pre, w_key)
    d_normed_part = d_normed_part + ein("ste,de->std", d_values, w_value)
    d_normed = lax.psum(d_normed_part.astype(bf16), "mlp").astype(f32)
    d_gain = jnp.sum(d_normed * unit, (0, 1))
    d_bias = jnp.sum(d_normed, (0, 1))
    d_unit = d_normed * ln_gain
    d_inputs = inv_std * (
        d_unit - jnp.mean(d_unit, -1, keepdims=True) - unit * jnp.mean(d_unit * unit, -1, keepdims=True)
    )
    d_tokens = (cot.astype(f32) + d_inputs).astype(bf16)

    def total(v):
        return lax.psum(v.astype(bf16), "seq").astype(f32)

    return (
        mixed[None],
        d_tokens[None],
        total(d_gain),
        total(d_bias),
        total(d_w_query),
        total(d_w_key),
        total(d_w_value),
        total(d_w_attn_out),
        total(d_w_in),
        total(d_b_in),
        total(d_w_mlp_out),
        total(d_b_out),
    )


anywhere = pl.BlockSpec(memory_space=pl.ANY)


def call(
    kernel, grid, ins, in_specs, out_specs, out_shape, us, after=(), scalars=(), scratch=(), alias=None, vmem=24, pinned=None, loose=(),
    free=(), free_out=()
):
    used = len(scalars) + len(ins)
    pinned = len(ins) if pinned is None else pinned

    def body(*refs):
        kernel(*refs[:used], *refs[used + len(after) :])

    held = [pltpu.with_memory_space_constraint(x, pltpu.HBM) if i < pinned and i not in free else x for i, x in enumerate(ins)]
    after = tuple(pltpu.with_memory_space_constraint(x, pltpu.HBM) if pinned else x for x in after) + tuple(loose)
    if pinned:
        one = not isinstance(out_shape, list)
        shapes = [out_shape] if one else out_shape
        shapes = [s if i in free_out else pltpu.HBM(s.shape, s.dtype) for i, s in enumerate(shapes)]
        out_shape = shapes[0] if one else shapes
    return pl.pallas_call(
        body,
        name=getattr(kernel, "func", kernel).__name__.strip("<>"),
        grid_spec=pltpu.PrefetchScalarGridSpec(
            num_scalar_prefetch=len(scalars),
            grid=grid,
            in_specs=list(in_specs) + [anywhere] * len(after),
            out_specs=out_specs,
            scratch_shapes=list(scratch),
        ),
        out_shape=out_shape,
        input_output_aliases={len(scalars) + k: v for k, v in (alias or {}).items()},
        compiler_params=pltpu.CompilerParams(vmem_limit_bytes=vmem * 2**20),
        cost_estimate=pl.CostEstimate(flops=int(us * 0.5e9), bytes_accessed=0, transcendentals=0),
    )(*scalars, *held, *after)


def fence(x, *after):
    return call(
        lambda *refs: None, (1,), (x,), [anywhere], anywhere, jax.ShapeDtypeStruct(x.shape, x.dtype), 0, after, alias={0: 0}, vmem=1, pinned=0
    )


def dot(a, b):
    return jnp.dot(a, b, preferred_element_type=f32)


def dot_nt(a, b):
    return lax.dot_general(a, b, (((1,), (1,)), ((), ())), preferred_element_type=f32)


def dot_tn(a, b):
    return lax.dot_general(a, b, (((0,), (0,)), ((), ())), preferred_element_type=f32)


def whole(x):
    return pl.BlockSpec(x.shape, lambda *_: (0,) * x.ndim, pipeline_mode=pl.Buffered(1))


def mine(rows):
    return pl.BlockSpec((rows, 2 * HEAD_DIM), lambda i, at: (at[0], 0), pipeline_mode=pl.Buffered(1))


def shape_of(*shape, dtype=bf16):
    return jax.ShapeDtypeStruct(shape, dtype)


def unit_rows(x):
    average = jnp.mean(x, -1, keepdims=True)
    centred = x - average
    inv_std = lax.rsqrt(jnp.mean(centred * centred, -1, keepdims=True) + epsilon)
    return centred * inv_std, inv_std


def half_swap(low, high, lane, keep_low):
    if keep_low:
        return jnp.where(lane < HEAD_DIM, low, pltpu.roll(high, HEAD_DIM, 1))
    return jnp.where(lane < HEAD_DIM, pltpu.roll(low, HEAD_DIM, 1), high)


def rope_tile(v, cosine, from_right, from_left):
    width = v.shape[1]
    return v * cosine + pltpu.roll(v, width - 1, 1) * from_right + pltpu.roll(v, 1, 1) * from_left


def position_tables(total):
    column = np.arange(2 * HEAD_DIM) % HEAD_DIM
    freq = np.float32(10000.0) ** (np.float32(-2.0 / ROT) * (column // 2).astype(np.float32))
    angle = np.arange(total, dtype=np.float32)[:, None] * freq.astype(np.float32)[None, :]
    active = (column < ROT)[None, :]
    cosine = np.where(active, np.cos(angle.astype(np.float64)), 1.0).astype(np.float32)
    sine = np.where(active, np.sin(angle.astype(np.float64)), 0.0).astype(np.float32)
    return cosine, sine


def signed(cosine, sine):
    even = lax.broadcasted_iota(jnp.int32, sine.shape, 1) % 2 == 0
    return cosine, jnp.where(even, -sine, 0.0), jnp.where(even, 0.0, sine)


def pre_kernel(shard_ref, x_ref, g_ref, gain, bias, wq, wk, wv, wo, cosine, sine, *rest):
    normed_ref, packed_ref = rest[-2:]
    unit, _ = unit_rows(x_ref[0].astype(f32))
    normed = (unit * gain[...] + bias[...]).astype(bf16)
    normed_ref[...] = normed
    q, k, v = dot(normed, wq[...]), dot(normed, wk[...]), dot(normed, wv[...])
    a = dot_nt(g_ref[0], wo[...])
    tables = signed(cosine[...], sine[...])
    lane = lax.broadcasted_iota(jnp.int32, tables[0].shape, 1)
    for tile in range(q.shape[1] // 128):
        cols = slice(tile * 128, (tile + 1) * 128)
        qt, kt = rope_tile(q[:, cols], *tables), rope_tile(k[:, cols], *tables)
        for side in (0, 1):
            head = tile * 2 + side
            packed_ref[head, :, 0:128] = half_swap(qt, kt, lane, side == 0).astype(bf16)
            packed_ref[head, :, 128:256] = half_swap(v[:, cols], a[:, cols], lane, side == 0).astype(bf16)


def pre(c, count, shard, x, g, consts, tables, before):
    seqs, rows, width = x.shape
    heads = consts[2].shape[1] // HEAD_DIM
    by_seq = pl.BlockSpec((1, rows, width), lambda i, _: (c * count + i, 0, 0))
    ins, specs = (x, g) + consts + tables, [by_seq, by_seq] + [whole(w) for w in consts] + [mine(rows)] * 2
    alias = {}
    if before is not None:
        alias = {len(ins): 0}
        ins, specs = ins + (before,), specs + [anywhere]
    return call(
        pre_kernel,
        (count,),
        ins,
        specs,
        [
            pl.BlockSpec((rows, width), lambda i, _: (c * count + i, 0)),
            pl.BlockSpec((heads, rows, 4 * HEAD_DIM), lambda i, _: (i, 0, 0)),
        ],
        [shape_of(seqs * rows, width), shape_of(count * heads, rows, 4 * HEAD_DIM)],
        3,
        scalars=(shard,),
        alias=alias,
        free_out=(1,),
    )


def mlp_kernel(n_ref, g_ref, w_in, b_in, w_out, *rest):
    hidden_ref, dgate_ref, part_ref, dn_ref, db_in, db_out = rest[-6:]
    c0, c1 = 0.7978845608028654, 0.044715
    g = g_ref[...]
    gate = dot(n_ref[...], w_in[...]) + b_in[...]
    square = gate * gate
    tanh = jnp.tanh(c0 * gate * (1.0 + c1 * square))
    left = 0.5 * (1.0 + tanh)
    hidden = (gate * left).astype(bf16)
    slope = left + 0.5 * gate * (1.0 - tanh * tanh) * (c0 * (1.0 + 3.0 * c1 * square))
    dgate = (dot_nt(g, w_out[...]) * slope).astype(bf16)
    hidden_ref[...] = hidden
    dgate_ref[...] = dgate
    part_ref[...] = dot(hidden, w_out[...]).astype(bf16)
    dn_ref[...] = dot_nt(dgate, w_in[...]).astype(bf16)

    @pl.when(pl.program_id(0) == 0)
    def _():
        db_in[...] = jnp.zeros_like(db_in)
        db_out[...] = jnp.zeros_like(db_out)

    db_in[...] += jnp.sum(dgate.astype(f32), 0, keepdims=True)
    db_out[...] += jnp.sum(g.astype(f32), 0, keepdims=True)


def mlp(c, count, rows, normed, g, w_in, b_in, w_out, before, after):
    total, width = g.shape
    ff = w_in.shape[1]
    there = lambda w: pl.BlockSpec((rows, w), lambda i: (c * count + i, 0))
    here = lambda w: pl.BlockSpec((rows, w), lambda i: (i, 0))
    one = lambda w: pl.BlockSpec((1, w), lambda i: (0, 0))
    ins = (normed, g, w_in, b_in, w_out)
    specs = [there(width), there(width), whole(w_in), whole(b_in), whole(w_out)]
    alias = {}
    if before is not None:
        alias = {len(ins): 0, len(ins) + 1: 1}
        ins, specs = ins + tuple(before), specs + [anywhere] * 2
    return call(
        mlp_kernel,
        (count,),
        ins,
        specs,
        [there(ff), there(ff), here(width), here(width), one(ff), one(width)],
        [
            shape_of(total, ff),
            shape_of(total, ff),
            shape_of(count * rows, width),
            shape_of(count * rows, width),
            shape_of(1, ff, dtype=f32),
            shape_of(1, width, dtype=f32),
        ],
        5,
        after,
        alias=alias,
        vmem=32,
    )


def dense_grads_kernel(core_ref, n_ref, dgate_ref, hidden_ref, g_ref, *outs):
    step, half = pl.program_id(0), pl.num_programs(0) // 2
    both = dot_tn(n_ref[...], dgate_ref[...]).astype(bf16), dot_tn(hidden_ref[...], g_ref[...]).astype(bf16)
    for at in range((len(outs) - 1) // 2):

        @pl.when(step == at)
        def _():
            outs[2 * at][0], outs[2 * at + 1][0] = both

    @pl.when(step >= half)
    def _():
        outs[-1][0], outs[-1][1] = both


def halves(steps, rows, wide, slots):
    half = steps // 2

    def place(i, core):
        return jnp.where(i < half, (1 - core[0]) * half + i, core[0] * half + i - half)

    cols = lambda total: pl.BlockSpec((total, rows), lambda i, core: (0, place(i, core)))
    give = pl.BlockSpec((1, rows, wide), lambda i, core: (0, jnp.minimum(i, half - 1), 0))
    keep = pl.BlockSpec((slots, rows, wide), lambda i, core: (0, jnp.maximum(i - half, 0), 0))
    return cols, [give, keep]


def dense_grads(core, normed, dgate, hidden, g, loose, steps=4):
    total, width = g.shape
    rows = width // steps
    cols, (_, keep) = halves(steps, rows, width, 2)
    part = pl.BlockSpec((1, rows, width), lambda i, core: (0, 0, 0))
    return call(
        dense_grads_kernel,
        (steps,),
        (normed, dgate, hidden, g),
        [cols(total), whole(dgate), cols(total), whole(g)],
        [part] * steps + [keep],
        [shape_of(1, rows, width)] * steps + [shape_of(2, width // 2, width)],
        6,
        scalars=(core,),
        loose=loose,
    )


def post_kernel(place_ref, back_ref, x_ref, part_ref, dn_ref, b_out, wq, wk, wv, wo, cosine, sine, *rest):
    share_refs, flat_ref, dgain, dbias = rest[-5:-3], rest[-3], rest[-2], rest[-1]
    tables = signed(cosine[...], sine[...])
    lane = lax.broadcasted_iota(jnp.int32, tables[0].shape, 1)
    inner = wo.shape[0]
    for tile in range(inner // 128):
        even, odd = back_ref[2 * tile].astype(f32), back_ref[2 * tile + 1].astype(f32)
        lows = half_swap(even[:, 0:128], odd[:, 0:128], lane, True)
        dq = half_swap(even[:, 0:128], odd[:, 0:128], lane, False)
        dk = half_swap(even[:, 128:256], odd[:, 128:256], lane, True)
        dv = half_swap(even[:, 128:256], odd[:, 128:256], lane, False)
        dq = rope_tile(dq, tables[0], -tables[1], -tables[2])
        dk = rope_tile(dk, tables[0], -tables[1], -tables[2])
        for which, value in enumerate((lows, dq, dk, dv)):
            at = which * inner + tile * 128
            flat_ref[:, at : at + 128] = value.astype(bf16)
    x = x_ref[0].astype(f32)
    z = place_ref[1]
    first = (z == 0).astype(f32)
    mixed = dot(flat_ref[:, 0:inner], wo[...]) + part_ref[...].astype(f32) + first * (x + b_out[...])
    dn = dn_ref[...].astype(f32)
    for which, w in enumerate((wq, wk, wv)):
        at = (which + 1) * inner
        dn = dn + dot_nt(flat_ref[:, at : at + inner], w[...])
    unit, _ = unit_rows(x)
    odd = z % 2 == 1
    half = dn.shape[0] // 2
    for which, share in enumerate((dn, mixed)):
        top, bottom = share[:half].astype(bf16), share[half:].astype(bf16)
        share_refs[0][0, which] = jnp.where(odd, top, bottom)
        share_refs[1][0, which] = jnp.where(odd, bottom, top)

    @pl.when(pl.program_id(0) == 0)
    def _():
        dgain[...] = jnp.zeros_like(dgain)
        dbias[...] = jnp.zeros_like(dbias)

    dgain[...] += jnp.sum(dn * unit, 0, keepdims=True)
    dbias[...] += jnp.sum(dn, 0, keepdims=True)


def post(c, count, place, back, x, part, dn, consts, tables, before, after):
    seqs, rows, width = x.shape
    inner = consts[1].shape[1]
    heads = inner // HEAD_DIM
    here = pl.BlockSpec((rows, width), lambda i, _: (i, 0))
    one = pl.BlockSpec((1, width), lambda i, _: (0, 0))
    ins = (back, x, part, dn) + consts + tables
    specs = [
        pl.BlockSpec((heads, rows, 4 * HEAD_DIM), lambda i, _: (i, 0, 0)),
        pl.BlockSpec((1, rows, width), lambda i, _: (c * count + i, 0, 0)),
        here,
        here,
    ]
    specs += [whole(w) for w in consts] + [mine(rows)] * 2
    alias = {}
    if before is not None:
        alias = {len(ins): 2}
        ins, specs = ins + (before,), specs + [anywhere]
    share_spec = pl.BlockSpec((1, 2, rows // 2, width), lambda i, place: (i ^ (place[1] // 2), 0, 0, 0))
    share_shape = shape_of(count, 2, rows // 2, width)
    return call(
        post_kernel,
        (count,),
        ins,
        specs,
        [share_spec] * 2 + [pl.BlockSpec((rows, 4 * inner), lambda i, _: (c * count + i, 0)), one, one],
        [share_shape] * 2 + [shape_of(seqs * rows, 4 * inner)] + [shape_of(1, width, dtype=f32)] * 2,
        4,
        after,
        (place,),
        alias=alias,
        free=(0,),
    )


def head_grads_kernel(core_ref, n_ref, g_ref, flat_ref, give_ref, keep_ref, *, inner):
    step, half = pl.program_id(0), pl.num_programs(0) // 2
    out = dot_tn(g_ref[...], flat_ref[:, 0:inner])
    rest = dot_tn(n_ref[...], flat_ref[:, inner:])

    @pl.when(step < half)
    def _():
        give_ref[0, :, 0:inner] = out.astype(bf16)
        give_ref[0, :, inner:] = rest.astype(bf16)

    @pl.when(step >= half)
    def _():
        keep_ref[0, :, 0:inner] = out.astype(bf16)
        keep_ref[0, :, inner:] = rest.astype(bf16)


def head_grads(core, normed, g, flat, loose, steps=4):
    total, width = g.shape
    wide = flat.shape[1]
    cols, outs = halves(steps, width // steps, wide, 1)
    return call(
        partial(head_grads_kernel, inner=wide // 4),
        (steps,),
        (normed, g, flat),
        [cols(total), cols(total), whole(flat)],
        outs,
        [shape_of(1, width // 2, wide)] * 2,
        4,
        scalars=(core,),
        loose=loose,
    )


def split_kernel(chip_ref, keep_ref, *refs, chips):
    outs, gots = refs[-chips:], refs[:-chips]
    slots, blocks = keep_ref.shape[0], len(gots) // keep_ref.shape[0]
    block = (chip_ref[0] ^ pl.program_id(0)) * blocks // chips
    for k, out in enumerate(outs):

        @pl.when(pl.program_id(0) == k)
        def _():
            for slot in range(slots):
                got = gots[slot][0].astype(f32)
                for at in range(1, blocks):
                    got = jnp.where(block == at, gots[at * slots + slot][0].astype(f32), got)
                out[slot] = (keep_ref[slot].astype(f32) + got).astype(bf16)


def split(chip, keep, gots, chips, loose):
    slots, rows, wide = keep.shape
    per = chips * slots // len(gots)
    rows = rows // chips
    block = pl.BlockSpec((slots, rows, wide), lambda k, chip: (0, chip[0] ^ k, 0))
    one = pl.BlockSpec((1, rows, wide), lambda k, chip: (0, (chip[0] ^ k) % per, 0))
    return call(
        partial(split_kernel, chips=chips),
        (chips,),
        (keep,) + tuple(gots),
        [block] + [one] * len(gots),
        [pl.BlockSpec((slots, rows, wide), lambda k, chip: (0, 0, 0))] * chips,
        [shape_of(slots, rows, wide)] * chips,
        2,
        scalars=(chip,),
        vmem=20,
        pinned=0,
        loose=loose,
    )


def dense_outs_kernel(place_ref, *refs):
    out_in, out_out = refs[-2:]
    for at, ref in enumerate(refs[:-2]):

        @pl.when(pl.program_id(0) == at)
        def _():
            out_in[...] = ref[0].astype(f32)
            out_out[...] = ref[1].astype(f32)


def head_outs_kernel(place_ref, *refs, inner):
    out_t, out_q, out_k, out_v = refs[-4:]
    for at, ref in enumerate(refs[:-4]):

        @pl.when(pl.program_id(0) == at)
        def _():
            out_t[...] = ref[0, :, 0:inner].astype(f32).T
            out_q[...] = ref[0, :, inner : 2 * inner].astype(f32)
            out_k[...] = ref[0, :, 2 * inner : 3 * inner].astype(f32)
            out_v[...] = ref[0, :, 3 * inner :].astype(f32)


def dense_outs(places, pieces, width, loose):
    _, rows, wide = pieces[0].shape
    down = pl.BlockSpec((rows, wide), lambda i, places: (places[i], 0))
    return call(
        dense_outs_kernel,
        (len(pieces),),
        tuple(pieces),
        [whole(p) for p in pieces],
        [down, down],
        [pltpu.HBM((width, wide), f32)] * 2,
        4,
        scalars=(places,),
        vmem=20,
        pinned=0,
        loose=loose,
    )


def head_outs(places, pieces, width, loose):
    _, rows, wide = pieces[0].shape
    inner = wide // 4
    down = pl.BlockSpec((rows, inner), lambda i, places: (places[i], 0))
    return call(
        partial(head_outs_kernel, inner=inner),
        (len(pieces),),
        tuple(pieces),
        [whole(p) for p in pieces],
        [pl.BlockSpec((inner, rows), lambda i, places: (0, places[i])), down, down, down],
        [pltpu.HBM((inner, width), f32)] + [pltpu.HBM((width, inner), f32)] * 3,
        3,
        scalars=(places,),
        vmem=16,
        pinned=0,
        loose=loose,
    )


def input_grad(x, g, dn, gain):
    unit, inv_std = unit_rows(x.astype(f32))
    du = dn.astype(f32) * gain
    d = inv_std * (du - jnp.mean(du, -1, keepdims=True) - unit * jnp.mean(du * unit, -1, keepdims=True))
    return (g.astype(f32) + d).astype(bf16)


def pair_sum_kernel(keep_ref, got_ref, own_ref, other_ref):
    total = (keep_ref[0].astype(f32) + got_ref[0].astype(f32)).astype(bf16)

    @pl.when(pl.program_id(0) == 0)
    def _():
        own_ref[...] = total

    @pl.when(pl.program_id(0) == 1)
    def _():
        other_ref[...] = total


def pair_sum(keep, got, loose):
    block = pl.BlockSpec((1,) + keep.shape[1:], lambda i: (i, 0, 0, 0))
    out = pl.BlockSpec(keep.shape[1:], lambda i: (0, 0, 0))
    return call(
        pair_sum_kernel, (2,), (keep, got), [block, block], [out, out], [shape_of(*keep.shape[1:])] * 2, 1, vmem=12, pinned=0,
        loose=loose,
    )


def own_quarter_kernel(place_ref, x_ref, g_ref, own_ref, got_ref, gain, out_ref):
    total = own_ref[...].astype(f32) + got_ref[...].astype(f32)
    out_ref[0] = input_grad(x_ref[0], g_ref[0], total[0], gain[...])
    out_ref[1] = total[1].astype(bf16)


def own_quarter(place, start, x, g, own, got, gain, loose):
    _, rows, width = own.shape
    per = x.shape[1] // rows
    block = pl.BlockSpec((1, rows, width), lambda i, place: (start + place[1] // per, place[1] % per, 0))
    return call(
        own_quarter_kernel,
        (1,),
        (x, g, own, got, gain),
        [block, block, whole(own), whole(got), whole(gain)],
        pl.BlockSpec(own.shape, lambda i, _: (0, 0, 0)),
        shape_of(*own.shape),
        1,
        (),
        (place,),
        vmem=12,
        pinned=2,
        loose=loose,
    )


def placed_kernel(place_ref, *refs, pieces):
    tokens_ref, mixed_ref = refs[-2:]
    for at, ref in enumerate(refs[:pieces]):

        @pl.when(pl.program_id(0) == at)
        def _():
            tokens_ref[0] = ref[0]
            mixed_ref[0] = ref[1]


def placed(place, shape, start, pieces, before, loose):
    _, rows, width = pieces[0].shape
    per = shape[1] // rows

    def spot(i, place):
        quarter = place[1] ^ i
        return start + quarter // per, quarter % per, 0

    block = pl.BlockSpec((1, rows, width), spot)
    ins, specs, alias = tuple(pieces), [whole(p) for p in pieces], {}
    if before is not None:
        alias = {len(ins): 0, len(ins) + 1: 1}
        ins += tuple(pltpu.with_memory_space_constraint(v, pltpu.HBM) for v in before)
        specs += [anywhere] * 2
    return call(
        partial(placed_kernel, pieces=len(pieces)),
        (len(pieces),),
        ins,
        specs,
        [block, block],
        [pltpu.HBM(shape, bf16)] * 2,
        2,
        scalars=(place,),
        alias=alias,
        vmem=12,
        pinned=0,
        loose=loose,
    )


def exchanged(x, bits):
    return lax.ppermute(x, "seq", [(i, i ^ bits) for i in range(lax.axis_size("seq"))])


def by_pairs(
    tokens, ln_gain, ln_bias, w_query, w_key, w_value, w_attn_out, w_in, b_in, w_mlp_out, b_out, cotangent
):
    x, cot = tokens[0], cotangent[0]
    seqs, rows, width = x.shape
    inner = w_query.shape[1]
    ff = w_in.shape[1]
    heads = inner // HEAD_DIM
    shards = lax.axis_size("seq")
    count = shards // heads
    row = lambda v: v.reshape(1, -1)
    gain, b_in, b_out = row(ln_gain), row(b_in), row(b_out)
    flat_cot = cot.reshape(-1, width)
    shard = lax.axis_index("seq").astype(jnp.int32)
    core, chip, chips = (shard % 2).reshape(1), (shard // 2).reshape(1), shards // 2
    z = lax.axis_index("mlp").astype(jnp.int32)
    place = jnp.stack([shard, z])
    tables = position_tables(shards * rows)
    weights = (w_query, w_key, w_value, w_attn_out)
    pre_consts = (gain, row(ln_bias)) + weights
    post_consts = (b_out,) + weights

    def attend(sent, after):
        done = attention(sent.reshape(1, shards * rows, 4 * HEAD_DIM), after)
        return done.reshape(shards, rows, 4 * HEAD_DIM)

    def traded(v):
        return lax.all_to_all(v, "seq", 0, 0, tiled=True)

    def over_line(v, bits):
        return lax.ppermute(v, "mlp", [(i, i ^ bits) for i in range(4)])

    dense_args = (flat_cot, w_in, b_in, w_mlp_out)
    normed, packed_a = pre(0, count, place, x, cot, pre_consts, tables, None)
    sent_a = traded(packed_a)
    normed, packed_b = pre(1, count, place, x, cot, pre_consts, tables, normed)
    hidden, dgate, part_a, dn_a, db_in_a, db_out_a = mlp(0, count, rows, normed, *dense_args, None, (packed_b,))
    sent_b = traded(fence(packed_b, sent_a, db_in_a))
    done_a = fence(attend(sent_a, (db_in_a,)), sent_b)
    back_a = traded(done_a)
    done_b = fence(attend(sent_b, (done_a,)), back_a)
    back_b = traded(done_b)
    give_a, keep_a, flat, gain_a, bias_a = post(
        0, count, place, back_a, x, part_a, dn_a, post_consts, tables, None, (done_b,)
    )
    got_a = over_line(give_a, 1)
    hidden, dgate, part_b, dn_b, db_in_b, db_out_b = mlp(1, count, rows, normed, *dense_args, (hidden, dgate), (gain_a,))
    give_b, keep_b, flat, gain_b, bias_b = post(
        1, count, place, back_b, x, part_b, dn_b, post_consts, tables, flat, (db_in_b,)
    )
    got_b = over_line(give_b, 1)
    *gives, keep_e = dense_grads(core, normed, dgate, hidden, flat_cot, (gain_b,))
    gots_e = [exchanged(v, 1) for v in gives]
    small = [gain_a + gain_b, bias_a + bias_b, db_in_a + db_in_b, db_out_a + db_out_b]
    small = jnp.concatenate(small, 1).reshape(8, -1)
    small_got = exchanged(small, 1)
    give, keep_l = head_grads(core, normed, flat_cot, flat, (keep_e,))
    gots_l = [exchanged(give, 1)]
    own_a, other_a = pair_sum(keep_a, got_a, (keep_l,))
    got_a = over_line(other_a, 2)

    def over_chips(pieces):
        return [pieces[0]] + [exchanged(pieces[k], 2 * k) for k in range(1, chips)]

    def summed(pieces, token):
        total = pieces[0].astype(f32)
        for piece in pieces[1:]:
            total = total + fence(piece, token).astype(f32)
        return total.astype(bf16)

    dense = split(chip, keep_e, gots_e, chips, (own_a,))
    token = dense[0]
    dense = over_chips(dense)
    own_b, other_b = pair_sum(keep_b, got_b, (token,))
    got_b = over_line(other_b, 2)
    head = split(chip, keep_l, gots_l, chips, (own_b,))
    token = head[0]
    head = over_chips(head)
    small = small + fence(small_got, token)
    small_got = exchanged(small, 2)
    done_a = own_quarter(place, 0, x, cot, own_a, got_a, gain, (token,))
    far_a, near_a = over_line(done_a, 2), over_line(done_a, 1)
    token = summed(dense, done_a)
    dense = over_chips([token] * chips)
    token = summed(head, token)
    head = over_chips([token] * chips)
    done_b = own_quarter(place, count, x, cot, own_b, got_b, gain, (token,))
    far_b, near_b = over_line(done_b, 2), over_line(done_b, 1)
    far_a = fence(far_a, done_b)
    beside_a = over_line(far_a, 1)
    small = small + fence(small_got, done_b)
    small_got = exchanged(small, 4)
    near_a = fence(near_a, far_a)
    dense = [dense[0]] + [fence(v, near_a) for v in dense[1:]]
    dense = dense + [exchanged(v, 1) for v in dense]
    far_b = fence(far_b, dense[3])
    beside_b = over_line(far_b, 1)
    head = [head[0]] + [fence(v, far_b) for v in head[1:]]
    head = head + [exchanged(v, 1) for v in head]
    beside_a = fence(beside_a, head[3])
    d_tokens, mixed = placed(place, x.shape, 0, (done_a, near_a, far_a, beside_a), None, ())
    small = small + fence(small_got, d_tokens)
    vectors = small.reshape(-1)[: 2 * width].reshape(2, width)
    vectors_got = over_line(vectors, 1)
    row_blocks = jnp.concatenate([(core ^ side) * chips + (chip ^ k) for side in (0, 1) for k in range(chips)])
    d_in, d_out = dense_outs(row_blocks, dense, width, (d_tokens,))
    vectors = vectors + fence(vectors_got, d_out)
    vectors_got = over_line(vectors, 2)
    d_attn_out, d_query, d_key, d_value = head_outs(row_blocks, head, width, (d_out,))
    vectors = vectors + fence(vectors_got, d_value)
    d_tokens, mixed = placed(place, x.shape, count, (done_b, near_b, far_b, beside_b), (d_tokens, mixed), (d_value,))
    small = small.reshape(-1)
    return (
        mixed.reshape(tokens.shape),
        d_tokens[None],
        vectors[0],
        vectors[1],
        d_query,
        d_key,
        d_value,
        d_attn_out,
        d_in,
        small[2 * width : 2 * width + ff],
        d_out,
        small[2 * width + ff :],
    )


def per_device(
    tokens, ln_gain, ln_bias, w_query, w_key, w_value, w_attn_out, w_in, b_in, w_mlp_out, b_out, cotangent
):
    _, seqs, rows, width = tokens.shape
    inner = w_query.shape[1]
    heads = inner // HEAD_DIM
    shards = lax.axis_size("seq")
    fits = shards == 8 and lax.axis_size("mlp") == 4 and seqs * heads == 2 * shards and shards % heads == 0
    fits = fits and inner % 128 == 0 and rows % 256 == 0 and width % 1024 == 0 and w_in.shape[1] % 1024 == 0
    plan = by_pairs if fits else by_ring
    return plan(
        tokens, ln_gain, ln_bias, w_query, w_key, w_value, w_attn_out, w_in, b_in, w_mlp_out, b_out, cotangent
    )


def solution(mesh):
    rows, whole = P("seq", None, None, None), P()
    cols, down = P(None, "mlp"), P("mlp", None)
    return jax.shard_map(
        per_device,
        mesh=mesh,
        in_specs=(rows, whole, whole, cols, cols, cols, down, cols, P("mlp"), down, whole, rows),
        out_specs=(rows, rows, whole, whole, cols, cols, cols, down, cols, P("mlp"), down, whole),
        check_vma=False,
    )
```

```python
from functools import partial

import jax
import jax.numpy as jnp
import numpy as np
from jax import lax
from jax.experimental import pallas as pl
from jax.experimental.pallas import tpu as pltpu
from jax.sharding import PartitionSpec as P

HEAD_DIM = 64
ROT = 32

epsilon = 1e-05
neg_big = -1e30
bf16 = jnp.bfloat16
f32 = jnp.float32


def passed_along(x, axis, by):
    peers = lax.axis_size(axis)
    pairs = [(i, i + by) for i in range(peers) if 0 <= i + by < peers]
    return lax.ppermute(x, axis, pairs)


def rotary_tables(positions, width):
    column = jnp.arange(width, dtype=jnp.int32) % HEAD_DIM
    pairs = (column // 2).astype(f32)
    freq = 10000.0 ** (-2.0 * pairs / ROT)
    angle = positions.astype(f32)[:, None] * freq[None, :]
    active = (column < ROT)[None, :]
    even = (column % 2 == 0)[None, :]
    cosine = jnp.where(active, jnp.cos(angle), 1.0)
    sine = jnp.where(active, jnp.sin(angle), 0.0)
    return cosine, jnp.where(even, -sine, 0.0), jnp.where(even, 0.0, sine)


def rotate(v, tables, sign):
    cosine, from_right, from_left = tables
    right = jnp.concatenate([v[..., 1:], v[..., :1]], -1)
    left = jnp.concatenate([v[..., -1:], v[..., :-1]], -1)
    return v * cosine + sign * (right * from_right + left * from_left)


def attention_kernel(x_ref, out_ref, xt, acc, sbuf, *, length, hd, tq, tk):
    xt[...] = x_ref[0].T
    scale = hd**-0.5
    nt = (((1,), (1,)), ((), ()))
    zero = jnp.zeros((hd, tq), bf16)

    def put(old, new, q0, join):
        if old is None:
            return new
        if q0 == 0:
            return join(old, new)
        return jnp.concatenate([old[:, :q0], join(old[:, q0:], new)], 1)

    add = lambda u, v: u + v
    for i in range(length // tq):
        first = i * tq
        qs = (xt[0:hd, first : first + tq].astype(f32) * scale).astype(bf16)
        at = xt[3 * hd : 4 * hd, first : first + tq].astype(f32)
        zq = jnp.concatenate([zero, qs], 0)
        qz = jnp.concatenate([qs, zero], 0)
        steps = [(k0, k0 + tk, 0) for k0 in range(0, first, tk)]
        steps += [(first + q0, first + q0 + tk // 2, q0) for q0 in range(0, tq, tk // 2)]
        top = None
        for k0, k1, q0 in steps:
            st = jnp.dot(x_ref[0, k0:k1, 0 : 2 * hd], zq[:, q0:], preferred_element_type=f32)
            if k0 >= first:
                kp = lax.broadcasted_iota(jnp.int32, st.shape, 0)
                qp = lax.broadcasted_iota(jnp.int32, st.shape, 1)
                st = jnp.where(kp <= qp, st, neg_big)
            sbuf[k0:k1, q0:] = st
            top = put(top, jnp.max(st, 0, keepdims=True), q0, jnp.maximum)
        tot = None
        ot = None
        for k0, k1, q0 in steps:
            e = jnp.exp(sbuf[k0:k1, q0:] - top[:, q0:])
            sbuf[k0:k1, q0:] = e
            tot = put(tot, jnp.sum(e, 0, keepdims=True), q0, add)
            ot = put(ot, jnp.dot(xt[2 * hd : 3 * hd, k0:k1], e.astype(bf16), preferred_element_type=f32), q0, add)
        r = 1.0 / tot
        ot = ot * r
        ar = (at * r).astype(bf16)
        spread = jnp.sum(ar.astype(f32) * ot, 0, keepdims=True)
        az = jnp.concatenate([ar, zero], 0)
        za = jnp.concatenate([zero, ar], 0)
        dqt = None
        for k0, k1, q0 in steps:
            dp = jnp.dot(x_ref[0, k0:k1, 2 * hd : 4 * hd], az[:, q0:], preferred_element_type=f32)
            e = sbuf[k0:k1, q0:]
            ds = (e * (dp - spread[:, q0:])).astype(bf16)
            dqt = put(dqt, jnp.dot(xt[hd : 2 * hd, k0:k1], ds, preferred_element_type=f32), q0, add)
            both = lax.dot_general(ds, qz[:, q0:], nt, preferred_element_type=f32) + lax.dot_general(
                e.astype(bf16), za[:, q0:], nt, preferred_element_type=f32
            )
            if k0 < first:
                both = acc[k0:k1, :] + both
            acc[k0:k1, :] = both
        both = jnp.concatenate([ot, dqt * scale], 0)
        out_ref[0, first : first + tq, 0 : 2 * hd] = both.T.astype(bf16)
    out_ref[0, :, 2 * hd : 4 * hd] = acc[...].astype(bf16)


def attention(x, after=()):
    n, length, width = x.shape
    hd = width // 4
    tq = 512 if length % 512 == 0 else 256
    spec = pl.BlockSpec((1, length, width), lambda i: (i, 0, 0))
    return call(
        partial(attention_kernel, length=length, hd=hd, tq=tq, tk=512),
        (n,),
        (x,),
        [spec],
        spec,
        shape_of(*x.shape),
        7,
        after,
        scratch=[pltpu.VMEM((width, length), bf16), pltpu.VMEM((length, 2 * hd), f32), pltpu.VMEM((length, tq), f32)],
        vmem=32,
        free_out=(0,),
    )


def ring_attention(q, k, v, a):
    seq_count, row_count, inner_width = q.shape
    score_scale = HEAD_DIM ** (-0.5)
    shard_total = lax.axis_size("seq")
    my_shard = lax.axis_index("seq")
    heads_of = lambda x: x.reshape(seq_count, row_count, inner_width // HEAD_DIM, HEAD_DIM)
    flat_of = lambda x: x.reshape(seq_count, row_count, inner_width)
    qh, gh = heads_of(q), heads_of(a)
    local = jnp.arange(row_count, dtype=jnp.int32)
    own_mask = local[:, None] >= local[None, :]
    ein = partial(jnp.einsum, preferred_element_type=f32)

    def attend_block(state, key_block, value_block, visible):
        running_max, exp_total, weighted = state
        raw = ein("sthd,suhd->shtu", qh, key_block) * score_scale
        raw = jnp.where(visible[None, None], raw, neg_big)
        new_max = jnp.maximum(running_max, jnp.max(raw, -1))
        weights = jnp.where(visible[None, None], jnp.exp(raw - new_max[..., None]), 0.0)
        shrink = jnp.exp(running_max - new_max)
        exp_total = exp_total * shrink + jnp.sum(weights, -1)
        weighted = weighted * jnp.transpose(shrink, (0, 2, 1))[..., None] + ein(
            "shtu,suhd->sthd", weights.astype(bf16), value_block
        )
        return (new_max, exp_total, weighted)

    head_count = inner_width // HEAD_DIM
    state = (
        jnp.full((seq_count, head_count, row_count), neg_big, f32),
        jnp.zeros((seq_count, head_count, row_count), f32),
        jnp.zeros(qh.shape, f32),
    )
    state = attend_block(state, heads_of(k), heads_of(v), own_mask)
    empty_stack = jnp.zeros((max(shard_total - 1, 1),) + q.shape, bf16)

    def forward_step(step, carry):
        state, near_keys, near_values, key_stack, value_stack = carry
        near_keys, near_values = passed_along((near_keys, near_values), "seq", 1)
        visible = jnp.broadcast_to(my_shard >= step, (row_count, row_count))
        state = attend_block(state, heads_of(near_keys), heads_of(near_values), visible)
        key_stack = lax.dynamic_update_index_in_dim(key_stack, near_keys, step - 1, 0)
        value_stack = lax.dynamic_update_index_in_dim(value_stack, near_values, step - 1, 0)
        return (state, near_keys, near_values, key_stack, value_stack)

    state, _, _, key_stack, value_stack = lax.fori_loop(
        1, shard_total, forward_step, (state, k, v, empty_stack, empty_stack)
    )
    running_max, exp_total, weighted = state
    log_total = running_max + jnp.log(exp_total)
    attended = weighted / jnp.transpose(exp_total, (0, 2, 1))[..., None]
    spread = jnp.transpose(jnp.sum(gh.astype(f32) * attended, -1), (0, 2, 1))

    def grads(key_block, value_block, visible):
        raw = ein("sthd,suhd->shtu", qh, key_block) * score_scale
        probs = jnp.where(visible[None, None], jnp.exp(raw - log_total[..., None]), 0.0)
        grad_probs = ein("sthd,suhd->shtu", gh, value_block)
        slopes = (probs * (grad_probs - spread[..., None])).astype(bf16)
        query_grad = ein("shtu,suhd->sthd", slopes, key_block) * score_scale
        key_grad = ein("shtu,sthd->suhd", slopes, qh) * score_scale
        value_grad = ein("shtu,sthd->suhd", probs.astype(bf16), gh)
        return query_grad, key_grad, value_grad

    d_query, d_keys, d_values = grads(heads_of(k), heads_of(v), own_mask)

    def return_step(index, carry):
        query_grad_total, travelling = carry
        step = shard_total - 1 - index
        near_keys = lax.dynamic_index_in_dim(key_stack, step - 1, 0, keepdims=False)
        near_values = lax.dynamic_index_in_dim(value_stack, step - 1, 0, keepdims=False)
        visible = jnp.broadcast_to(my_shard >= step, (row_count, row_count))
        query_grad, key_grad, value_grad = grads(heads_of(near_keys), heads_of(near_values), visible)
        joined = jnp.concatenate([flat_of(key_grad), flat_of(value_grad)], -1)
        travelling = passed_along((travelling + joined).astype(bf16), "seq", -1).astype(f32)
        return (query_grad_total + query_grad, travelling)

    start = jnp.zeros((seq_count, row_count, 2 * inner_width), f32)
    d_query, travelling = lax.fori_loop(0, shard_total - 1, return_step, (d_query, start))
    d_keys = flat_of(d_keys) + travelling[..., :inner_width]
    d_values = flat_of(d_values) + travelling[..., inner_width:]
    return tuple(x.astype(bf16) for x in (flat_of(attended), flat_of(d_query), d_keys, d_values))


def by_ring(
    tokens, ln_gain, ln_bias, w_query, w_key, w_value, w_attn_out, w_in, b_in, w_mlp_out, b_out, cotangent
):
    x_low = tokens[0]
    cot = cotangent[0]
    seqs, rows, width = x_low.shape
    inner = w_query.shape[1]
    my_shard = lax.axis_index("seq")
    ein = partial(jnp.einsum, preferred_element_type=f32)
    positions = my_shard * rows + jnp.arange(rows, dtype=jnp.int32)
    tables = rotary_tables(positions, inner)
    x = x_low.astype(f32)
    centred = x - jnp.mean(x, -1, keepdims=True)
    inv_std = lax.rsqrt(jnp.mean(centred * centred, -1, keepdims=True) + epsilon)
    unit = centred * inv_std
    normed = (unit * ln_gain + ln_bias).astype(bf16)
    query = rotate(ein("std,de->ste", normed, w_query), tables, 1.0).astype(bf16)
    keys = rotate(ein("std,de->ste", normed, w_key), tables, 1.0).astype(bf16)
    values = ein("std,de->ste", normed, w_value).astype(bf16)
    d_attended = ein("std,ed->ste", cot, w_attn_out).astype(bf16)

    attended, d_query, d_keys, d_values = ring_attention(query, keys, values, d_attended)

    gate_in = ein("std,df->stf", normed, w_in) + b_in
    hidden, gelu_pull = jax.vjp(partial(jax.nn.gelu, approximate=True), gate_in)
    hidden = hidden.astype(bf16)
    d_hidden = ein("std,fd->stf", cot, w_mlp_out)
    d_gate = gelu_pull(d_hidden)[0].astype(bf16)
    d_b_in = jnp.sum(d_gate, (0, 1), dtype=f32)
    d_b_out = jnp.sum(cot, (0, 1), dtype=f32)
    d_w_mlp_out = ein("stf,std->fd", hidden, cot)
    d_w_in = ein("std,stf->df", normed, d_gate)
    mlp_part = ein("stf,fd->std", hidden, w_mlp_out)
    d_normed_mlp = ein("stf,df->std", d_gate, w_in)

    attn_part = ein("ste,ed->std", attended, w_attn_out)
    branches = lax.psum((attn_part + mlp_part).astype(bf16), "mlp").astype(f32)
    mixed = (x + branches + b_out).astype(bf16)
    d_w_attn_out = ein("ste,std->ed", attended, cot)
    d_query_pre = rotate(d_query.astype(f32), tables, -1.0).astype(bf16)
    d_key_pre = rotate(d_keys.astype(f32), tables, -1.0).astype(bf16)
    d_w_query = ein("std,ste->de", normed, d_query_pre)
    d_w_key = ein("std,ste->de", normed, d_key_pre)
    d_w_value = ein("std,ste->de", normed, d_values)
    d_normed_part = d_normed_mlp + ein("ste,de->std", d_query_pre, w_query)
    d_normed_part = d_normed_part + ein("ste,de->std", d_key_pre, w_key)
    d_normed_part = d_normed_part + ein("ste,de->std", d_values, w_value)
    d_normed = lax.psum(d_normed_part.astype(bf16), "mlp").astype(f32)
    d_gain = jnp.sum(d_normed * unit, (0, 1))
    d_bias = jnp.sum(d_normed, (0, 1))
    d_unit = d_normed * ln_gain
    d_inputs = inv_std * (
        d_unit - jnp.mean(d_unit, -1, keepdims=True) - unit * jnp.mean(d_unit * unit, -1, keepdims=True)
    )
    d_tokens = (cot.astype(f32) + d_inputs).astype(bf16)

    def total(v):
        return lax.psum(v.astype(bf16), "seq").astype(f32)

    return (
        mixed[None],
        d_tokens[None],
        total(d_gain),
        total(d_bias),
        total(d_w_query),
        total(d_w_key),
        total(d_w_value),
        total(d_w_attn_out),
        total(d_w_in),
        total(d_b_in),
        total(d_w_mlp_out),
        total(d_b_out),
    )


anywhere = pl.BlockSpec(memory_space=pl.ANY)


class Placed(list):
    def add(self, *arrays):
        self.extend(arrays)

    def pin(self, x):
        return pltpu.with_memory_space_constraint(x, pltpu.HBM) if any(x is y for y in self) else x


in_hbm = Placed()


def call(
    kernel, grid, ins, in_specs, out_specs, out_shape, us, after=(), scalars=(), scratch=(), alias=None, vmem=24, free_out=()
):
    used = len(scalars) + len(ins)

    def body(*refs):
        kernel(*refs[:used], *refs[used + len(after) :])

    one = not isinstance(out_shape, list)
    shapes = [out_shape] if one else out_shape
    shapes = [s if i in free_out else pltpu.HBM(s.shape, s.dtype) for i, s in enumerate(shapes)]
    results = pl.pallas_call(
        body,
        name=getattr(kernel, "func", kernel).__name__.strip("<>"),
        grid_spec=pltpu.PrefetchScalarGridSpec(
            num_scalar_prefetch=len(scalars),
            grid=grid,
            in_specs=list(in_specs) + [anywhere] * len(after),
            out_specs=out_specs,
            scratch_shapes=list(scratch),
        ),
        out_shape=shapes[0] if one else shapes,
        input_output_aliases={len(scalars) + k: v for k, v in (alias or {}).items()},
        compiler_params=pltpu.CompilerParams(vmem_limit_bytes=vmem * 2**20),
        cost_estimate=pl.CostEstimate(flops=int(us * 1e11), bytes_accessed=0, transcendentals=0),
    )(*scalars, *map(in_hbm.pin, ins), *map(in_hbm.pin, after))
    in_hbm.add(*[r for i, r in enumerate([results] if one else results) if i not in free_out])
    return results


def fence(x, *after):
    known = any(x is y for y in in_hbm)
    return call(
        lambda *refs: None,
        (1,),
        (x,),
        [anywhere],
        anywhere,
        shape_of(*x.shape, dtype=x.dtype),
        1,
        after,
        alias={0: 0},
        vmem=1,
        free_out=() if known else (0,),
    )


def dot(a, b):
    return jnp.dot(a, b, preferred_element_type=f32)


def dot_nt(a, b):
    return lax.dot_general(a, b, (((1,), (1,)), ((), ())), preferred_element_type=f32)


def dot_tn(a, b):
    return lax.dot_general(a, b, (((0,), (0,)), ((), ())), preferred_element_type=f32)


def whole(x):
    return pl.BlockSpec(x.shape, lambda *_: (0,) * x.ndim, pipeline_mode=pl.Buffered(1))


def mine(rows):
    return pl.BlockSpec((rows, 2 * HEAD_DIM), lambda i, at: (at[0], 0), pipeline_mode=pl.Buffered(1))


def shape_of(*shape, dtype=bf16):
    return jax.ShapeDtypeStruct(shape, dtype)


def unit_rows(x):
    average = jnp.mean(x, -1, keepdims=True)
    centred = x - average
    inv_std = lax.rsqrt(jnp.mean(centred * centred, -1, keepdims=True) + epsilon)
    return centred * inv_std, inv_std


def half_swap(low, high, lane, keep_low):
    if keep_low:
        return jnp.where(lane < HEAD_DIM, low, pltpu.roll(high, HEAD_DIM, 1))
    return jnp.where(lane < HEAD_DIM, pltpu.roll(low, HEAD_DIM, 1), high)


def rope_tile(v, cosine, from_right, from_left):
    width = v.shape[1]
    return v * cosine + pltpu.roll(v, width - 1, 1) * from_right + pltpu.roll(v, 1, 1) * from_left


def position_tables(total):
    column = np.arange(2 * HEAD_DIM) % HEAD_DIM
    freq = np.float32(10000.0) ** (np.float32(-2.0 / ROT) * (column // 2).astype(np.float32))
    angle = np.arange(total, dtype=np.float32)[:, None] * freq.astype(np.float32)[None, :]
    active = (column < ROT)[None, :]
    cosine = np.where(active, np.cos(angle.astype(np.float64)), 1.0).astype(np.float32)
    sine = np.where(active, np.sin(angle.astype(np.float64)), 0.0).astype(np.float32)
    return cosine, sine


def signed(cosine, sine):
    even = lax.broadcasted_iota(jnp.int32, sine.shape, 1) % 2 == 0
    return cosine, jnp.where(even, -sine, 0.0), jnp.where(even, 0.0, sine)


def pre_kernel(shard_ref, x_ref, g_ref, gain, bias, wq, wk, wv, wo, cosine, sine, *rest):
    normed_ref, packed_ref = rest[-2:]
    unit, _ = unit_rows(x_ref[0].astype(f32))
    normed = (unit * gain[...] + bias[...]).astype(bf16)
    normed_ref[...] = normed
    q, k, v = dot(normed, wq[...]), dot(normed, wk[...]), dot(normed, wv[...])
    a = dot_nt(g_ref[0], wo[...])
    tables = signed(cosine[...], sine[...])
    lane = lax.broadcasted_iota(jnp.int32, tables[0].shape, 1)
    for tile in range(q.shape[1] // 128):
        cols = slice(tile * 128, (tile + 1) * 128)
        qt, kt = rope_tile(q[:, cols], *tables), rope_tile(k[:, cols], *tables)
        for side in (0, 1):
            head = tile * 2 + side
            packed_ref[head, :, 0:128] = half_swap(qt, kt, lane, side == 0).astype(bf16)
            packed_ref[head, :, 128:256] = half_swap(v[:, cols], a[:, cols], lane, side == 0).astype(bf16)


def pre(c, count, shard, x, g, consts, tables, before):
    seqs, rows, width = x.shape
    heads = consts[2].shape[1] // HEAD_DIM
    by_seq = pl.BlockSpec((1, rows, width), lambda i, _: (c * count + i, 0, 0))
    ins, specs = (x, g) + consts + tables, [by_seq, by_seq] + [whole(w) for w in consts] + [mine(rows)] * 2
    alias = {}
    if before is not None:
        alias = {len(ins): 0}
        ins, specs = ins + (before,), specs + [anywhere]
    return call(
        pre_kernel,
        (count,),
        ins,
        specs,
        [
            pl.BlockSpec((rows, width), lambda i, _: (c * count + i, 0)),
            pl.BlockSpec((heads, rows, 4 * HEAD_DIM), lambda i, _: (i, 0, 0)),
        ],
        [shape_of(seqs * rows, width), shape_of(count * heads, rows, 4 * HEAD_DIM)],
        3,
        scalars=(shard,),
        alias=alias,
        free_out=(1,),
    )


def mlp_kernel(n_ref, g_ref, w_in, b_in, w_out, *rest):
    hidden_ref, dgate_ref, part_ref, dn_ref, db_in, db_out = rest[-6:]
    c0, c1 = 0.7978845608028654, 0.044715
    g = g_ref[...]
    gate = dot(n_ref[...], w_in[...]) + b_in[...]
    square = gate * gate
    tanh = jnp.tanh(c0 * gate * (1.0 + c1 * square))
    left = 0.5 * (1.0 + tanh)
    hidden = (gate * left).astype(bf16)
    slope = left + 0.5 * gate * (1.0 - tanh * tanh) * (c0 * (1.0 + 3.0 * c1 * square))
    dgate = (dot_nt(g, w_out[...]) * slope).astype(bf16)
    hidden_ref[...] = hidden
    dgate_ref[...] = dgate
    part_ref[...] = dot(hidden, w_out[...]).astype(bf16)
    dn_ref[...] = dot_nt(dgate, w_in[...]).astype(bf16)

    @pl.when(pl.program_id(0) == 0)
    def _():
        db_in[...] = jnp.zeros_like(db_in)
        db_out[...] = jnp.zeros_like(db_out)

    db_in[...] += jnp.sum(dgate.astype(f32), 0, keepdims=True)
    db_out[...] += jnp.sum(g.astype(f32), 0, keepdims=True)


def mlp(c, count, rows, normed, g, w_in, b_in, w_out, before, after):
    total, width = g.shape
    ff = w_in.shape[1]
    there = lambda w: pl.BlockSpec((rows, w), lambda i: (c * count + i, 0))
    here = lambda w: pl.BlockSpec((rows, w), lambda i: (i, 0))
    one = lambda w: pl.BlockSpec((1, w), lambda i: (0, 0))
    ins = (normed, g, w_in, b_in, w_out)
    specs = [there(width), there(width), whole(w_in), whole(b_in), whole(w_out)]
    alias = {}
    if before is not None:
        alias = {len(ins): 0, len(ins) + 1: 1}
        ins, specs = ins + tuple(before), specs + [anywhere] * 2
    return call(
        mlp_kernel,
        (count,),
        ins,
        specs,
        [there(ff), there(ff), here(width), here(width), one(ff), one(width)],
        [
            shape_of(total, ff),
            shape_of(total, ff),
            shape_of(count * rows, width),
            shape_of(count * rows, width),
            shape_of(1, ff, dtype=f32),
            shape_of(1, width, dtype=f32),
        ],
        5,
        after,
        alias=alias,
        vmem=32,
    )


def dense_grads_kernel(core_ref, n_ref, dgate_ref, hidden_ref, g_ref, give_ref, keep_ref):
    step, half = pl.program_id(0), pl.num_programs(0) // 2
    both = dot_tn(n_ref[...], dgate_ref[...]).astype(bf16), dot_tn(hidden_ref[...], g_ref[...]).astype(bf16)

    @pl.when(step < half)
    def _():
        give_ref[0], give_ref[1] = both

    @pl.when(step >= half)
    def _():
        keep_ref[0], keep_ref[1] = both


def halves(steps, rows, wide, slots):
    half = steps // 2

    def place(i, core):
        return jnp.where(i < half, (1 - core[0]) * half + i, core[0] * half + i - half)

    cols = lambda total: pl.BlockSpec((total, rows), lambda i, core: (0, place(i, core)))
    give = pl.BlockSpec((slots, rows, wide), lambda i, core: (0, jnp.minimum(i, half - 1), 0))
    keep = pl.BlockSpec((slots, rows, wide), lambda i, core: (0, jnp.maximum(i - half, 0), 0))
    return cols, [give, keep]


def dense_grads(core, normed, dgate, hidden, g, loose, steps=4):
    total, width = g.shape
    cols, outs = halves(steps, width // steps, width, 2)
    return call(
        dense_grads_kernel,
        (steps,),
        (normed, dgate, hidden, g),
        [cols(total), whole(dgate), cols(total), whole(g)],
        outs,
        [shape_of(2, width // 2, width)] * 2,
        6,
        scalars=(core,),
        after=loose,
    )


def post_kernel(place_ref, back_ref, x_ref, part_ref, dn_ref, b_out, wq, wk, wv, wo, cosine, sine, *rest):
    give_ref, keep_ref, flat_ref, dgain, dbias = rest[-5:]
    tables = signed(cosine[...], sine[...])
    lane = lax.broadcasted_iota(jnp.int32, tables[0].shape, 1)
    inner = wo.shape[0]
    for tile in range(inner // 128):
        even, odd = back_ref[2 * tile].astype(f32), back_ref[2 * tile + 1].astype(f32)
        lows = half_swap(even[:, 0:128], odd[:, 0:128], lane, True)
        dq = half_swap(even[:, 0:128], odd[:, 0:128], lane, False)
        dk = half_swap(even[:, 128:256], odd[:, 128:256], lane, True)
        dv = half_swap(even[:, 128:256], odd[:, 128:256], lane, False)
        dq = rope_tile(dq, tables[0], -tables[1], -tables[2])
        dk = rope_tile(dk, tables[0], -tables[1], -tables[2])
        for which, value in enumerate((lows, dq, dk, dv)):
            at = which * inner + tile * 128
            flat_ref[:, at : at + 128] = value.astype(bf16)
    x = x_ref[0].astype(f32)
    z = place_ref[1]
    first = (z == 0).astype(f32)
    mixed = dot(flat_ref[:, 0:inner], wo[...]) + part_ref[...].astype(f32) + first * (x + b_out[...])
    dn = dn_ref[...].astype(f32)
    for which, w in enumerate((wq, wk, wv)):
        at = (which + 1) * inner
        dn = dn + dot_nt(flat_ref[:, at : at + inner], w[...])
    unit, _ = unit_rows(x)
    odd = z % 2 == 1
    half = dn.shape[0] // 2
    for which, share in enumerate((dn, mixed)):
        top, bottom = share[:half].astype(bf16), share[half:].astype(bf16)
        give_ref[0, which] = jnp.where(odd, top, bottom)
        keep_ref[0, which] = jnp.where(odd, bottom, top)

    @pl.when(pl.program_id(0) == 0)
    def _():
        dgain[...] = jnp.zeros_like(dgain)
        dbias[...] = jnp.zeros_like(dbias)

    dgain[...] += jnp.sum(dn * unit, 0, keepdims=True)
    dbias[...] += jnp.sum(dn, 0, keepdims=True)


def post(c, count, place, back, x, part, dn, consts, tables, before, after):
    seqs, rows, width = x.shape
    inner = consts[1].shape[1]
    heads = inner // HEAD_DIM
    here = pl.BlockSpec((rows, width), lambda i, _: (i, 0))
    one = pl.BlockSpec((1, width), lambda i, _: (0, 0))
    ins = (back, x, part, dn) + consts + tables
    specs = [
        pl.BlockSpec((heads, rows, 4 * HEAD_DIM), lambda i, _: (i, 0, 0)),
        pl.BlockSpec((1, rows, width), lambda i, _: (c * count + i, 0, 0)),
        here,
        here,
    ]
    specs += [whole(w) for w in consts] + [mine(rows)] * 2
    alias = {}
    if before is not None:
        alias = {len(ins): 2}
        ins, specs = ins + (before,), specs + [anywhere]
    share_spec = pl.BlockSpec((1, 2, rows // 2, width), lambda i, place: (i ^ (place[1] // 2), 0, 0, 0))
    return call(
        post_kernel,
        (count,),
        ins,
        specs,
        [share_spec] * 2 + [pl.BlockSpec((rows, 4 * inner), lambda i, _: (c * count + i, 0)), one, one],
        [shape_of(count, 2, rows // 2, width)] * 2
        + [shape_of(seqs * rows, 4 * inner)]
        + [shape_of(1, width, dtype=f32)] * 2,
        4,
        after,
        (place,),
        alias=alias,
    )


def head_grads_kernel(core_ref, n_ref, g_ref, flat_ref, small_ref, give_ref, keep_ref, *, inner):
    step, half = pl.program_id(0), pl.num_programs(0) // 2
    out = dot_tn(g_ref[...], flat_ref[:, 0:inner])
    rest = dot_tn(n_ref[...], flat_ref[:, inner:])

    @pl.when(step < half)
    def _():
        give_ref[0, :, 0:inner] = out.astype(bf16)
        give_ref[0, :, inner:] = rest.astype(bf16)

    @pl.when(step >= half)
    def _():
        give_ref[0, 0 : small_ref.shape[0]] = small_ref[...]
        keep_ref[0, :, 0:inner] = out.astype(bf16)
        keep_ref[0, :, inner:] = rest.astype(bf16)


def head_grads(core, normed, g, flat, small, after, steps=4):
    total, width = g.shape
    wide = flat.shape[1]
    rows, half = width // steps, steps // 2
    cols, (_, keep) = halves(steps, rows, wide, 1)
    give = pl.BlockSpec((1, rows, wide), lambda i, core: (0, jnp.minimum(i, half), 0))
    return call(
        partial(head_grads_kernel, inner=wide // 4),
        (steps,),
        (normed, g, flat, small),
        [cols(total), cols(total), whole(flat), whole(small)],
        [give, keep],
        [shape_of(1, (half + 1) * rows, wide), shape_of(1, half * rows, wide)],
        4,
        after,
        (core,),
    )


def split_kernel(keep_ref, got_ref, *rest, small):
    out_ref, token_ref = rest[-2:]
    token_ref[...] = jnp.zeros_like(token_ref)
    rows = keep_ref.shape[1]
    out_ref[0, :, 0:rows] = (keep_ref[...].astype(f32) + got_ref[...].astype(f32)).astype(bf16)
    if small:
        own, got = rest[0], rest[1]
        out_ref[0, 0, rows:] = (own[...].astype(f32) + got[0].astype(f32)).astype(bf16)


def split(keep, got, small, chips, after):
    slots, total, wide = keep.shape
    rows = total // chips
    block = pl.BlockSpec((slots, rows, wide), lambda k: (0, k, 0))
    ins, specs, extra = (keep, got), [block, block], 0
    if small is not None:
        extra = small.shape[0]
        ins += (small, got)
        specs += [whole(small), pl.BlockSpec((1, extra, wide), lambda k: (0, total // extra, 0))]
    return call(
        partial(split_kernel, small=extra > 0),
        (chips,),
        ins,
        specs,
        [pl.BlockSpec((1, slots, rows + extra, wide), lambda k: (k, 0, 0, 0)), pl.BlockSpec((8, 128), lambda k: (0, 0))],
        [shape_of(chips, slots, rows + extra, wide), shape_of(8, 128, dtype=f32)],
        2,
        after,
        vmem=16,
    )


def total_kernel(parts_ref, out_ref, token_ref):
    token_ref[...] = jnp.zeros_like(token_ref)
    total = parts_ref[0].astype(f32)
    for k in range(1, parts_ref.shape[0]):
        total = total + parts_ref[k].astype(f32)
    for k in range(out_ref.shape[0]):
        out_ref[k] = total.astype(bf16)


def total(parts, copies, loose):
    chips, slots, rows, wide = parts.shape
    steps = 2 * slots
    block = lambda n: pl.BlockSpec((n, 1, rows, wide // 2), lambda i: (0, i // 2, 0, i % 2))
    return call(
        total_kernel,
        (steps,),
        (parts,),
        [block(chips)],
        [block(copies), pl.BlockSpec((8, 128), lambda i: (0, 0))],
        [shape_of(copies, slots, rows, wide), shape_of(8, 128, dtype=f32)],
        2,
        vmem=16,
        after=loose,
    )


def widened(at_ref, own_ref, other_ref, stage, in_sems, take):
    chips = own_ref.shape[0]
    loads = [
        pltpu.make_async_copy((own_ref, other_ref)[i // chips].at[i % chips], stage.at[i], in_sems.at[i])
        for i in range(2 * chips)
    ]
    for load in loads:
        load.start()
    stores = []
    for i, load in enumerate(loads):
        load.wait()
        spot = (at_ref[0] ^ (i // chips)) * chips + (at_ref[1] ^ (i % chips))
        for store in take(i, spot):
            store.start()
            stores.append(store)
    for store in stores:
        store.wait()


def dense_outs_kernel(at_ref, own_ref, other_ref, out_in, out_out, stage, wide_stage, in_sems, out_sems):
    rows = stage.shape[2]

    def take(i, spot):
        for which, out in enumerate((out_in, out_out)):
            wide_stage[i, which] = stage[i, which].astype(f32)
            here = out.at[pl.ds(spot * rows, rows)]
            yield pltpu.make_async_copy(wide_stage.at[i, which], here, out_sems.at[i, which])

    widened(at_ref, own_ref, other_ref, stage, in_sems, take)


def head_outs_kernel(at_ref, own_ref, other_ref, out_t, out_q, out_k, out_v, stage, turned, wide_stage, in_sems, out_sems):
    rows, inner = wide_stage.shape[2:]

    def take(i, spot):
        here = pl.ds(spot * rows, rows)
        turned[i] = stage[i, 0, 0:rows, 0:inner].astype(f32).T
        yield pltpu.make_async_copy(turned.at[i], out_t.at[:, here], out_sems.at[i, 0])
        for which, out in enumerate((out_q, out_k, out_v)):
            cols = slice((which + 1) * inner, (which + 2) * inner)
            wide_stage[i, which] = stage[i, 0, 0:rows, cols].astype(f32)
            yield pltpu.make_async_copy(wide_stage.at[i, which], out.at[here], out_sems.at[i, which + 1])

    widened(at_ref, own_ref, other_ref, stage, in_sems, take)


def dense_outs(at, own, other, width, after):
    chips, slots, rows, wide = own.shape
    dma = pltpu.SemaphoreType.DMA
    return call(
        dense_outs_kernel,
        (1,),
        (own, other),
        [anywhere] * 2,
        [anywhere] * 2,
        [shape_of(width, wide, dtype=f32)] * 2,
        4,
        after,
        (at,),
        [
            pltpu.VMEM((2 * chips, slots, rows, wide), bf16),
            pltpu.VMEM((2 * chips, slots, rows, wide), f32),
            dma((2 * chips,)),
            dma((2 * chips, slots)),
        ],
        vmem=20,
    )


def head_outs(at, own, other, width, after):
    chips, slots, tall, wide = own.shape
    rows, inner = width // (2 * chips), wide // 4
    dma = pltpu.SemaphoreType.DMA
    return call(
        head_outs_kernel,
        (1,),
        (own, other),
        [anywhere] * 2,
        [anywhere] * 4,
        [shape_of(inner, width, dtype=f32)] + [shape_of(width, inner, dtype=f32)] * 3,
        3,
        after,
        (at,),
        [
            pltpu.VMEM((2 * chips, slots, tall, wide), bf16),
            pltpu.VMEM((2 * chips, inner, rows), f32),
            pltpu.VMEM((2 * chips, 3, rows, inner), f32),
            dma((2 * chips,)),
            dma((2 * chips, 4)),
        ],
        vmem=16,
    )


def input_grad(x, g, dn, gain):
    unit, inv_std = unit_rows(x.astype(f32))
    du = dn.astype(f32) * gain
    d = inv_std * (du - jnp.mean(du, -1, keepdims=True) - unit * jnp.mean(du * unit, -1, keepdims=True))
    return (g.astype(f32) + d).astype(bf16)


def pair_sum_kernel(keep_ref, got_ref, own_ref, other_ref):
    for at, ref in enumerate((own_ref, other_ref)):

        @pl.when(pl.program_id(0) == at)
        def _():
            ref[...] = (keep_ref[0].astype(f32) + got_ref[0].astype(f32)).astype(bf16)


def pair_sum(keep, got, after):
    _, _, rows, width = keep.shape
    block = pl.BlockSpec((1, 2, rows, width), lambda i: (i, 0, 0, 0))
    out = pl.BlockSpec((2, rows, width), lambda i: (0, 0, 0))
    return call(
        pair_sum_kernel, (2,), (keep, got), [block, block], [out, out], [shape_of(2, rows, width)] * 2, 1, after, vmem=12
    )


def own_quarter_kernel(place_ref, x_ref, g_ref, own_ref, got_ref, gain, out_ref, again_ref):
    total = own_ref[...].astype(f32) + got_ref[...].astype(f32)
    tokens = input_grad(x_ref[0], g_ref[0], total[0], gain[...])
    mixed = total[1].astype(bf16)
    for ref in (out_ref, again_ref):
        ref[0] = tokens
        ref[1] = mixed


def own_quarter(place, start, x, g, own, got, gain, loose):
    _, rows, width = own.shape
    per = x.shape[1] // rows
    block = pl.BlockSpec((1, rows, width), lambda i, place: (start + place[1] // per, place[1] % per, 0))
    return call(
        own_quarter_kernel,
        (1,),
        (x, g, own, got, gain),
        [block, block, whole(own), whole(got), whole(gain)],
        [pl.BlockSpec(own.shape, lambda i, _: (0, 0, 0))] * 2,
        [shape_of(*own.shape)] * 2,
        2,
        scalars=(place,),
        vmem=12,
        after=loose,
    )


def placed_kernel(place_ref, *refs, pieces, start):
    tokens_ref, mixed_ref, stage, in_sems, out_sems = refs[-5:]
    rows = stage.shape[2]
    per = tokens_ref.shape[1] // rows
    loads = [pltpu.make_async_copy(ref, stage.at[at], in_sems.at[at]) for at, ref in enumerate(refs[:pieces])]
    for load in loads:
        load.start()
    stores = []
    for at, load in enumerate(loads):
        load.wait()
        quarter = place_ref[1] ^ at
        spot = start + quarter // per, pl.ds((quarter % per) * rows, rows)
        for which, out in enumerate((tokens_ref, mixed_ref)):
            stores.append(pltpu.make_async_copy(stage.at[at, which], out.at[spot], out_sems.at[at, which]))
            stores[-1].start()
    for store in stores:
        store.wait()


def placed(place, shape, start, pieces, before, after):
    ins, alias, count = tuple(pieces), {}, len(pieces)
    if before is not None:
        alias = {count: 0, count + 1: 1}
        ins += tuple(before)
    dma = pltpu.SemaphoreType.DMA
    return call(
        partial(placed_kernel, pieces=count, start=start),
        (1,),
        ins,
        [anywhere] * len(ins),
        [anywhere, anywhere],
        [shape_of(*shape)] * 2,
        2,
        after,
        (place,),
        [pltpu.VMEM((count,) + pieces[0].shape, bf16), dma((count,)), dma((count, 2))],
        alias,
        vmem=6,
    )


def exchanged(x, bits):
    return lax.ppermute(x, "seq", [(i, i ^ bits) for i in range(lax.axis_size("seq"))])


def by_pairs(
    tokens, ln_gain, ln_bias, w_query, w_key, w_value, w_attn_out, w_in, b_in, w_mlp_out, b_out, cotangent
):
    x, cot = tokens[0], cotangent[0]
    seqs, rows, width = x.shape
    inner = w_query.shape[1]
    ff = w_in.shape[1]
    heads = inner // HEAD_DIM
    shards = lax.axis_size("seq")
    count = shards // heads
    in_hbm.clear()
    in_hbm.add(x, cot, w_query, w_key, w_value, w_attn_out, w_in, w_mlp_out)
    row = lambda v: v.reshape(1, -1)
    gain, b_in, b_out = row(ln_gain), row(b_in), row(b_out)
    flat_cot = cot.reshape(-1, width)
    in_hbm.add(flat_cot)
    shard = lax.axis_index("seq").astype(jnp.int32)
    core, chip, chips = (shard % 2).reshape(1), (shard // 2).reshape(1), shards // 2
    z = lax.axis_index("mlp").astype(jnp.int32)
    place = jnp.stack([shard, z])
    tables = tuple(map(jnp.asarray, position_tables(shards * rows)))
    in_hbm.add(*tables)
    weights = (w_query, w_key, w_value, w_attn_out)
    pre_consts = (gain, row(ln_bias)) + weights
    post_consts = (b_out,) + weights

    def attend(sent, after):
        done = attention(sent.reshape(1, shards * rows, 4 * HEAD_DIM), after)
        return done.reshape(shards, rows, 4 * HEAD_DIM)

    def traded(v):
        return lax.all_to_all(v, "seq", 0, 0, tiled=True)

    def over_line(v, bits):
        return lax.ppermute(v, "mlp", [(i, i ^ bits) for i in range(4)])

    dense_args = (flat_cot, w_in, b_in, w_mlp_out)
    normed, packed_a = pre(0, count, place, x, cot, pre_consts, tables, None)
    sent_a = traded(packed_a)
    normed, packed_b = pre(1, count, place, x, cot, pre_consts, tables, normed)
    hidden, dgate, part_a, dn_a, db_in_a, db_out_a = mlp(0, count, rows, normed, *dense_args, None, (packed_b,))
    done_a = attend(sent_a, (db_in_a,))
    back_a = traded(done_a)
    hidden, dgate, part_b, dn_b, db_in_b, db_out_b = mlp(1, count, rows, normed, *dense_args, (hidden, dgate), (done_a,))
    sent_b = traded(fence(packed_b, back_a, db_in_b))
    give_a, keep_a, flat, gain_a, bias_a = post(
        0, count, place, back_a, x, part_a, dn_a, post_consts, tables, None, (db_in_b,)
    )
    got_a = over_line(give_a, 1)
    done_b = attend(sent_b, (gain_a,))
    back_b = traded(done_b)
    own_a, other_a = pair_sum(keep_a, got_a, (done_b,))
    got_a = over_line(other_a, 2)
    give_e, keep_e = dense_grads(core, normed, dgate, hidden, flat_cot, (own_a,))
    got_e = exchanged(give_e, 1)
    give_b, keep_b, flat, gain_b, bias_b = post(
        1, count, place, back_b, x, part_b, dn_b, post_consts, tables, flat, (keep_e,)
    )

    def over_chips(v):
        same_core = [list(range(side, shards, 2)) for side in (0, 1)]
        return lax.all_to_all(v, "seq", 0, 0, axis_index_groups=same_core, tiled=True)

    dense, token = split(keep_e, got_e, None, chips, (gain_b,))
    dense = over_chips(dense)
    done_a, more_a = own_quarter(place, 0, x, cot, own_a, got_a, gain, (token,))
    small = jnp.concatenate([gain_a + gain_b, bias_a + bias_b, db_in_a + db_in_b, db_out_a + db_out_b], 0)
    small = jnp.concatenate([small, jnp.zeros((12, width), f32)], 0).astype(bf16)
    give_l, keep_l = head_grads(core, normed, flat_cot, flat, small, (more_a,))
    far_a = over_line(more_a, 2)
    got_b = over_line(give_b, 1)
    own_b, other_b = pair_sum(keep_b, got_b, (keep_l,))
    near_a = over_line(fence(done_a, own_b), 1)
    got_b = over_line(other_b, 2)
    got_l = exchanged(give_l, 1)
    head, token = split(keep_l, got_l, small, chips, (own_b,))
    dense, token = total(dense, 1, (token,))
    head = over_chips(fence(head, token))
    dense = [dense[0]] + [exchanged(dense[0], 2 * k) for k in range(1, chips)]
    far_a = fence(far_a, token)
    beside_a = over_line(far_a, 1)
    near_a = fence(near_a, far_a)
    done_b, more_b = own_quarter(place, count, x, cot, own_b, got_b, gain, (near_a,))
    near_b = over_line(done_b, 1)
    far_b = over_line(more_b, 2)
    dense = jnp.stack([dense[0]] + [fence(v, done_b) for v in dense[1:]])
    dense_other = exchanged(dense, 1)
    head, token = total(head, chips, (dense,))
    small = head[0, 0, -small.shape[0] :].astype(f32)
    vectors = small[:2]
    vectors_got = over_line(vectors, 1)
    head = over_chips(head)
    far_b = fence(far_b, token)
    beside_b = over_line(far_b, 1)
    dense_other = fence(dense_other, far_b)
    d_in, d_out = dense_outs(jnp.concatenate([core, chip]), dense, dense_other, width, (far_b,))
    beside_a = fence(beside_a, d_out)
    d_tokens, mixed = placed(place, x.shape, 0, (more_a, near_a, far_a, beside_a), None, (beside_a,))
    head = fence(head, d_tokens)
    head_other = exchanged(head, 1)
    near_b = fence(near_b, head)
    beside_b = fence(beside_b, near_b)
    d_tokens, mixed = placed(place, x.shape, count, (more_b, near_b, far_b, beside_b), (d_tokens, mixed), (beside_b,))
    vectors = vectors + fence(vectors_got, d_tokens)
    vectors_got = over_line(vectors, 2)
    head_other = fence(head_other, d_tokens)
    d_attn_out, d_query, d_key, d_value = head_outs(
        jnp.concatenate([core, jnp.zeros_like(core)]), head, head_other, width, (d_tokens,)
    )
    vectors = vectors + fence(vectors_got, d_value)
    return (
        mixed.reshape(tokens.shape),
        d_tokens[None],
        vectors[0],
        vectors[1],
        d_query,
        d_key,
        d_value,
        d_attn_out,
        d_in,
        small[2],
        d_out,
        small[3],
    )


def per_device(
    tokens, ln_gain, ln_bias, w_query, w_key, w_value, w_attn_out, w_in, b_in, w_mlp_out, b_out, cotangent
):
    _, seqs, rows, width = tokens.shape
    inner = w_query.shape[1]
    heads = inner // HEAD_DIM
    shards = lax.axis_size("seq")
    fits = shards == 8 and lax.axis_size("mlp") == 4 and seqs * heads == 2 * shards and shards % heads == 0
    fits = fits and inner % 128 == 0 and rows % 256 == 0 and width % 1024 == 0 and w_in.shape[1] == width
    fits = fits and 4 * inner == width
    plan = by_pairs if fits else by_ring
    return plan(
        tokens, ln_gain, ln_bias, w_query, w_key, w_value, w_attn_out, w_in, b_in, w_mlp_out, b_out, cotangent
    )


def solution(mesh):
    rows, whole = P("seq", None, None, None), P()
    cols, down = P(None, "mlp"), P("mlp", None)
    return jax.shard_map(
        per_device,
        mesh=mesh,
        in_specs=(rows, whole, whole, cols, cols, cols, down, cols, P("mlp"), down, whole, rows),
        out_specs=(rows, rows, whole, whole, cols, cols, cols, down, cols, P("mlp"), down, whole),
        check_vma=False,
    )
```

```python
from functools import partial

import jax
import jax.numpy as jnp
import numpy as np
from jax import lax
from jax.experimental import pallas as pl
from jax.experimental.pallas import tpu as pltpu
from jax.sharding import PartitionSpec as P

HEAD_DIM = 64
ROT = 32

epsilon = 1e-05
neg_big = -1e30
bf16 = jnp.bfloat16
f32 = jnp.float32


def passed_along(x, axis, by):
    peers = lax.axis_size(axis)
    pairs = [(i, i + by) for i in range(peers) if 0 <= i + by < peers]
    return lax.ppermute(x, axis, pairs)


def rotary_tables(positions, width):
    column = jnp.arange(width, dtype=jnp.int32) % HEAD_DIM
    pairs = (column // 2).astype(f32)
    freq = 10000.0 ** (-2.0 * pairs / ROT)
    angle = positions.astype(f32)[:, None] * freq[None, :]
    active = (column < ROT)[None, :]
    even = (column % 2 == 0)[None, :]
    cosine = jnp.where(active, jnp.cos(angle), 1.0)
    sine = jnp.where(active, jnp.sin(angle), 0.0)
    return cosine, jnp.where(even, -sine, 0.0), jnp.where(even, 0.0, sine)


def rotate(v, tables, sign):
    cosine, from_right, from_left = tables
    right = jnp.concatenate([v[..., 1:], v[..., :1]], -1)
    left = jnp.concatenate([v[..., -1:], v[..., :-1]], -1)
    return v * cosine + sign * (right * from_right + left * from_left)


def attention_kernel(x_ref, out_ref, xt, acc, sbuf, *, length, hd, tq, tk):
    xt[...] = x_ref[0].T
    scale = hd**-0.5
    nt = (((1,), (1,)), ((), ()))
    zero = jnp.zeros((hd, tq), bf16)

    def put(old, new, q0, join):
        if old is None:
            return new
        if q0 == 0:
            return join(old, new)
        return jnp.concatenate([old[:, :q0], join(old[:, q0:], new)], 1)

    add = lambda u, v: u + v
    for i in range(length // tq):
        first = i * tq
        qs = (xt[0:hd, first : first + tq].astype(f32) * scale).astype(bf16)
        at = xt[3 * hd : 4 * hd, first : first + tq].astype(f32)
        zq = jnp.concatenate([zero, qs], 0)
        qz = jnp.concatenate([qs, zero], 0)
        steps = [(k0, k0 + tk, 0) for k0 in range(0, first, tk)]
        steps += [(first + q0, first + q0 + tk // 2, q0) for q0 in range(0, tq, tk // 2)]
        top = None
        for k0, k1, q0 in steps:
            st = jnp.dot(x_ref[0, k0:k1, 0 : 2 * hd], zq[:, q0:], preferred_element_type=f32)
            if k0 >= first:
                kp = lax.broadcasted_iota(jnp.int32, st.shape, 0)
                qp = lax.broadcasted_iota(jnp.int32, st.shape, 1)
                st = jnp.where(kp <= qp, st, neg_big)
            sbuf[k0:k1, q0:] = st
            top = put(top, jnp.max(st, 0, keepdims=True), q0, jnp.maximum)
        tot = None
        ot = None
        for k0, k1, q0 in steps:
            e = jnp.exp(sbuf[k0:k1, q0:] - top[:, q0:])
            sbuf[k0:k1, q0:] = e
            tot = put(tot, jnp.sum(e, 0, keepdims=True), q0, add)
            ot = put(ot, jnp.dot(xt[2 * hd : 3 * hd, k0:k1], e.astype(bf16), preferred_element_type=f32), q0, add)
        r = 1.0 / tot
        ot = ot * r
        ar = (at * r).astype(bf16)
        spread = jnp.sum(ar.astype(f32) * ot, 0, keepdims=True)
        az = jnp.concatenate([ar, zero], 0)
        za = jnp.concatenate([zero, ar], 0)
        dqt = None
        for k0, k1, q0 in steps:
            dp = jnp.dot(x_ref[0, k0:k1, 2 * hd : 4 * hd], az[:, q0:], preferred_element_type=f32)
            e = sbuf[k0:k1, q0:]
            ds = (e * (dp - spread[:, q0:])).astype(bf16)
            dqt = put(dqt, jnp.dot(xt[hd : 2 * hd, k0:k1], ds, preferred_element_type=f32), q0, add)
            both = lax.dot_general(ds, qz[:, q0:], nt, preferred_element_type=f32) + lax.dot_general(
                e.astype(bf16), za[:, q0:], nt, preferred_element_type=f32
            )
            if k0 < first:
                both = acc[k0:k1, :] + both
            acc[k0:k1, :] = both
        both = jnp.concatenate([ot, dqt * scale], 0)
        out_ref[0, first : first + tq, 0 : 2 * hd] = both.T.astype(bf16)
    out_ref[0, :, 2 * hd : 4 * hd] = acc[...].astype(bf16)


def attention(x, after=()):
    n, length, width = x.shape
    hd = width // 4
    tq = 512 if length % 512 == 0 else 256
    spec = pl.BlockSpec((1, length, width), lambda i: (i, 0, 0))
    return call(
        partial(attention_kernel, length=length, hd=hd, tq=tq, tk=512),
        (n,),
        (x,),
        [spec],
        spec,
        shape_of(*x.shape),
        7,
        after,
        scratch=[pltpu.VMEM((width, length), bf16), pltpu.VMEM((length, 2 * hd), f32), pltpu.VMEM((length, tq), f32)],
        vmem=32,
        free_out=(0,),
    )


def ring_attention(q, k, v, a):
    seq_count, row_count, inner_width = q.shape
    score_scale = HEAD_DIM ** (-0.5)
    shard_total = lax.axis_size("seq")
    my_shard = lax.axis_index("seq")
    heads_of = lambda x: x.reshape(seq_count, row_count, inner_width // HEAD_DIM, HEAD_DIM)
    flat_of = lambda x: x.reshape(seq_count, row_count, inner_width)
    qh, gh = heads_of(q), heads_of(a)
    local = jnp.arange(row_count, dtype=jnp.int32)
    own_mask = local[:, None] >= local[None, :]
    ein = partial(jnp.einsum, preferred_element_type=f32)

    def attend_block(state, key_block, value_block, visible):
        running_max, exp_total, weighted = state
        raw = ein("sthd,suhd->shtu", qh, key_block) * score_scale
        raw = jnp.where(visible[None, None], raw, neg_big)
        new_max = jnp.maximum(running_max, jnp.max(raw, -1))
        weights = jnp.where(visible[None, None], jnp.exp(raw - new_max[..., None]), 0.0)
        shrink = jnp.exp(running_max - new_max)
        exp_total = exp_total * shrink + jnp.sum(weights, -1)
        weighted = weighted * jnp.transpose(shrink, (0, 2, 1))[..., None] + ein(
            "shtu,suhd->sthd", weights.astype(bf16), value_block
        )
        return (new_max, exp_total, weighted)

    head_count = inner_width // HEAD_DIM
    state = (
        jnp.full((seq_count, head_count, row_count), neg_big, f32),
        jnp.zeros((seq_count, head_count, row_count), f32),
        jnp.zeros(qh.shape, f32),
    )
    state = attend_block(state, heads_of(k), heads_of(v), own_mask)
    empty_stack = jnp.zeros((max(shard_total - 1, 1),) + q.shape, bf16)

    def forward_step(step, carry):
        state, near_keys, near_values, key_stack, value_stack = carry
        near_keys, near_values = passed_along((near_keys, near_values), "seq", 1)
        visible = jnp.broadcast_to(my_shard >= step, (row_count, row_count))
        state = attend_block(state, heads_of(near_keys), heads_of(near_values), visible)
        key_stack = lax.dynamic_update_index_in_dim(key_stack, near_keys, step - 1, 0)
        value_stack = lax.dynamic_update_index_in_dim(value_stack, near_values, step - 1, 0)
        return (state, near_keys, near_values, key_stack, value_stack)

    state, _, _, key_stack, value_stack = lax.fori_loop(
        1, shard_total, forward_step, (state, k, v, empty_stack, empty_stack)
    )
    running_max, exp_total, weighted = state
    log_total = running_max + jnp.log(exp_total)
    attended = weighted / jnp.transpose(exp_total, (0, 2, 1))[..., None]
    spread = jnp.transpose(jnp.sum(gh.astype(f32) * attended, -1), (0, 2, 1))

    def grads(key_block, value_block, visible):
        raw = ein("sthd,suhd->shtu", qh, key_block) * score_scale
        probs = jnp.where(visible[None, None], jnp.exp(raw - log_total[..., None]), 0.0)
        grad_probs = ein("sthd,suhd->shtu", gh, value_block)
        slopes = (probs * (grad_probs - spread[..., None])).astype(bf16)
        query_grad = ein("shtu,suhd->sthd", slopes, key_block) * score_scale
        key_grad = ein("shtu,sthd->suhd", slopes, qh) * score_scale
        value_grad = ein("shtu,sthd->suhd", probs.astype(bf16), gh)
        return query_grad, key_grad, value_grad

    d_query, d_keys, d_values = grads(heads_of(k), heads_of(v), own_mask)

    def return_step(index, carry):
        query_grad_total, travelling = carry
        step = shard_total - 1 - index
        near_keys = lax.dynamic_index_in_dim(key_stack, step - 1, 0, keepdims=False)
        near_values = lax.dynamic_index_in_dim(value_stack, step - 1, 0, keepdims=False)
        visible = jnp.broadcast_to(my_shard >= step, (row_count, row_count))
        query_grad, key_grad, value_grad = grads(heads_of(near_keys), heads_of(near_values), visible)
        joined = jnp.concatenate([flat_of(key_grad), flat_of(value_grad)], -1)
        travelling = passed_along((travelling + joined).astype(bf16), "seq", -1).astype(f32)
        return (query_grad_total + query_grad, travelling)

    start = jnp.zeros((seq_count, row_count, 2 * inner_width), f32)
    d_query, travelling = lax.fori_loop(0, shard_total - 1, return_step, (d_query, start))
    d_keys = flat_of(d_keys) + travelling[..., :inner_width]
    d_values = flat_of(d_values) + travelling[..., inner_width:]
    return tuple(x.astype(bf16) for x in (flat_of(attended), flat_of(d_query), d_keys, d_values))


def by_ring(
    tokens, ln_gain, ln_bias, w_query, w_key, w_value, w_attn_out, w_in, b_in, w_mlp_out, b_out, cotangent
):
    x_low = tokens[0]
    cot = cotangent[0]
    seqs, rows, width = x_low.shape
    inner = w_query.shape[1]
    my_shard = lax.axis_index("seq")
    ein = partial(jnp.einsum, preferred_element_type=f32)
    positions = my_shard * rows + jnp.arange(rows, dtype=jnp.int32)
    tables = rotary_tables(positions, inner)
    x = x_low.astype(f32)
    centred = x - jnp.mean(x, -1, keepdims=True)
    inv_std = lax.rsqrt(jnp.mean(centred * centred, -1, keepdims=True) + epsilon)
    unit = centred * inv_std
    normed = (unit * ln_gain + ln_bias).astype(bf16)
    query = rotate(ein("std,de->ste", normed, w_query), tables, 1.0).astype(bf16)
    keys = rotate(ein("std,de->ste", normed, w_key), tables, 1.0).astype(bf16)
    values = ein("std,de->ste", normed, w_value).astype(bf16)
    d_attended = ein("std,ed->ste", cot, w_attn_out).astype(bf16)

    attended, d_query, d_keys, d_values = ring_attention(query, keys, values, d_attended)

    gate_in = ein("std,df->stf", normed, w_in) + b_in
    hidden, gelu_pull = jax.vjp(partial(jax.nn.gelu, approximate=True), gate_in)
    hidden = hidden.astype(bf16)
    d_hidden = ein("std,fd->stf", cot, w_mlp_out)
    d_gate = gelu_pull(d_hidden)[0].astype(bf16)
    d_b_in = jnp.sum(d_gate, (0, 1), dtype=f32)
    d_b_out = jnp.sum(cot, (0, 1), dtype=f32)
    d_w_mlp_out = ein("stf,std->fd", hidden, cot)
    d_w_in = ein("std,stf->df", normed, d_gate)
    mlp_part = ein("stf,fd->std", hidden, w_mlp_out)
    d_normed_mlp = ein("stf,df->std", d_gate, w_in)

    attn_part = ein("ste,ed->std", attended, w_attn_out)
    branches = lax.psum((attn_part + mlp_part).astype(bf16), "mlp").astype(f32)
    mixed = (x + branches + b_out).astype(bf16)
    d_w_attn_out = ein("ste,std->ed", attended, cot)
    d_query_pre = rotate(d_query.astype(f32), tables, -1.0).astype(bf16)
    d_key_pre = rotate(d_keys.astype(f32), tables, -1.0).astype(bf16)
    d_w_query = ein("std,ste->de", normed, d_query_pre)
    d_w_key = ein("std,ste->de", normed, d_key_pre)
    d_w_value = ein("std,ste->de", normed, d_values)
    d_normed_part = d_normed_mlp + ein("ste,de->std", d_query_pre, w_query)
    d_normed_part = d_normed_part + ein("ste,de->std", d_key_pre, w_key)
    d_normed_part = d_normed_part + ein("ste,de->std", d_values, w_value)
    d_normed = lax.psum(d_normed_part.astype(bf16), "mlp").astype(f32)
    d_gain = jnp.sum(d_normed * unit, (0, 1))
    d_bias = jnp.sum(d_normed, (0, 1))
    d_unit = d_normed * ln_gain
    d_inputs = inv_std * (
        d_unit - jnp.mean(d_unit, -1, keepdims=True) - unit * jnp.mean(d_unit * unit, -1, keepdims=True)
    )
    d_tokens = (cot.astype(f32) + d_inputs).astype(bf16)

    def total(v):
        return lax.psum(v.astype(bf16), "seq").astype(f32)

    return (
        mixed[None],
        d_tokens[None],
        total(d_gain),
        total(d_bias),
        total(d_w_query),
        total(d_w_key),
        total(d_w_value),
        total(d_w_attn_out),
        total(d_w_in),
        total(d_b_in),
        total(d_w_mlp_out),
        total(d_b_out),
    )


anywhere = pl.BlockSpec(memory_space=pl.ANY)


class Placed(list):
    def add(self, *arrays):
        self.extend(arrays)

    def pin(self, x):
        return pltpu.with_memory_space_constraint(x, pltpu.HBM) if any(x is y for y in self) else x


in_hbm = Placed()


def call(
    kernel, grid, ins, in_specs, out_specs, out_shape, us, after=(), scalars=(), scratch=(), alias=None, vmem=24, free_out=()
):
    used = len(scalars) + len(ins)

    def body(*refs):
        kernel(*refs[:used], *refs[used + len(after) :])

    one = not isinstance(out_shape, list)
    shapes = [out_shape] if one else out_shape
    shapes = [s if i in free_out else pltpu.HBM(s.shape, s.dtype) for i, s in enumerate(shapes)]
    results = pl.pallas_call(
        body,
        name=getattr(kernel, "func", kernel).__name__.strip("<>"),
        grid_spec=pltpu.PrefetchScalarGridSpec(
            num_scalar_prefetch=len(scalars),
            grid=grid,
            in_specs=list(in_specs) + [anywhere] * len(after),
            out_specs=out_specs,
            scratch_shapes=list(scratch),
        ),
        out_shape=shapes[0] if one else shapes,
        input_output_aliases={len(scalars) + k: v for k, v in (alias or {}).items()},
        compiler_params=pltpu.CompilerParams(vmem_limit_bytes=vmem * 2**20),
        cost_estimate=pl.CostEstimate(flops=int(us * 1e11), bytes_accessed=0, transcendentals=0),
    )(*scalars, *map(in_hbm.pin, ins), *map(in_hbm.pin, after))
    in_hbm.add(*[r for i, r in enumerate([results] if one else results) if i not in free_out])
    return results


def fence(x, *after):
    known = any(x is y for y in in_hbm)
    return call(
        lambda *refs: None,
        (1,),
        (x,),
        [anywhere],
        anywhere,
        shape_of(*x.shape, dtype=x.dtype),
        1,
        after,
        alias={0: 0},
        vmem=1,
        free_out=() if known else (0,),
    )


def dot(a, b):
    return jnp.dot(a, b, preferred_element_type=f32)


def dot_nt(a, b):
    return lax.dot_general(a, b, (((1,), (1,)), ((), ())), preferred_element_type=f32)


def dot_tn(a, b):
    return lax.dot_general(a, b, (((0,), (0,)), ((), ())), preferred_element_type=f32)


def whole(x):
    return pl.BlockSpec(x.shape, lambda *_: (0,) * x.ndim, pipeline_mode=pl.Buffered(1))


def mine(rows):
    return pl.BlockSpec((rows, 2 * HEAD_DIM), lambda i, at: (at[0], 0), pipeline_mode=pl.Buffered(1))


def shape_of(*shape, dtype=bf16):
    return jax.ShapeDtypeStruct(shape, dtype)


def unit_rows(x):
    average = jnp.mean(x, -1, keepdims=True)
    centred = x - average
    inv_std = lax.rsqrt(jnp.mean(centred * centred, -1, keepdims=True) + epsilon)
    return centred * inv_std, inv_std


def half_swap(low, high, lane, keep_low):
    if keep_low:
        return jnp.where(lane < HEAD_DIM, low, pltpu.roll(high, HEAD_DIM, 1))
    return jnp.where(lane < HEAD_DIM, pltpu.roll(low, HEAD_DIM, 1), high)


def rope_tile(v, cosine, from_right, from_left):
    width = v.shape[1]
    return v * cosine + pltpu.roll(v, width - 1, 1) * from_right + pltpu.roll(v, 1, 1) * from_left


def position_tables(total):
    column = np.arange(2 * HEAD_DIM) % HEAD_DIM
    freq = np.float32(10000.0) ** (np.float32(-2.0 / ROT) * (column // 2).astype(np.float32))
    angle = np.arange(total, dtype=np.float32)[:, None] * freq.astype(np.float32)[None, :]
    active = (column < ROT)[None, :]
    cosine = np.where(active, np.cos(angle.astype(np.float64)), 1.0).astype(np.float32)
    sine = np.where(active, np.sin(angle.astype(np.float64)), 0.0).astype(np.float32)
    return cosine, sine


def signed(cosine, sine):
    even = lax.broadcasted_iota(jnp.int32, sine.shape, 1) % 2 == 0
    return cosine, jnp.where(even, -sine, 0.0), jnp.where(even, 0.0, sine)


def pre_kernel(shard_ref, x_ref, g_ref, gain, bias, wq, wk, wv, wo, cosine, sine, *rest):
    normed_ref, packed_ref = rest[-2:]
    unit, _ = unit_rows(x_ref[0].astype(f32))
    normed = (unit * gain[...] + bias[...]).astype(bf16)
    normed_ref[...] = normed
    q, k, v = dot(normed, wq[...]), dot(normed, wk[...]), dot(normed, wv[...])
    a = dot_nt(g_ref[0], wo[...])
    tables = signed(cosine[...], sine[...])
    lane = lax.broadcasted_iota(jnp.int32, tables[0].shape, 1)
    for tile in range(q.shape[1] // 128):
        cols = slice(tile * 128, (tile + 1) * 128)
        qt, kt = rope_tile(q[:, cols], *tables), rope_tile(k[:, cols], *tables)
        for side in (0, 1):
            head = tile * 2 + side
            packed_ref[head, :, 0:128] = half_swap(qt, kt, lane, side == 0).astype(bf16)
            packed_ref[head, :, 128:256] = half_swap(v[:, cols], a[:, cols], lane, side == 0).astype(bf16)


def pre(c, count, shard, x, g, consts, tables, before):
    seqs, rows, width = x.shape
    heads = consts[2].shape[1] // HEAD_DIM
    by_seq = pl.BlockSpec((1, rows, width), lambda i, _: (c * count + i, 0, 0))
    ins, specs = (x, g) + consts + tables, [by_seq, by_seq] + [whole(w) for w in consts] + [mine(rows)] * 2
    alias = {}
    if before is not None:
        alias = {len(ins): 0}
        ins, specs = ins + (before,), specs + [anywhere]
    return call(
        pre_kernel,
        (count,),
        ins,
        specs,
        [
            pl.BlockSpec((rows, width), lambda i, _: (c * count + i, 0)),
            pl.BlockSpec((heads, rows, 4 * HEAD_DIM), lambda i, _: (i, 0, 0)),
        ],
        [shape_of(seqs * rows, width), shape_of(count * heads, rows, 4 * HEAD_DIM)],
        3,
        scalars=(shard,),
        alias=alias,
        free_out=(1,),
    )


def mlp_kernel(n_ref, g_ref, w_in, b_in, w_out, *rest):
    hidden_ref, dgate_ref, part_ref, dn_ref, db_in, db_out = rest[-6:]
    c0, c1 = 0.7978845608028654, 0.044715
    g = g_ref[...]
    gate = dot(n_ref[...], w_in[...]) + b_in[...]
    square = gate * gate
    tanh = jnp.tanh(c0 * gate * (1.0 + c1 * square))
    left = 0.5 * (1.0 + tanh)
    hidden = (gate * left).astype(bf16)
    slope = left + 0.5 * gate * (1.0 - tanh * tanh) * (c0 * (1.0 + 3.0 * c1 * square))
    dgate = (dot_nt(g, w_out[...]) * slope).astype(bf16)
    hidden_ref[...] = hidden
    dgate_ref[...] = dgate
    part_ref[...] = dot(hidden, w_out[...]).astype(bf16)
    dn_ref[...] = dot_nt(dgate, w_in[...]).astype(bf16)

    @pl.when(pl.program_id(0) == 0)
    def _():
        db_in[...] = jnp.zeros_like(db_in)
        db_out[...] = jnp.zeros_like(db_out)

    db_in[...] += jnp.sum(dgate.astype(f32), 0, keepdims=True)
    db_out[...] += jnp.sum(g.astype(f32), 0, keepdims=True)


def mlp(c, count, rows, normed, g, w_in, b_in, w_out, before, after):
    total, width = g.shape
    ff = w_in.shape[1]
    there = lambda w: pl.BlockSpec((rows, w), lambda i: (c * count + i, 0))
    here = lambda w: pl.BlockSpec((rows, w), lambda i: (i, 0))
    one = lambda w: pl.BlockSpec((1, w), lambda i: (0, 0))
    ins = (normed, g, w_in, b_in, w_out)
    specs = [there(width), there(width), whole(w_in), whole(b_in), whole(w_out)]
    alias = {}
    if before is not None:
        alias = {len(ins): 0, len(ins) + 1: 1}
        ins, specs = ins + tuple(before), specs + [anywhere] * 2
    return call(
        mlp_kernel,
        (count,),
        ins,
        specs,
        [there(ff), there(ff), here(width), here(width), one(ff), one(width)],
        [
            shape_of(total, ff),
            shape_of(total, ff),
            shape_of(count * rows, width),
            shape_of(count * rows, width),
            shape_of(1, ff, dtype=f32),
            shape_of(1, width, dtype=f32),
        ],
        5,
        after,
        alias=alias,
        vmem=32,
    )


def dense_grads_kernel(core_ref, n_ref, dgate_ref, hidden_ref, g_ref, give_ref, keep_ref):
    step, half = pl.program_id(0), pl.num_programs(0) // 2
    both = dot_tn(n_ref[...], dgate_ref[...]).astype(bf16), dot_tn(hidden_ref[...], g_ref[...]).astype(bf16)

    @pl.when(step < half)
    def _():
        give_ref[0], give_ref[1] = both

    @pl.when(step >= half)
    def _():
        keep_ref[0], keep_ref[1] = both


def halves(steps, rows, wide, slots):
    half = steps // 2

    def place(i, core):
        return jnp.where(i < half, (1 - core[0]) * half + i, core[0] * half + i - half)

    cols = lambda total: pl.BlockSpec((total, rows), lambda i, core: (0, place(i, core)))
    give = pl.BlockSpec((slots, rows, wide), lambda i, core: (0, jnp.minimum(i, half - 1), 0))
    keep = pl.BlockSpec((slots, rows, wide), lambda i, core: (0, jnp.maximum(i - half, 0), 0))
    return cols, [give, keep]


def dense_grads(core, normed, dgate, hidden, g, loose, steps=4):
    total, width = g.shape
    cols, outs = halves(steps, width // steps, width, 2)
    return call(
        dense_grads_kernel,
        (steps,),
        (normed, dgate, hidden, g),
        [cols(total), whole(dgate), cols(total), whole(g)],
        outs,
        [shape_of(2, width // 2, width)] * 2,
        6,
        scalars=(core,),
        after=loose,
    )


def post_kernel(place_ref, back_ref, x_ref, part_ref, dn_ref, b_out, wq, wk, wv, wo, cosine, sine, *rest):
    give_ref, keep_ref, flat_ref, dgain, dbias = rest[-5:]
    tables = signed(cosine[...], sine[...])
    lane = lax.broadcasted_iota(jnp.int32, tables[0].shape, 1)
    inner = wo.shape[0]
    for tile in range(inner // 128):
        even, odd = back_ref[2 * tile].astype(f32), back_ref[2 * tile + 1].astype(f32)
        lows = half_swap(even[:, 0:128], odd[:, 0:128], lane, True)
        dq = half_swap(even[:, 0:128], odd[:, 0:128], lane, False)
        dk = half_swap(even[:, 128:256], odd[:, 128:256], lane, True)
        dv = half_swap(even[:, 128:256], odd[:, 128:256], lane, False)
        dq = rope_tile(dq, tables[0], -tables[1], -tables[2])
        dk = rope_tile(dk, tables[0], -tables[1], -tables[2])
        for which, value in enumerate((lows, dq, dk, dv)):
            at = which * inner + tile * 128
            flat_ref[:, at : at + 128] = value.astype(bf16)
    x = x_ref[0].astype(f32)
    z = place_ref[1]
    first = (z == 0).astype(f32)
    mixed = dot(flat_ref[:, 0:inner], wo[...]) + part_ref[...].astype(f32) + first * (x + b_out[...])
    dn = dn_ref[...].astype(f32)
    for which, w in enumerate((wq, wk, wv)):
        at = (which + 1) * inner
        dn = dn + dot_nt(flat_ref[:, at : at + inner], w[...])
    unit, _ = unit_rows(x)
    odd = z % 2 == 1
    half = dn.shape[0] // 2
    for which, share in enumerate((dn, mixed)):
        top, bottom = share[:half].astype(bf16), share[half:].astype(bf16)
        give_ref[0, which] = jnp.where(odd, top, bottom)
        keep_ref[0, which] = jnp.where(odd, bottom, top)

    @pl.when(pl.program_id(0) == 0)
    def _():
        dgain[...] = jnp.zeros_like(dgain)
        dbias[...] = jnp.zeros_like(dbias)

    dgain[...] += jnp.sum(dn * unit, 0, keepdims=True)
    dbias[...] += jnp.sum(dn, 0, keepdims=True)


def post(c, count, place, back, x, part, dn, consts, tables, before, after):
    seqs, rows, width = x.shape
    inner = consts[1].shape[1]
    heads = inner // HEAD_DIM
    here = pl.BlockSpec((rows, width), lambda i, _: (i, 0))
    one = pl.BlockSpec((1, width), lambda i, _: (0, 0))
    ins = (back, x, part, dn) + consts + tables
    specs = [
        pl.BlockSpec((heads, rows, 4 * HEAD_DIM), lambda i, _: (i, 0, 0)),
        pl.BlockSpec((1, rows, width), lambda i, _: (c * count + i, 0, 0)),
        here,
        here,
    ]
    specs += [whole(w) for w in consts] + [mine(rows)] * 2
    alias = {}
    if before is not None:
        alias = {len(ins): 2}
        ins, specs = ins + (before,), specs + [anywhere]
    share_spec = pl.BlockSpec((1, 2, rows // 2, width), lambda i, place: (i ^ (place[1] // 2), 0, 0, 0))
    return call(
        post_kernel,
        (count,),
        ins,
        specs,
        [share_spec] * 2 + [pl.BlockSpec((rows, 4 * inner), lambda i, _: (c * count + i, 0)), one, one],
        [shape_of(count, 2, rows // 2, width)] * 2
        + [shape_of(seqs * rows, 4 * inner)]
        + [shape_of(1, width, dtype=f32)] * 2,
        4,
        after,
        (place,),
        alias=alias,
    )


def head_grads_kernel(core_ref, n_ref, g_ref, flat_ref, small_ref, give_ref, keep_ref, *, inner):
    step, half = pl.program_id(0), pl.num_programs(0) // 2
    out = dot_tn(g_ref[...], flat_ref[:, 0:inner])
    rest = dot_tn(n_ref[...], flat_ref[:, inner:])

    @pl.when(step < half)
    def _():
        give_ref[0, :, 0:inner] = out.astype(bf16)
        give_ref[0, :, inner:] = rest.astype(bf16)

    @pl.when(step >= half)
    def _():
        give_ref[0, 0 : small_ref.shape[0]] = small_ref[...]
        keep_ref[0, :, 0:inner] = out.astype(bf16)
        keep_ref[0, :, inner:] = rest.astype(bf16)


def head_grads(core, normed, g, flat, small, after, steps=4):
    total, width = g.shape
    wide = flat.shape[1]
    rows, half = width // steps, steps // 2
    cols, (_, keep) = halves(steps, rows, wide, 1)
    give = pl.BlockSpec((1, rows, wide), lambda i, core: (0, jnp.minimum(i, half), 0))
    return call(
        partial(head_grads_kernel, inner=wide // 4),
        (steps,),
        (normed, g, flat, small),
        [cols(total), cols(total), whole(flat), whole(small)],
        [give, keep],
        [shape_of(1, (half + 1) * rows, wide), shape_of(1, half * rows, wide)],
        4,
        after,
        (core,),
    )


def split_kernel(keep_ref, got_ref, *rest, small):
    out_ref, token_ref = rest[-2:]
    token_ref[...] = jnp.zeros_like(token_ref)
    rows = keep_ref.shape[1]
    out_ref[0, :, 0:rows] = (keep_ref[...].astype(f32) + got_ref[...].astype(f32)).astype(bf16)
    if small:
        own, got = rest[0], rest[1]
        out_ref[0, 0, rows:] = (own[...].astype(f32) + got[0].astype(f32)).astype(bf16)


def split(keep, got, small, chips, after):
    slots, total, wide = keep.shape
    rows = total // chips
    block = pl.BlockSpec((slots, rows, wide), lambda k: (0, k, 0))
    ins, specs, extra = (keep, got), [block, block], 0
    if small is not None:
        extra = small.shape[0]
        ins += (small, got)
        specs += [whole(small), pl.BlockSpec((1, extra, wide), lambda k: (0, total // extra, 0))]
    return call(
        partial(split_kernel, small=extra > 0),
        (chips,),
        ins,
        specs,
        [pl.BlockSpec((1, slots, rows + extra, wide), lambda k: (k, 0, 0, 0)), pl.BlockSpec((8, 128), lambda k: (0, 0))],
        [shape_of(chips, slots, rows + extra, wide), shape_of(8, 128, dtype=f32)],
        2,
        after,
        vmem=16,
    )


def parted_kernel(chip_ref, keep_ref, got_ref, *outs):
    outs[-1][...] = jnp.zeros_like(outs[-1])
    total = (keep_ref[...].astype(f32) + got_ref[...].astype(f32)).astype(bf16)
    for k, out in enumerate(outs[:-1]):

        @pl.when(pl.program_id(0) == k)
        def _():
            out[...] = total


def parted(chip, keep, got, chips, after):
    slots, rows, wide = keep.shape
    rows = rows // chips
    block = pl.BlockSpec((slots, rows, wide), lambda k, chip: (0, chip[0] ^ k, 0))
    one = pl.BlockSpec((slots, rows, wide), lambda k, chip: (0, 0, 0))
    return call(
        parted_kernel,
        (chips,),
        (keep, got),
        [block, block],
        [one] * chips + [pl.BlockSpec((8, 128), lambda k, chip: (0, 0))],
        [shape_of(slots, rows, wide)] * chips + [shape_of(8, 128, dtype=f32)],
        2,
        after,
        (chip,),
        vmem=16,
    )


def joined_kernel(*refs):
    parts, (out_ref, token_ref) = refs[:-2], refs[-2:]
    token_ref[...] = jnp.zeros_like(token_ref)
    total = parts[0][...].astype(f32)
    for part in parts[1:]:
        total = total + part[...].astype(f32)
    for k in range(out_ref.shape[0]):
        out_ref[k] = total.astype(bf16)


def joined(parts, after):
    slots, rows, wide = parts[0].shape
    block = pl.BlockSpec((1, rows, wide // 2), lambda i: (i // 2, 0, i % 2))
    return call(
        joined_kernel,
        (2 * slots,),
        tuple(parts),
        [block] * len(parts),
        [
            pl.BlockSpec((len(parts), 1, rows, wide // 2), lambda i: (0, i // 2, 0, i % 2)),
            pl.BlockSpec((8, 128), lambda i: (0, 0)),
        ],
        [shape_of(len(parts), slots, rows, wide), shape_of(8, 128, dtype=f32)],
        2,
        after,
        vmem=16,
    )


def total_kernel(parts_ref, out_ref, token_ref):
    token_ref[...] = jnp.zeros_like(token_ref)
    total = parts_ref[0].astype(f32)
    for k in range(1, parts_ref.shape[0]):
        total = total + parts_ref[k].astype(f32)
    for k in range(out_ref.shape[0]):
        out_ref[k] = total.astype(bf16)


def total(parts, copies, loose):
    chips, slots, rows, wide = parts.shape
    steps = 2 * slots
    block = lambda n: pl.BlockSpec((n, 1, rows, wide // 2), lambda i: (0, i // 2, 0, i % 2))
    return call(
        total_kernel,
        (steps,),
        (parts,),
        [block(chips)],
        [block(copies), pl.BlockSpec((8, 128), lambda i: (0, 0))],
        [shape_of(copies, slots, rows, wide), shape_of(8, 128, dtype=f32)],
        2,
        vmem=16,
        after=loose,
    )


def widened(at_ref, own_ref, other_ref, stage, in_sems, take):
    chips = own_ref.shape[0]
    loads = [
        pltpu.make_async_copy((own_ref, other_ref)[i // chips].at[i % chips], stage.at[i], in_sems.at[i])
        for i in range(2 * chips)
    ]
    for load in loads:
        load.start()
    stores = []
    for i, load in enumerate(loads):
        load.wait()
        spot = (at_ref[0] ^ (i // chips)) * chips + (at_ref[1] ^ (i % chips))
        for store in take(i, spot):
            store.start()
            stores.append(store)
    for store in stores:
        store.wait()


def dense_outs_kernel(at_ref, own_ref, other_ref, out_in, out_out, stage, wide_stage, in_sems, out_sems):
    rows = stage.shape[2]

    def take(i, spot):
        for which, out in enumerate((out_in, out_out)):
            wide_stage[i, which] = stage[i, which].astype(f32)
            here = out.at[pl.ds(spot * rows, rows)]
            yield pltpu.make_async_copy(wide_stage.at[i, which], here, out_sems.at[i, which])

    widened(at_ref, own_ref, other_ref, stage, in_sems, take)


def head_outs_kernel(at_ref, own_ref, other_ref, out_t, out_q, out_k, out_v, stage, turned, wide_stage, in_sems, out_sems):
    rows, inner = wide_stage.shape[2:]

    def take(i, spot):
        here = pl.ds(spot * rows, rows)
        turned[i] = stage[i, 0, 0:rows, 0:inner].astype(f32).T
        yield pltpu.make_async_copy(turned.at[i], out_t.at[:, here], out_sems.at[i, 0])
        for which, out in enumerate((out_q, out_k, out_v)):
            cols = slice((which + 1) * inner, (which + 2) * inner)
            wide_stage[i, which] = stage[i, 0, 0:rows, cols].astype(f32)
            yield pltpu.make_async_copy(wide_stage.at[i, which], out.at[here], out_sems.at[i, which + 1])

    widened(at_ref, own_ref, other_ref, stage, in_sems, take)


def dense_outs(at, own, other, width, after):
    chips, slots, rows, wide = own.shape
    dma = pltpu.SemaphoreType.DMA
    return call(
        dense_outs_kernel,
        (1,),
        (own, other),
        [anywhere] * 2,
        [anywhere] * 2,
        [shape_of(width, wide, dtype=f32)] * 2,
        4,
        after,
        (at,),
        [
            pltpu.VMEM((2 * chips, slots, rows, wide), bf16),
            pltpu.VMEM((2 * chips, slots, rows, wide), f32),
            dma((2 * chips,)),
            dma((2 * chips, slots)),
        ],
        vmem=20,
    )


def head_outs(at, own, other, width, after):
    chips, slots, tall, wide = own.shape
    rows, inner = width // (2 * chips), wide // 4
    dma = pltpu.SemaphoreType.DMA
    return call(
        head_outs_kernel,
        (1,),
        (own, other),
        [anywhere] * 2,
        [anywhere] * 4,
        [shape_of(inner, width, dtype=f32)] + [shape_of(width, inner, dtype=f32)] * 3,
        3,
        after,
        (at,),
        [
            pltpu.VMEM((2 * chips, slots, tall, wide), bf16),
            pltpu.VMEM((2 * chips, inner, rows), f32),
            pltpu.VMEM((2 * chips, 3, rows, inner), f32),
            dma((2 * chips,)),
            dma((2 * chips, 4)),
        ],
        vmem=16,
    )


def input_grad(x, g, dn, gain):
    unit, inv_std = unit_rows(x.astype(f32))
    du = dn.astype(f32) * gain
    d = inv_std * (du - jnp.mean(du, -1, keepdims=True) - unit * jnp.mean(du * unit, -1, keepdims=True))
    return (g.astype(f32) + d).astype(bf16)


def pair_sum_kernel(keep_ref, got_ref, own_ref, other_ref):
    for at, ref in enumerate((own_ref, other_ref)):

        @pl.when(pl.program_id(0) == at)
        def _():
            ref[...] = (keep_ref[0].astype(f32) + got_ref[0].astype(f32)).astype(bf16)


def pair_sum(keep, got, after):
    _, _, rows, width = keep.shape
    block = pl.BlockSpec((1, 2, rows, width), lambda i: (i, 0, 0, 0))
    out = pl.BlockSpec((2, rows, width), lambda i: (0, 0, 0))
    return call(
        pair_sum_kernel, (2,), (keep, got), [block, block], [out, out], [shape_of(2, rows, width)] * 2, 1, after, vmem=12
    )


def own_quarter_kernel(place_ref, x_ref, g_ref, own_ref, got_ref, gain, *outs):
    total = own_ref[...].astype(f32) + got_ref[...].astype(f32)
    tokens = input_grad(x_ref[0], g_ref[0], total[0], gain[...])
    mixed = total[1].astype(bf16)
    for ref in outs:
        ref[0] = tokens
        ref[1] = mixed


def own_quarter(place, start, x, g, own, got, gain, copies, loose):
    _, rows, width = own.shape
    per = x.shape[1] // rows
    block = pl.BlockSpec((1, rows, width), lambda i, place: (start + place[1] // per, place[1] % per, 0))
    return call(
        own_quarter_kernel,
        (1,),
        (x, g, own, got, gain),
        [block, block, whole(own), whole(got), whole(gain)],
        [pl.BlockSpec(own.shape, lambda i, _: (0, 0, 0))] * copies,
        [shape_of(*own.shape)] * copies,
        2,
        scalars=(place,),
        vmem=12,
        after=loose,
    )


def placed_kernel(place_ref, *refs, pieces, start):
    tokens_ref, mixed_ref, stage, in_sems, out_sems = refs[-5:]
    rows = stage.shape[2]
    per = tokens_ref.shape[1] // rows
    loads = [pltpu.make_async_copy(ref, stage.at[at], in_sems.at[at]) for at, ref in enumerate(refs[:pieces])]
    for load in loads:
        load.start()
    stores = []
    for at, load in enumerate(loads):
        load.wait()
        quarter = place_ref[1] ^ at
        spot = start + quarter // per, pl.ds((quarter % per) * rows, rows)
        for which, out in enumerate((tokens_ref, mixed_ref)):
            stores.append(pltpu.make_async_copy(stage.at[at, which], out.at[spot], out_sems.at[at, which]))
            stores[-1].start()
    for store in stores:
        store.wait()


def placed(place, shape, start, pieces, before, after):
    ins, alias, count = tuple(pieces), {}, len(pieces)
    if before is not None:
        alias = {count: 0, count + 1: 1}
        ins += tuple(before)
    dma = pltpu.SemaphoreType.DMA
    return call(
        partial(placed_kernel, pieces=count, start=start),
        (1,),
        ins,
        [anywhere] * len(ins),
        [anywhere, anywhere],
        [shape_of(*shape)] * 2,
        2,
        after,
        (place,),
        [pltpu.VMEM((count,) + pieces[0].shape, bf16), dma((count,)), dma((count, 2))],
        alias,
        vmem=6,
    )


def exchanged(x, bits):
    return lax.ppermute(x, "seq", [(i, i ^ bits) for i in range(lax.axis_size("seq"))])


def by_pairs(
    tokens, ln_gain, ln_bias, w_query, w_key, w_value, w_attn_out, w_in, b_in, w_mlp_out, b_out, cotangent
):
    x, cot = tokens[0], cotangent[0]
    seqs, rows, width = x.shape
    inner = w_query.shape[1]
    ff = w_in.shape[1]
    heads = inner // HEAD_DIM
    shards = lax.axis_size("seq")
    count = shards // heads
    in_hbm.clear()
    in_hbm.add(x, cot, w_query, w_key, w_value, w_attn_out, w_in, w_mlp_out)
    row = lambda v: v.reshape(1, -1)
    gain, bias, b_in, b_out = row(ln_gain), row(ln_bias), row(b_in), row(b_out)
    in_hbm.add(gain, bias, b_in, b_out)
    flat_cot = cot.reshape(-1, width)
    in_hbm.add(flat_cot)
    shard = lax.axis_index("seq").astype(jnp.int32)
    core, chip, chips = (shard % 2).reshape(1), (shard // 2).reshape(1), shards // 2
    z = lax.axis_index("mlp").astype(jnp.int32)
    place = jnp.stack([shard, z])
    tables = tuple(map(jnp.asarray, position_tables(shards * rows)))
    in_hbm.add(*tables)
    weights = (w_query, w_key, w_value, w_attn_out)
    pre_consts = (gain, bias) + weights
    post_consts = (b_out,) + weights

    def attend(sent, after):
        done = attention(sent.reshape(1, shards * rows, 4 * HEAD_DIM), after)
        return done.reshape(shards, rows, 4 * HEAD_DIM)

    def traded(v):
        return lax.all_to_all(v, "seq", 0, 0, tiled=True)

    def over_line(v, bits):
        return lax.ppermute(v, "mlp", [(i, i ^ bits) for i in range(4)])

    dense_args = (flat_cot, w_in, b_in, w_mlp_out)
    normed, packed_a = pre(0, count, place, x, cot, pre_consts, tables, None)
    sent_a = traded(packed_a)
    normed, packed_b = pre(1, count, place, x, cot, pre_consts, tables, normed)
    hidden, dgate, part_a, dn_a, db_in_a, db_out_a = mlp(0, count, rows, normed, *dense_args, None, (packed_b,))
    done_a = attend(sent_a, (db_in_a,))
    back_a = traded(done_a)
    hidden, dgate, part_b, dn_b, db_in_b, db_out_b = mlp(1, count, rows, normed, *dense_args, (hidden, dgate), (done_a,))
    sent_b = traded(fence(packed_b, back_a, db_in_b))
    give_a, keep_a, flat, gain_a, bias_a = post(
        0, count, place, back_a, x, part_a, dn_a, post_consts, tables, None, (db_in_b,)
    )
    got_a = over_line(give_a, 1)
    give_e, keep_e = dense_grads(core, normed, dgate, hidden, flat_cot, (gain_a,))
    got_e = exchanged(give_e, 1)
    done_b = attend(sent_b, (keep_e,))
    back_b = traded(done_b)
    own_a, other_a = pair_sum(keep_a, got_a, (done_b,))
    *dense, token = parted(chip, keep_e, got_e, chips, (own_a,))
    dense = [dense[0]] + [exchanged(dense[k], 2 * k) for k in range(1, chips)]
    got_a = over_line(other_a, 2)
    give_b, keep_b, flat, gain_b, bias_b = post(
        1, count, place, back_b, x, part_b, dn_b, post_consts, tables, flat, (token,)
    )

    def over_chips(v):
        same_core = [list(range(side, shards, 2)) for side in (0, 1)]
        return lax.all_to_all(v, "seq", 0, 0, axis_index_groups=same_core, tiled=True)

    dense[1] = fence(dense[1], gain_b)
    dense[2] = fence(dense[2], dense[1])
    done_a, more_a, again_a = own_quarter(place, 0, x, cot, own_a, got_a, gain, 3, (dense[2],))
    dense, token = joined(dense, (more_a,))
    dense = over_chips(dense)
    small = jnp.concatenate([gain_a + gain_b, bias_a + bias_b, db_in_a + db_in_b, db_out_a + db_out_b], 0)
    small = jnp.concatenate([small, jnp.zeros((12, width), f32)], 0).astype(bf16)
    give_l, keep_l = head_grads(core, normed, flat_cot, flat, small, (token,))
    far_a = over_line(done_a, 2)
    got_b = over_line(give_b, 1)
    own_b, other_b = pair_sum(keep_b, got_b, (keep_l,))
    near_a = over_line(fence(again_a, own_b), 1)
    got_b = over_line(other_b, 2)
    got_l = exchanged(give_l, 1)
    head, token = split(keep_l, got_l, small, chips, (own_b,))
    dense = fence(dense, token)
    head = over_chips(fence(head, dense))
    dense_other = exchanged(dense, 1)
    far_a = fence(far_a, dense)
    beside_a = over_line(far_a, 1)
    done_b, more_b = own_quarter(place, count, x, cot, own_b, got_b, gain, 2, (far_a,))
    dense_other = fence(dense_other, done_b)
    d_in, d_out = dense_outs(jnp.concatenate([core, jnp.zeros_like(core)]), dense, dense_other, width, (done_b,))
    head, token = total(head, chips, (d_out,))
    near_b = over_line(done_b, 1)
    far_b = over_line(more_b, 2)
    small = head[0, 0, -small.shape[0] :].astype(f32)
    vectors = small[:2]
    vectors_got = over_line(vectors, 1)
    head = over_chips(head)
    near_a = fence(near_a, token)
    beside_a = fence(beside_a, near_a)
    d_tokens, mixed = placed(place, x.shape, 0, (more_a, near_a, far_a, beside_a), None, (beside_a,))
    far_b = fence(far_b, d_tokens)
    beside_b = over_line(far_b, 1)
    vectors = vectors + fence(vectors_got, far_b)
    vectors_got = over_line(vectors, 2)
    head = fence(head, far_b)
    head_other = exchanged(head, 1)
    head_other = fence(head_other, far_b)
    d_attn_out, d_query, d_key, d_value = head_outs(
        jnp.concatenate([core, jnp.zeros_like(core)]), head, head_other, width, (far_b,)
    )
    vectors = vectors + fence(vectors_got, d_value)
    near_b = fence(near_b, vectors)
    beside_b = fence(beside_b, near_b)
    d_tokens, mixed = placed(place, x.shape, count, (more_b, near_b, far_b, beside_b), (d_tokens, mixed), (beside_b,))
    return (
        mixed.reshape(tokens.shape),
        d_tokens[None],
        vectors[0],
        vectors[1],
        d_query,
        d_key,
        d_value,
        d_attn_out,
        d_in,
        small[2],
        d_out,
        small[3],
    )


def per_device(
    tokens, ln_gain, ln_bias, w_query, w_key, w_value, w_attn_out, w_in, b_in, w_mlp_out, b_out, cotangent
):
    _, seqs, rows, width = tokens.shape
    inner = w_query.shape[1]
    heads = inner // HEAD_DIM
    shards = lax.axis_size("seq")
    fits = shards == 8 and lax.axis_size("mlp") == 4 and seqs * heads == 2 * shards and shards % heads == 0
    fits = fits and inner % 128 == 0 and rows % 256 == 0 and width % 1024 == 0 and w_in.shape[1] == width
    fits = fits and 4 * inner == width
    plan = by_pairs if fits else by_ring
    return plan(
        tokens, ln_gain, ln_bias, w_query, w_key, w_value, w_attn_out, w_in, b_in, w_mlp_out, b_out, cotangent
    )


def solution(mesh):
    rows, whole = P("seq", None, None, None), P()
    cols, down = P(None, "mlp"), P("mlp", None)
    return jax.shard_map(
        per_device,
        mesh=mesh,
        in_specs=(rows, whole, whole, cols, cols, cols, down, cols, P("mlp"), down, whole, rows),
        out_specs=(rows, rows, whole, whole, cols, cols, cols, down, cols, P("mlp"), down, whole),
        check_vma=False,
    )
```

```python
from functools import partial

import jax
import jax.numpy as jnp
import numpy as np
from jax import lax
from jax.experimental import pallas as pl
from jax.experimental.pallas import tpu as pltpu
from jax.sharding import PartitionSpec as P

HEAD_DIM = 64
ROT = 32

epsilon = 1e-05
neg_big = -1e30
bf16 = jnp.bfloat16
f32 = jnp.float32


def passed_along(x, axis, by):
    peers = lax.axis_size(axis)
    pairs = [(i, i + by) for i in range(peers) if 0 <= i + by < peers]
    return lax.ppermute(x, axis, pairs)


def rotary_tables(positions, width):
    column = jnp.arange(width, dtype=jnp.int32) % HEAD_DIM
    pairs = (column // 2).astype(f32)
    freq = 10000.0 ** (-2.0 * pairs / ROT)
    angle = positions.astype(f32)[:, None] * freq[None, :]
    active = (column < ROT)[None, :]
    even = (column % 2 == 0)[None, :]
    cosine = jnp.where(active, jnp.cos(angle), 1.0)
    sine = jnp.where(active, jnp.sin(angle), 0.0)
    return cosine, jnp.where(even, -sine, 0.0), jnp.where(even, 0.0, sine)


def rotate(v, tables, sign):
    cosine, from_right, from_left = tables
    right = jnp.concatenate([v[..., 1:], v[..., :1]], -1)
    left = jnp.concatenate([v[..., -1:], v[..., :-1]], -1)
    return v * cosine + sign * (right * from_right + left * from_left)


def attention_kernel(x_ref, out_ref, xt, acc, sbuf, *, length, hd, tq, tk):
    xt[...] = x_ref[0].T
    scale = hd**-0.5
    nt = (((1,), (1,)), ((), ()))
    zero = jnp.zeros((hd, tq), bf16)

    def put(old, new, q0, join):
        if old is None:
            return new
        if q0 == 0:
            return join(old, new)
        return jnp.concatenate([old[:, :q0], join(old[:, q0:], new)], 1)

    add = lambda u, v: u + v
    for i in range(length // tq):
        first = i * tq
        qs = (xt[0:hd, first : first + tq].astype(f32) * scale).astype(bf16)
        at = xt[3 * hd : 4 * hd, first : first + tq].astype(f32)
        zq = jnp.concatenate([zero, qs], 0)
        qz = jnp.concatenate([qs, zero], 0)
        steps = [(k0, k0 + tk, 0) for k0 in range(0, first, tk)]
        steps += [(first + q0, first + q0 + tk // 2, q0) for q0 in range(0, tq, tk // 2)]
        top = None
        for k0, k1, q0 in steps:
            st = jnp.dot(x_ref[0, k0:k1, 0 : 2 * hd], zq[:, q0:], preferred_element_type=f32)
            if k0 >= first:
                kp = lax.broadcasted_iota(jnp.int32, st.shape, 0)
                qp = lax.broadcasted_iota(jnp.int32, st.shape, 1)
                st = jnp.where(kp <= qp, st, neg_big)
            sbuf[k0:k1, q0:] = st
            top = put(top, jnp.max(st, 0, keepdims=True), q0, jnp.maximum)
        tot = None
        ot = None
        for k0, k1, q0 in steps:
            e = jnp.exp(sbuf[k0:k1, q0:] - top[:, q0:])
            sbuf[k0:k1, q0:] = e
            tot = put(tot, jnp.sum(e, 0, keepdims=True), q0, add)
            ot = put(ot, jnp.dot(xt[2 * hd : 3 * hd, k0:k1], e.astype(bf16), preferred_element_type=f32), q0, add)
        r = 1.0 / tot
        ot = ot * r
        ar = (at * r).astype(bf16)
        spread = jnp.sum(ar.astype(f32) * ot, 0, keepdims=True)
        az = jnp.concatenate([ar, zero], 0)
        za = jnp.concatenate([zero, ar], 0)
        dqt = None
        for k0, k1, q0 in steps:
            dp = jnp.dot(x_ref[0, k0:k1, 2 * hd : 4 * hd], az[:, q0:], preferred_element_type=f32)
            e = sbuf[k0:k1, q0:]
            ds = (e * (dp - spread[:, q0:])).astype(bf16)
            dqt = put(dqt, jnp.dot(xt[hd : 2 * hd, k0:k1], ds, preferred_element_type=f32), q0, add)
            both = lax.dot_general(ds, qz[:, q0:], nt, preferred_element_type=f32) + lax.dot_general(
                e.astype(bf16), za[:, q0:], nt, preferred_element_type=f32
            )
            if k0 < first:
                both = acc[k0:k1, :] + both
            acc[k0:k1, :] = both
        both = jnp.concatenate([ot, dqt * scale], 0)
        out_ref[0, first : first + tq, 0 : 2 * hd] = both.T.astype(bf16)
    out_ref[0, :, 2 * hd : 4 * hd] = acc[...].astype(bf16)


def attention(x, after=()):
    n, length, width = x.shape
    hd = width // 4
    tq = 512 if length % 512 == 0 else 256
    spec = pl.BlockSpec((1, length, width), lambda i: (i, 0, 0))
    return call(
        partial(attention_kernel, length=length, hd=hd, tq=tq, tk=512),
        (n,),
        (x,),
        [spec],
        spec,
        shape_of(*x.shape),
        7,
        after,
        scratch=[pltpu.VMEM((width, length), bf16), pltpu.VMEM((length, 2 * hd), f32), pltpu.VMEM((length, tq), f32)],
        vmem=32,
        free_out=(0,),
    )


def gathered_kernel(shard_ref, *refs, parts, **sizes):
    x_ref = refs[parts + 1]
    rows = refs[0].shape[1]
    for k in range(parts):
        x_ref[0, pl.ds((shard_ref[0] ^ k) * rows, rows)] = refs[k][0]
    attention_kernel(x_ref, refs[parts], *refs[parts + 2 :], **sizes)


def attention_of(shard, same, other, after=()):
    _, rows, width = same[0].shape
    length, hd = 2 * rows * len(same), width // 4
    tq = 512 if length % 512 == 0 else 256
    specs = [pl.BlockSpec((1, rows, width), lambda i, _, side=side: (side, 0, 0)) for side in (0, 1)]
    return call(
        partial(gathered_kernel, parts=2 * len(same), length=length, hd=hd, tq=tq, tk=512),
        (1,),
        tuple(v for pair in zip(same, other) for v in pair),
        specs * len(same),
        pl.BlockSpec((1, length, width), lambda i, _: (0, 0, 0)),
        shape_of(1, length, width),
        7,
        after,
        (shard,),
        [
            pltpu.VMEM((1, length, width), bf16),
            pltpu.VMEM((width, length), bf16),
            pltpu.VMEM((length, 2 * hd), f32),
            pltpu.VMEM((length, tq), f32),
        ],
        vmem=32,
        free_out=(0,),
    )


def ring_attention(q, k, v, a):
    seq_count, row_count, inner_width = q.shape
    score_scale = HEAD_DIM ** (-0.5)
    shard_total = lax.axis_size("seq")
    my_shard = lax.axis_index("seq")
    heads_of = lambda x: x.reshape(seq_count, row_count, inner_width // HEAD_DIM, HEAD_DIM)
    flat_of = lambda x: x.reshape(seq_count, row_count, inner_width)
    qh, gh = heads_of(q), heads_of(a)
    local = jnp.arange(row_count, dtype=jnp.int32)
    own_mask = local[:, None] >= local[None, :]
    ein = partial(jnp.einsum, preferred_element_type=f32)

    def attend_block(state, key_block, value_block, visible):
        running_max, exp_total, weighted = state
        raw = ein("sthd,suhd->shtu", qh, key_block) * score_scale
        raw = jnp.where(visible[None, None], raw, neg_big)
        new_max = jnp.maximum(running_max, jnp.max(raw, -1))
        weights = jnp.where(visible[None, None], jnp.exp(raw - new_max[..., None]), 0.0)
        shrink = jnp.exp(running_max - new_max)
        exp_total = exp_total * shrink + jnp.sum(weights, -1)
        weighted = weighted * jnp.transpose(shrink, (0, 2, 1))[..., None] + ein(
            "shtu,suhd->sthd", weights.astype(bf16), value_block
        )
        return (new_max, exp_total, weighted)

    head_count = inner_width // HEAD_DIM
    state = (
        jnp.full((seq_count, head_count, row_count), neg_big, f32),
        jnp.zeros((seq_count, head_count, row_count), f32),
        jnp.zeros(qh.shape, f32),
    )
    state = attend_block(state, heads_of(k), heads_of(v), own_mask)
    empty_stack = jnp.zeros((max(shard_total - 1, 1),) + q.shape, bf16)

    def forward_step(step, carry):
        state, near_keys, near_values, key_stack, value_stack = carry
        near_keys, near_values = passed_along((near_keys, near_values), "seq", 1)
        visible = jnp.broadcast_to(my_shard >= step, (row_count, row_count))
        state = attend_block(state, heads_of(near_keys), heads_of(near_values), visible)
        key_stack = lax.dynamic_update_index_in_dim(key_stack, near_keys, step - 1, 0)
        value_stack = lax.dynamic_update_index_in_dim(value_stack, near_values, step - 1, 0)
        return (state, near_keys, near_values, key_stack, value_stack)

    state, _, _, key_stack, value_stack = lax.fori_loop(
        1, shard_total, forward_step, (state, k, v, empty_stack, empty_stack)
    )
    running_max, exp_total, weighted = state
    log_total = running_max + jnp.log(exp_total)
    attended = weighted / jnp.transpose(exp_total, (0, 2, 1))[..., None]
    spread = jnp.transpose(jnp.sum(gh.astype(f32) * attended, -1), (0, 2, 1))

    def grads(key_block, value_block, visible):
        raw = ein("sthd,suhd->shtu", qh, key_block) * score_scale
        probs = jnp.where(visible[None, None], jnp.exp(raw - log_total[..., None]), 0.0)
        grad_probs = ein("sthd,suhd->shtu", gh, value_block)
        slopes = (probs * (grad_probs - spread[..., None])).astype(bf16)
        query_grad = ein("shtu,suhd->sthd", slopes, key_block) * score_scale
        key_grad = ein("shtu,sthd->suhd", slopes, qh) * score_scale
        value_grad = ein("shtu,sthd->suhd", probs.astype(bf16), gh)
        return query_grad, key_grad, value_grad

    d_query, d_keys, d_values = grads(heads_of(k), heads_of(v), own_mask)

    def return_step(index, carry):
        query_grad_total, travelling = carry
        step = shard_total - 1 - index
        near_keys = lax.dynamic_index_in_dim(key_stack, step - 1, 0, keepdims=False)
        near_values = lax.dynamic_index_in_dim(value_stack, step - 1, 0, keepdims=False)
        visible = jnp.broadcast_to(my_shard >= step, (row_count, row_count))
        query_grad, key_grad, value_grad = grads(heads_of(near_keys), heads_of(near_values), visible)
        joined = jnp.concatenate([flat_of(key_grad), flat_of(value_grad)], -1)
        travelling = passed_along((travelling + joined).astype(bf16), "seq", -1).astype(f32)
        return (query_grad_total + query_grad, travelling)

    start = jnp.zeros((seq_count, row_count, 2 * inner_width), f32)
    d_query, travelling = lax.fori_loop(0, shard_total - 1, return_step, (d_query, start))
    d_keys = flat_of(d_keys) + travelling[..., :inner_width]
    d_values = flat_of(d_values) + travelling[..., inner_width:]
    return tuple(x.astype(bf16) for x in (flat_of(attended), flat_of(d_query), d_keys, d_values))


def by_ring(
    tokens, ln_gain, ln_bias, w_query, w_key, w_value, w_attn_out, w_in, b_in, w_mlp_out, b_out, cotangent
):
    x_low = tokens[0]
    cot = cotangent[0]
    seqs, rows, width = x_low.shape
    inner = w_query.shape[1]
    my_shard = lax.axis_index("seq")
    ein = partial(jnp.einsum, preferred_element_type=f32)
    positions = my_shard * rows + jnp.arange(rows, dtype=jnp.int32)
    tables = rotary_tables(positions, inner)
    x = x_low.astype(f32)
    centred = x - jnp.mean(x, -1, keepdims=True)
    inv_std = lax.rsqrt(jnp.mean(centred * centred, -1, keepdims=True) + epsilon)
    unit = centred * inv_std
    normed = (unit * ln_gain + ln_bias).astype(bf16)
    query = rotate(ein("std,de->ste", normed, w_query), tables, 1.0).astype(bf16)
    keys = rotate(ein("std,de->ste", normed, w_key), tables, 1.0).astype(bf16)
    values = ein("std,de->ste", normed, w_value).astype(bf16)
    d_attended = ein("std,ed->ste", cot, w_attn_out).astype(bf16)

    attended, d_query, d_keys, d_values = ring_attention(query, keys, values, d_attended)

    gate_in = ein("std,df->stf", normed, w_in) + b_in
    hidden, gelu_pull = jax.vjp(partial(jax.nn.gelu, approximate=True), gate_in)
    hidden = hidden.astype(bf16)
    d_hidden = ein("std,fd->stf", cot, w_mlp_out)
    d_gate = gelu_pull(d_hidden)[0].astype(bf16)
    d_b_in = jnp.sum(d_gate, (0, 1), dtype=f32)
    d_b_out = jnp.sum(cot, (0, 1), dtype=f32)
    d_w_mlp_out = ein("stf,std->fd", hidden, cot)
    d_w_in = ein("std,stf->df", normed, d_gate)
    mlp_part = ein("stf,fd->std", hidden, w_mlp_out)
    d_normed_mlp = ein("stf,df->std", d_gate, w_in)

    attn_part = ein("ste,ed->std", attended, w_attn_out)
    branches = lax.psum((attn_part + mlp_part).astype(bf16), "mlp").astype(f32)
    mixed = (x + branches + b_out).astype(bf16)
    d_w_attn_out = ein("ste,std->ed", attended, cot)
    d_query_pre = rotate(d_query.astype(f32), tables, -1.0).astype(bf16)
    d_key_pre = rotate(d_keys.astype(f32), tables, -1.0).astype(bf16)
    d_w_query = ein("std,ste->de", normed, d_query_pre)
    d_w_key = ein("std,ste->de", normed, d_key_pre)
    d_w_value = ein("std,ste->de", normed, d_values)
    d_normed_part = d_normed_mlp + ein("ste,de->std", d_query_pre, w_query)
    d_normed_part = d_normed_part + ein("ste,de->std", d_key_pre, w_key)
    d_normed_part = d_normed_part + ein("ste,de->std", d_values, w_value)
    d_normed = lax.psum(d_normed_part.astype(bf16), "mlp").astype(f32)
    d_gain = jnp.sum(d_normed * unit, (0, 1))
    d_bias = jnp.sum(d_normed, (0, 1))
    d_unit = d_normed * ln_gain
    d_inputs = inv_std * (
        d_unit - jnp.mean(d_unit, -1, keepdims=True) - unit * jnp.mean(d_unit * unit, -1, keepdims=True)
    )
    d_tokens = (cot.astype(f32) + d_inputs).astype(bf16)

    def total(v):
        return lax.psum(v.astype(bf16), "seq").astype(f32)

    return (
        mixed[None],
        d_tokens[None],
        total(d_gain),
        total(d_bias),
        total(d_w_query),
        total(d_w_key),
        total(d_w_value),
        total(d_w_attn_out),
        total(d_w_in),
        total(d_b_in),
        total(d_w_mlp_out),
        total(d_b_out),
    )


anywhere = pl.BlockSpec(memory_space=pl.ANY)


class Placed(list):
    def add(self, *arrays):
        self.extend(arrays)

    def pin(self, x):
        return pltpu.with_memory_space_constraint(x, pltpu.HBM) if any(x is y for y in self) else x


in_hbm = Placed()


def call(
    kernel, grid, ins, in_specs, out_specs, out_shape, us, after=(), scalars=(), scratch=(), alias=None, vmem=24, free_out=()
):
    used = len(scalars) + len(ins)

    def body(*refs):
        kernel(*refs[:used], *refs[used + len(after) :])

    one = not isinstance(out_shape, list)
    shapes = [out_shape] if one else out_shape
    shapes = [s if i in free_out else pltpu.HBM(s.shape, s.dtype) for i, s in enumerate(shapes)]
    results = pl.pallas_call(
        body,
        name=getattr(kernel, "func", kernel).__name__.strip("<>"),
        grid_spec=pltpu.PrefetchScalarGridSpec(
            num_scalar_prefetch=len(scalars),
            grid=grid,
            in_specs=list(in_specs) + [anywhere] * len(after),
            out_specs=out_specs,
            scratch_shapes=list(scratch),
        ),
        out_shape=shapes[0] if one else shapes,
        input_output_aliases={len(scalars) + k: v for k, v in (alias or {}).items()},
        compiler_params=pltpu.CompilerParams(vmem_limit_bytes=vmem * 2**20),
        cost_estimate=pl.CostEstimate(flops=int(us * 1e11), bytes_accessed=0, transcendentals=0),
    )(*scalars, *map(in_hbm.pin, ins), *map(in_hbm.pin, after))
    in_hbm.add(*[r for i, r in enumerate([results] if one else results) if i not in free_out])
    return results


def fence(x, *after):
    known = any(x is y for y in in_hbm)
    return call(
        lambda *refs: None,
        (1,),
        (x,),
        [anywhere],
        anywhere,
        shape_of(*x.shape, dtype=x.dtype),
        1,
        after,
        alias={0: 0},
        vmem=1,
        free_out=() if known else (0,),
    )


def dot(a, b):
    return jnp.dot(a, b, preferred_element_type=f32)


def dot_nt(a, b):
    return lax.dot_general(a, b, (((1,), (1,)), ((), ())), preferred_element_type=f32)


def dot_tn(a, b):
    return lax.dot_general(a, b, (((0,), (0,)), ((), ())), preferred_element_type=f32)


def whole(x):
    return pl.BlockSpec(x.shape, lambda *_: (0,) * x.ndim, pipeline_mode=pl.Buffered(1))


def mine(rows):
    return pl.BlockSpec((rows, 2 * HEAD_DIM), lambda i, at: (at[0], 0), pipeline_mode=pl.Buffered(1))


def shape_of(*shape, dtype=bf16):
    return jax.ShapeDtypeStruct(shape, dtype)


def unit_rows(x):
    average = jnp.mean(x, -1, keepdims=True)
    centred = x - average
    inv_std = lax.rsqrt(jnp.mean(centred * centred, -1, keepdims=True) + epsilon)
    return centred * inv_std, inv_std


def half_swap(low, high, lane, keep_low):
    if keep_low:
        return jnp.where(lane < HEAD_DIM, low, pltpu.roll(high, HEAD_DIM, 1))
    return jnp.where(lane < HEAD_DIM, pltpu.roll(low, HEAD_DIM, 1), high)


def rope_tile(v, cosine, from_right, from_left):
    width = v.shape[1]
    return v * cosine + pltpu.roll(v, width - 1, 1) * from_right + pltpu.roll(v, 1, 1) * from_left


def position_tables(total):
    column = np.arange(2 * HEAD_DIM) % HEAD_DIM
    freq = np.float32(10000.0) ** (np.float32(-2.0 / ROT) * (column // 2).astype(np.float32))
    angle = np.arange(total, dtype=np.float32)[:, None] * freq.astype(np.float32)[None, :]
    active = (column < ROT)[None, :]
    cosine = np.where(active, np.cos(angle.astype(np.float64)), 1.0).astype(np.float32)
    sine = np.where(active, np.sin(angle.astype(np.float64)), 0.0).astype(np.float32)
    return cosine, sine


def signed(cosine, sine):
    even = lax.broadcasted_iota(jnp.int32, sine.shape, 1) % 2 == 0
    return cosine, jnp.where(even, -sine, 0.0), jnp.where(even, 0.0, sine)


def pre_kernel(shard_ref, x_ref, g_ref, gain, bias, wq, wk, wv, wo, cosine, sine, *rest, partners):
    if partners:
        normed_ref, packed_ref = rest[-2 - partners], rest[-1]
        outs = rest[-1 - partners : -1]
    else:
        normed_ref, packed_ref = rest[-2:]
    unit, _ = unit_rows(x_ref[0].astype(f32))
    normed = (unit * gain[...] + bias[...]).astype(bf16)
    normed_ref[...] = normed
    q, k, v = dot(normed, wq[...]), dot(normed, wk[...]), dot(normed, wv[...])
    a = dot_nt(g_ref[0], wo[...])
    tables = signed(cosine[...], sine[...])
    lane = lax.broadcasted_iota(jnp.int32, tables[0].shape, 1)
    for tile in range(q.shape[1] // 128):
        cols = slice(tile * 128, (tile + 1) * 128)
        qt, kt = rope_tile(q[:, cols], *tables), rope_tile(k[:, cols], *tables)
        for side in (0, 1):
            head = tile * 2 + side
            packed_ref[head, :, 0:128] = half_swap(qt, kt, lane, side == 0).astype(bf16)
            packed_ref[head, :, 128:256] = half_swap(v[:, cols], a[:, cols], lane, side == 0).astype(bf16)
    for k in range(partners):
        for side in range(2):
            pair = shard_ref[0] ^ (2 * k + side)
            heads = packed_ref.shape[0]

            @pl.when(pair // heads == pl.program_id(0))
            def _():
                outs[k][side] = packed_ref[pair % heads]


def pre(c, count, shard, x, g, consts, tables, before, partners=0):
    seqs, rows, width = x.shape
    heads = consts[2].shape[1] // HEAD_DIM
    by_seq = pl.BlockSpec((1, rows, width), lambda i, _: (c * count + i, 0, 0))
    ins, specs = (x, g) + consts + tables, [by_seq, by_seq] + [whole(w) for w in consts] + [mine(rows)] * 2
    alias = {}
    if before is not None:
        alias = {len(ins): 0}
        ins, specs = ins + (before,), specs + [anywhere]
    blocks = pl.BlockSpec((heads, rows, 4 * HEAD_DIM), lambda i, _: (i, 0, 0))
    shapes = [shape_of(count * heads, rows, 4 * HEAD_DIM)]
    scratch = []
    if partners:
        shapes = [shape_of(2, rows, 4 * HEAD_DIM)] * partners
        scratch = [pltpu.VMEM((heads, rows, 4 * HEAD_DIM), bf16)]
        blocks = pl.BlockSpec((2, rows, 4 * HEAD_DIM), lambda i, _: (0, 0, 0))
    return call(
        partial(pre_kernel, partners=partners),
        (count,),
        ins,
        specs,
        [
            pl.BlockSpec((rows, width), lambda i, _: (c * count + i, 0)),
        ]
        + [blocks] * len(shapes),
        [shape_of(seqs * rows, width)] + shapes,
        3,
        scalars=(shard,),
        alias=alias,
        scratch=scratch,
        free_out=range(1, 1 + len(shapes)),
    )


def mlp_kernel(n_ref, g_ref, w_in, b_in, w_out, *rest):
    hidden_ref, dgate_ref, part_ref, dn_ref, db_in, db_out = rest[-6:]
    c0, c1 = 0.7978845608028654, 0.044715
    g = g_ref[...]
    gate = dot(n_ref[...], w_in[...]) + b_in[...]
    square = gate * gate
    tanh = jnp.tanh(c0 * gate * (1.0 + c1 * square))
    left = 0.5 * (1.0 + tanh)
    hidden = (gate * left).astype(bf16)
    slope = left + 0.5 * gate * (1.0 - tanh * tanh) * (c0 * (1.0 + 3.0 * c1 * square))
    dgate = (dot_nt(g, w_out[...]) * slope).astype(bf16)
    hidden_ref[...] = hidden
    dgate_ref[...] = dgate
    part_ref[...] = dot(hidden, w_out[...]).astype(bf16)
    dn_ref[...] = dot_nt(dgate, w_in[...]).astype(bf16)

    @pl.when(pl.program_id(0) == 0)
    def _():
        db_in[...] = jnp.zeros_like(db_in)
        db_out[...] = jnp.zeros_like(db_out)

    db_in[...] += jnp.sum(dgate.astype(f32), 0, keepdims=True)
    db_out[...] += jnp.sum(g.astype(f32), 0, keepdims=True)


def mlp(c, count, rows, normed, g, w_in, b_in, w_out, before, after):
    total, width = g.shape
    ff = w_in.shape[1]
    there = lambda w: pl.BlockSpec((rows, w), lambda i: (c * count + i, 0))
    here = lambda w: pl.BlockSpec((rows, w), lambda i: (i, 0))
    one = lambda w: pl.BlockSpec((1, w), lambda i: (0, 0))
    ins = (normed, g, w_in, b_in, w_out)
    specs = [there(width), there(width), whole(w_in), whole(b_in), whole(w_out)]
    alias = {}
    if before is not None:
        alias = {len(ins): 0, len(ins) + 1: 1}
        ins, specs = ins + tuple(before), specs + [anywhere] * 2
    return call(
        mlp_kernel,
        (count,),
        ins,
        specs,
        [there(ff), there(ff), here(width), here(width), one(ff), one(width)],
        [
            shape_of(total, ff),
            shape_of(total, ff),
            shape_of(count * rows, width),
            shape_of(count * rows, width),
            shape_of(1, ff, dtype=f32),
            shape_of(1, width, dtype=f32),
        ],
        5,
        after,
        alias=alias,
        vmem=32,
    )


def dense_grads_kernel(core_ref, n_ref, dgate_ref, hidden_ref, g_ref, give_ref, keep_ref):
    step, half = pl.program_id(0), pl.num_programs(0) // 2
    both = dot_tn(n_ref[...], dgate_ref[...]).astype(bf16), dot_tn(hidden_ref[...], g_ref[...]).astype(bf16)

    @pl.when(step < half)
    def _():
        give_ref[0], give_ref[1] = both

    @pl.when(step >= half)
    def _():
        keep_ref[0], keep_ref[1] = both


def halves(steps, rows, wide, slots):
    half = steps // 2

    def place(i, core):
        return jnp.where(i < half, (1 - core[0]) * half + i, core[0] * half + i - half)

    cols = lambda total: pl.BlockSpec((total, rows), lambda i, core: (0, place(i, core)))
    give = pl.BlockSpec((slots, rows, wide), lambda i, core: (0, jnp.minimum(i, half - 1), 0))
    keep = pl.BlockSpec((slots, rows, wide), lambda i, core: (0, jnp.maximum(i - half, 0), 0))
    return cols, [give, keep]


def dense_grads(core, normed, dgate, hidden, g, loose, steps=4):
    total, width = g.shape
    cols, outs = halves(steps, width // steps, width, 2)
    return call(
        dense_grads_kernel,
        (steps,),
        (normed, dgate, hidden, g),
        [cols(total), whole(dgate), cols(total), whole(g)],
        outs,
        [shape_of(2, width // 2, width)] * 2,
        6,
        scalars=(core,),
        after=loose,
    )


def post_kernel(place_ref, back_ref, x_ref, part_ref, dn_ref, b_out, wq, wk, wv, wo, cosine, sine, *rest):
    give_ref, keep_ref, flat_ref, dgain, dbias = rest[-5:]
    tables = signed(cosine[...], sine[...])
    lane = lax.broadcasted_iota(jnp.int32, tables[0].shape, 1)
    inner = wo.shape[0]
    for tile in range(inner // 128):
        even, odd = back_ref[2 * tile].astype(f32), back_ref[2 * tile + 1].astype(f32)
        lows = half_swap(even[:, 0:128], odd[:, 0:128], lane, True)
        dq = half_swap(even[:, 0:128], odd[:, 0:128], lane, False)
        dk = half_swap(even[:, 128:256], odd[:, 128:256], lane, True)
        dv = half_swap(even[:, 128:256], odd[:, 128:256], lane, False)
        dq = rope_tile(dq, tables[0], -tables[1], -tables[2])
        dk = rope_tile(dk, tables[0], -tables[1], -tables[2])
        for which, value in enumerate((lows, dq, dk, dv)):
            at = which * inner + tile * 128
            flat_ref[:, at : at + 128] = value.astype(bf16)
    x = x_ref[0].astype(f32)
    z = place_ref[1]
    first = (z == 0).astype(f32)
    mixed = dot(flat_ref[:, 0:inner], wo[...]) + part_ref[...].astype(f32) + first * (x + b_out[...])
    dn = dn_ref[...].astype(f32)
    for which, w in enumerate((wq, wk, wv)):
        at = (which + 1) * inner
        dn = dn + dot_nt(flat_ref[:, at : at + inner], w[...])
    unit, _ = unit_rows(x)
    odd = z % 2 == 1
    half = dn.shape[0] // 2
    for which, share in enumerate((dn, mixed)):
        top, bottom = share[:half].astype(bf16), share[half:].astype(bf16)
        give_ref[0, which] = jnp.where(odd, top, bottom)
        keep_ref[0, which] = jnp.where(odd, bottom, top)

    @pl.when(pl.program_id(0) == 0)
    def _():
        dgain[...] = jnp.zeros_like(dgain)
        dbias[...] = jnp.zeros_like(dbias)

    dgain[...] += jnp.sum(dn * unit, 0, keepdims=True)
    dbias[...] += jnp.sum(dn, 0, keepdims=True)


def post(c, count, place, back, x, part, dn, consts, tables, before, after):
    seqs, rows, width = x.shape
    inner = consts[1].shape[1]
    heads = inner // HEAD_DIM
    here = pl.BlockSpec((rows, width), lambda i, _: (i, 0))
    one = pl.BlockSpec((1, width), lambda i, _: (0, 0))
    ins = (back, x, part, dn) + consts + tables
    specs = [
        pl.BlockSpec((heads, rows, 4 * HEAD_DIM), lambda i, _: (i, 0, 0)),
        pl.BlockSpec((1, rows, width), lambda i, _: (c * count + i, 0, 0)),
        here,
        here,
    ]
    specs += [whole(w) for w in consts] + [mine(rows)] * 2
    alias = {}
    if before is not None:
        alias = {len(ins): 2}
        ins, specs = ins + (before,), specs + [anywhere]
    share_spec = pl.BlockSpec((1, 2, rows // 2, width), lambda i, place: (i ^ (place[1] // 2), 0, 0, 0))
    return call(
        post_kernel,
        (count,),
        ins,
        specs,
        [share_spec] * 2 + [pl.BlockSpec((rows, 4 * inner), lambda i, _: (c * count + i, 0)), one, one],
        [shape_of(count, 2, rows // 2, width)] * 2
        + [shape_of(seqs * rows, 4 * inner)]
        + [shape_of(1, width, dtype=f32)] * 2,
        4,
        after,
        (place,),
        alias=alias,
    )


def head_grads_kernel(core_ref, n_ref, g_ref, flat_ref, small_ref, give_ref, keep_ref, *, inner):
    step, half = pl.program_id(0), pl.num_programs(0) // 2
    out = dot_tn(g_ref[...], flat_ref[:, 0:inner])
    rest = dot_tn(n_ref[...], flat_ref[:, inner:])

    @pl.when(step < half)
    def _():
        give_ref[0, :, 0:inner] = out.astype(bf16)
        give_ref[0, :, inner:] = rest.astype(bf16)

    @pl.when(step >= half)
    def _():
        give_ref[0, 0 : small_ref.shape[0]] = small_ref[...]
        keep_ref[0, :, 0:inner] = out.astype(bf16)
        keep_ref[0, :, inner:] = rest.astype(bf16)


def head_grads(core, normed, g, flat, small, after, steps=4):
    total, width = g.shape
    wide = flat.shape[1]
    rows, half = width // steps, steps // 2
    cols, (_, keep) = halves(steps, rows, wide, 1)
    give = pl.BlockSpec((1, rows, wide), lambda i, core: (0, jnp.minimum(i, half), 0))
    return call(
        partial(head_grads_kernel, inner=wide // 4),
        (steps,),
        (normed, g, flat, small),
        [cols(total), cols(total), whole(flat), whole(small)],
        [give, keep],
        [shape_of(1, (half + 1) * rows, wide), shape_of(1, half * rows, wide)],
        4,
        after,
        (core,),
    )


def split_kernel(keep_ref, got_ref, *rest, small):
    out_ref, token_ref = rest[-2:]
    token_ref[...] = jnp.zeros_like(token_ref)
    rows = keep_ref.shape[1]
    out_ref[0, :, 0:rows] = (keep_ref[...].astype(f32) + got_ref[...].astype(f32)).astype(bf16)
    if small:
        own, got = rest[0], rest[1]
        out_ref[0, 0, rows:] = (own[...].astype(f32) + got[0].astype(f32)).astype(bf16)


def split(keep, got, small, chips, after):
    slots, total, wide = keep.shape
    rows = total // chips
    block = pl.BlockSpec((slots, rows, wide), lambda k: (0, k, 0))
    ins, specs, extra = (keep, got), [block, block], 0
    if small is not None:
        extra = small.shape[0]
        ins += (small, got)
        specs += [whole(small), pl.BlockSpec((1, extra, wide), lambda k: (0, total // extra, 0))]
    return call(
        partial(split_kernel, small=extra > 0),
        (chips,),
        ins,
        specs,
        [pl.BlockSpec((1, slots, rows + extra, wide), lambda k: (k, 0, 0, 0)), pl.BlockSpec((8, 128), lambda k: (0, 0))],
        [shape_of(chips, slots, rows + extra, wide), shape_of(8, 128, dtype=f32)],
        2,
        after,
        vmem=16,
    )


def parted_kernel(chip_ref, keep_ref, got_ref, *outs):
    outs[-1][...] = jnp.zeros_like(outs[-1])
    total = (keep_ref[...].astype(f32) + got_ref[...].astype(f32)).astype(bf16)
    for k, out in enumerate(outs[:-1]):

        @pl.when(pl.program_id(0) == k)
        def _():
            out[...] = total


def parted(chip, keep, got, chips, after):
    slots, rows, wide = keep.shape
    rows = rows // chips
    block = pl.BlockSpec((slots, rows, wide), lambda k, chip: (0, chip[0] ^ k, 0))
    one = pl.BlockSpec((slots, rows, wide), lambda k, chip: (0, 0, 0))
    return call(
        parted_kernel,
        (chips,),
        (keep, got),
        [block, block],
        [one] * chips + [pl.BlockSpec((8, 128), lambda k, chip: (0, 0))],
        [shape_of(slots, rows, wide)] * chips + [shape_of(8, 128, dtype=f32)],
        2,
        after,
        (chip,),
        vmem=16,
    )


def joined_kernel(*refs):
    parts, (out_ref, token_ref) = refs[:-2], refs[-2:]
    token_ref[...] = jnp.zeros_like(token_ref)
    total = parts[0][...].astype(f32)
    for part in parts[1:]:
        total = total + part[...].astype(f32)
    for k in range(out_ref.shape[0]):
        out_ref[k] = total.astype(bf16)


def joined(parts, after):
    slots, rows, wide = parts[0].shape
    block = pl.BlockSpec((1, rows, wide // 2), lambda i: (i // 2, 0, i % 2))
    return call(
        joined_kernel,
        (2 * slots,),
        tuple(parts),
        [block] * len(parts),
        [
            pl.BlockSpec((len(parts), 1, rows, wide // 2), lambda i: (0, i // 2, 0, i % 2)),
            pl.BlockSpec((8, 128), lambda i: (0, 0)),
        ],
        [shape_of(len(parts), slots, rows, wide), shape_of(8, 128, dtype=f32)],
        2,
        after,
        vmem=16,
    )


def total_kernel(parts_ref, out_ref, token_ref):
    token_ref[...] = jnp.zeros_like(token_ref)
    total = parts_ref[0].astype(f32)
    for k in range(1, parts_ref.shape[0]):
        total = total + parts_ref[k].astype(f32)
    for k in range(out_ref.shape[0]):
        out_ref[k] = total.astype(bf16)


def total(parts, copies, loose):
    chips, slots, rows, wide = parts.shape
    steps = 2 * slots
    block = lambda n: pl.BlockSpec((n, 1, rows, wide // 2), lambda i: (0, i // 2, 0, i % 2))
    return call(
        total_kernel,
        (steps,),
        (parts,),
        [block(chips)],
        [block(copies), pl.BlockSpec((8, 128), lambda i: (0, 0))],
        [shape_of(copies, slots, rows, wide), shape_of(8, 128, dtype=f32)],
        2,
        vmem=16,
        after=loose,
    )


def widened(at_ref, own_ref, other_ref, stage, in_sems, take):
    chips = own_ref.shape[0]
    loads = [
        pltpu.make_async_copy((own_ref, other_ref)[i // chips].at[i % chips], stage.at[i], in_sems.at[i])
        for i in range(2 * chips)
    ]
    for load in loads:
        load.start()
    stores = []
    for i, load in enumerate(loads):
        load.wait()
        spot = (at_ref[0] ^ (i // chips)) * chips + (at_ref[1] ^ (i % chips))
        for store in take(i, spot):
            store.start()
            stores.append(store)
    for store in stores:
        store.wait()


def dense_outs_kernel(at_ref, own_ref, other_ref, out_in, out_out, stage, wide_stage, in_sems, out_sems):
    rows = stage.shape[2]

    def take(i, spot):
        for which, out in enumerate((out_in, out_out)):
            wide_stage[i, which] = stage[i, which].astype(f32)
            here = out.at[pl.ds(spot * rows, rows)]
            yield pltpu.make_async_copy(wide_stage.at[i, which], here, out_sems.at[i, which])

    widened(at_ref, own_ref, other_ref, stage, in_sems, take)


def head_outs_kernel(at_ref, own_ref, other_ref, out_t, out_q, out_k, out_v, stage, turned, wide_stage, in_sems, out_sems):
    rows, inner = wide_stage.shape[2:]

    def take(i, spot):
        here = pl.ds(spot * rows, rows)
        turned[i] = stage[i, 0, 0:rows, 0:inner].astype(f32).T
        yield pltpu.make_async_copy(turned.at[i], out_t.at[:, here], out_sems.at[i, 0])
        for which, out in enumerate((out_q, out_k, out_v)):
            cols = slice((which + 1) * inner, (which + 2) * inner)
            wide_stage[i, which] = stage[i, 0, 0:rows, cols].astype(f32)
            yield pltpu.make_async_copy(wide_stage.at[i, which], out.at[here], out_sems.at[i, which + 1])

    widened(at_ref, own_ref, other_ref, stage, in_sems, take)


def dense_outs(at, own, other, width, after):
    chips, slots, rows, wide = own.shape
    dma = pltpu.SemaphoreType.DMA
    return call(
        dense_outs_kernel,
        (1,),
        (own, other),
        [anywhere] * 2,
        [anywhere] * 2,
        [shape_of(width, wide, dtype=f32)] * 2,
        4,
        after,
        (at,),
        [
            pltpu.VMEM((2 * chips, slots, rows, wide), bf16),
            pltpu.VMEM((2 * chips, slots, rows, wide), f32),
            dma((2 * chips,)),
            dma((2 * chips, slots)),
        ],
        vmem=20,
    )


def head_outs(at, own, other, width, after):
    chips, slots, tall, wide = own.shape
    rows, inner = width // (2 * chips), wide // 4
    dma = pltpu.SemaphoreType.DMA
    return call(
        head_outs_kernel,
        (1,),
        (own, other),
        [anywhere] * 2,
        [anywhere] * 4,
        [shape_of(inner, width, dtype=f32)] + [shape_of(width, inner, dtype=f32)] * 3,
        3,
        after,
        (at,),
        [
            pltpu.VMEM((2 * chips, slots, tall, wide), bf16),
            pltpu.VMEM((2 * chips, inner, rows), f32),
            pltpu.VMEM((2 * chips, 3, rows, inner), f32),
            dma((2 * chips,)),
            dma((2 * chips, 4)),
        ],
        vmem=16,
    )


def input_grad(x, g, dn, gain):
    unit, inv_std = unit_rows(x.astype(f32))
    du = dn.astype(f32) * gain
    d = inv_std * (du - jnp.mean(du, -1, keepdims=True) - unit * jnp.mean(du * unit, -1, keepdims=True))
    return (g.astype(f32) + d).astype(bf16)


def pair_sum_kernel(keep_ref, got_ref, own_ref, other_ref):
    for at, ref in enumerate((own_ref, other_ref)):

        @pl.when(pl.program_id(0) == at)
        def _():
            ref[...] = (keep_ref[0].astype(f32) + got_ref[0].astype(f32)).astype(bf16)


def pair_sum(keep, got, after):
    _, _, rows, width = keep.shape
    block = pl.BlockSpec((1, 2, rows, width), lambda i: (i, 0, 0, 0))
    out = pl.BlockSpec((2, rows, width), lambda i: (0, 0, 0))
    return call(
        pair_sum_kernel, (2,), (keep, got), [block, block], [out, out], [shape_of(2, rows, width)] * 2, 1, after, vmem=12
    )


def own_quarter_kernel(place_ref, x_ref, g_ref, own_ref, got_ref, gain, *outs):
    total = own_ref[...].astype(f32) + got_ref[...].astype(f32)
    tokens = input_grad(x_ref[0], g_ref[0], total[0], gain[...])
    mixed = total[1].astype(bf16)
    for ref in outs:
        ref[0] = tokens
        ref[1] = mixed


def own_quarter(place, start, x, g, own, got, gain, copies, loose):
    _, rows, width = own.shape
    per = x.shape[1] // rows
    block = pl.BlockSpec((1, rows, width), lambda i, place: (start + place[1] // per, place[1] % per, 0))
    return call(
        own_quarter_kernel,
        (1,),
        (x, g, own, got, gain),
        [block, block, whole(own), whole(got), whole(gain)],
        [pl.BlockSpec(own.shape, lambda i, _: (0, 0, 0))] * copies,
        [shape_of(*own.shape)] * copies,
        2,
        scalars=(place,),
        vmem=12,
        after=loose,
    )


def placed_kernel(place_ref, *refs, pieces, start):
    tokens_ref, mixed_ref, stage, in_sems, out_sems = refs[-5:]
    rows = stage.shape[2]
    per = tokens_ref.shape[1] // rows
    loads = [pltpu.make_async_copy(ref, stage.at[at], in_sems.at[at]) for at, ref in enumerate(refs[:pieces])]
    for load in loads:
        load.start()
    stores = []
    for at, load in enumerate(loads):
        load.wait()
        quarter = place_ref[1] ^ at
        spot = start + quarter // per, pl.ds((quarter % per) * rows, rows)
        for which, out in enumerate((tokens_ref, mixed_ref)):
            stores.append(pltpu.make_async_copy(stage.at[at, which], out.at[spot], out_sems.at[at, which]))
            stores[-1].start()
    for store in stores:
        store.wait()


def placed(place, shape, start, pieces, before, after):
    ins, alias, count = tuple(pieces), {}, len(pieces)
    if before is not None:
        alias = {count: 0, count + 1: 1}
        ins += tuple(before)
    dma = pltpu.SemaphoreType.DMA
    return call(
        partial(placed_kernel, pieces=count, start=start),
        (1,),
        ins,
        [anywhere] * len(ins),
        [anywhere, anywhere],
        [shape_of(*shape)] * 2,
        2,
        after,
        (place,),
        [pltpu.VMEM((count,) + pieces[0].shape, bf16), dma((count,)), dma((count, 2))],
        alias,
        vmem=6,
    )


def exchanged(x, bits):
    return lax.ppermute(x, "seq", [(i, i ^ bits) for i in range(lax.axis_size("seq"))])


def by_pairs(
    tokens, ln_gain, ln_bias, w_query, w_key, w_value, w_attn_out, w_in, b_in, w_mlp_out, b_out, cotangent
):
    x, cot = tokens[0], cotangent[0]
    seqs, rows, width = x.shape
    inner = w_query.shape[1]
    ff = w_in.shape[1]
    heads = inner // HEAD_DIM
    shards = lax.axis_size("seq")
    count = shards // heads
    in_hbm.clear()
    in_hbm.add(x, cot, w_query, w_key, w_value, w_attn_out, w_in, w_mlp_out)
    row = lambda v: v.reshape(1, -1)
    gain, bias, b_in, b_out = row(ln_gain), row(ln_bias), row(b_in), row(b_out)
    in_hbm.add(gain, bias, b_in, b_out)
    flat_cot = cot.reshape(-1, width)
    in_hbm.add(flat_cot)
    shard = lax.axis_index("seq").astype(jnp.int32)
    core, chip, chips = (shard % 2).reshape(1), (shard // 2).reshape(1), shards // 2
    z = lax.axis_index("mlp").astype(jnp.int32)
    place = jnp.stack([shard, z])
    tables = tuple(map(jnp.asarray, position_tables(shards * rows)))
    in_hbm.add(*tables)
    weights = (w_query, w_key, w_value, w_attn_out)
    pre_consts = (gain, bias) + weights
    post_consts = (b_out,) + weights

    def attend(sent, after):
        done = attention(sent.reshape(1, shards * rows, 4 * HEAD_DIM), after)
        return done.reshape(shards, rows, 4 * HEAD_DIM)

    def traded(v):
        return lax.all_to_all(v, "seq", 0, 0, tiled=True)

    def over_line(v, bits):
        return lax.ppermute(v, "mlp", [(i, i ^ bits) for i in range(4)])

    dense_args = (flat_cot, w_in, b_in, w_mlp_out)
    normed, packed_a = pre(0, count, place, x, cot, pre_consts, tables, None)
    sent_a = traded(packed_a)
    normed, *packed_b = pre(1, count, place, x, cot, pre_consts, tables, normed, chips)
    hidden, dgate, part_a, dn_a, db_in_a, db_out_a = mlp(0, count, rows, normed, *dense_args, None, (normed,))
    done_a = attend(sent_a, (db_in_a,))
    back_a = traded(done_a)
    hidden, dgate, part_b, dn_b, db_in_b, db_out_b = mlp(1, count, rows, normed, *dense_args, (hidden, dgate), (done_a,))
    packed_b = [fence(v, db_in_b) for v in packed_b]
    same = [packed_b[0]] + [exchanged(packed_b[k], 2 * k) for k in (1, 2, 3)]
    beside = exchanged(packed_b[0], 1)
    give_a, keep_a, flat, gain_a, bias_a = post(
        0, count, place, back_a, x, part_a, dn_a, post_consts, tables, None, (db_in_b,)
    )
    same = [same[0]] + [fence(v, gain_a) for v in same[1:]]
    got_a = over_line(give_a, 1)
    other = [beside] + [exchanged(v, 1) for v in same[1:]]
    done_b = attention_of(shard.reshape(1), same, other, (gain_a,))
    done_b = done_b.reshape(shards, rows, 4 * HEAD_DIM)
    back_b = traded(done_b)
    give_e, keep_e = dense_grads(core, normed, dgate, hidden, flat_cot, (done_b,))
    got_e = exchanged(give_e, 1)
    own_a, other_a = pair_sum(keep_a, got_a, (keep_e,))
    got_a = over_line(other_a, 2)
    give_b, keep_b, flat, gain_b, bias_b = post(
        1, count, place, back_b, x, part_b, dn_b, post_consts, tables, flat, (own_a,)
    )

    def over_chips(v):
        same_core = [list(range(side, shards, 2)) for side in (0, 1)]
        return lax.all_to_all(v, "seq", 0, 0, axis_index_groups=same_core, tiled=True)

    *dense, token = parted(chip, keep_e, got_e, chips, (gain_b,))
    dense = [dense[0]] + [exchanged(dense[k], 2 * k) for k in range(1, chips)]
    small = jnp.concatenate([gain_a + gain_b, bias_a + bias_b, db_in_a + db_in_b, db_out_a + db_out_b], 0)
    small = jnp.concatenate([small, jnp.zeros((12, width), f32)], 0).astype(bf16)
    give_l, keep_l = head_grads(core, normed, flat_cot, flat, small, (token,))
    got_l = exchanged(give_l, 1)
    done_a, more_a, again_a = own_quarter(place, 0, x, cot, own_a, got_a, gain, 3, (keep_l,))
    got_l = fence(got_l, more_a)
    head, token = split(keep_l, got_l, small, chips, (more_a,))
    head = over_chips(head)
    far_a = over_line(done_a, 2)
    got_b = over_line(give_b, 1)
    own_b, other_b = pair_sum(keep_b, got_b, (token,))
    near_a = over_line(fence(again_a, own_b), 1)
    got_b = over_line(other_b, 2)
    dense[1] = fence(dense[1], own_b)
    dense[2] = fence(dense[2], dense[1])
    dense, token = joined(dense, (dense[2],))
    head, token = total(head, chips, (token,))
    dense = over_chips(fence(dense, token))
    far_a = fence(far_a, token)
    beside_a = over_line(far_a, 1)
    done_b, more_b = own_quarter(place, count, x, cot, own_b, got_b, gain, 2, (far_a,))
    near_b = over_line(done_b, 1)
    far_b = over_line(more_b, 2)
    small = head[0, 0, -small.shape[0] :].astype(f32)
    dense = fence(dense, done_b)
    vectors = fence(small[:2], dense)
    head = over_chips(fence(head, dense))
    dense_other = exchanged(dense, 1)
    near_a = fence(near_a, dense)
    vectors_got = over_line(vectors, 1)
    beside_a = fence(beside_a, near_a)
    d_tokens, mixed = placed(place, x.shape, 0, (more_a, near_a, far_a, beside_a), None, (beside_a,))
    far_b = fence(far_b, d_tokens)
    beside_b = over_line(far_b, 1)
    dense_other = fence(dense_other, far_b)
    d_in, d_out = dense_outs(jnp.concatenate([core, jnp.zeros_like(core)]), dense, dense_other, width, (far_b,))
    vectors = vectors + fence(vectors_got, d_out)
    vectors_got = over_line(vectors, 2)
    head = fence(head, d_out)
    head_other = exchanged(head, 1)
    head_other = fence(head_other, d_out)
    d_attn_out, d_query, d_key, d_value = head_outs(
        jnp.concatenate([core, jnp.zeros_like(core)]), head, head_other, width, (d_out,)
    )
    vectors = vectors + fence(vectors_got, d_value)
    near_b = fence(near_b, vectors)
    beside_b = fence(beside_b, near_b)
    d_tokens, mixed = placed(place, x.shape, count, (more_b, near_b, far_b, beside_b), (d_tokens, mixed), (beside_b,))
    return (
        mixed.reshape(tokens.shape),
        d_tokens[None],
        vectors[0],
        vectors[1],
        d_query,
        d_key,
        d_value,
        d_attn_out,
        d_in,
        small[2],
        d_out,
        small[3],
    )


def per_device(
    tokens, ln_gain, ln_bias, w_query, w_key, w_value, w_attn_out, w_in, b_in, w_mlp_out, b_out, cotangent
):
    _, seqs, rows, width = tokens.shape
    inner = w_query.shape[1]
    heads = inner // HEAD_DIM
    shards = lax.axis_size("seq")
    fits = shards == 8 and lax.axis_size("mlp") == 4 and seqs * heads == 2 * shards and shards % heads == 0
    fits = fits and inner % 128 == 0 and rows % 256 == 0 and width % 1024 == 0 and w_in.shape[1] == width
    fits = fits and 4 * inner == width
    plan = by_pairs if fits else by_ring
    return plan(
        tokens, ln_gain, ln_bias, w_query, w_key, w_value, w_attn_out, w_in, b_in, w_mlp_out, b_out, cotangent
    )


def solution(mesh):
    rows, whole = P("seq", None, None, None), P()
    cols, down = P(None, "mlp"), P("mlp", None)
    return jax.shard_map(
        per_device,
        mesh=mesh,
        in_specs=(rows, whole, whole, cols, cols, cols, down, cols, P("mlp"), down, whole, rows),
        out_specs=(rows, rows, whole, whole, cols, cols, cols, down, cols, P("mlp"), down, whole),
        check_vma=False,
    )
```

```python
from functools import partial

import jax
import jax.numpy as jnp
import numpy as np
from jax import lax
from jax.experimental import pallas as pl
from jax.experimental.pallas import tpu as pltpu
from jax.sharding import PartitionSpec as P

HEAD_DIM = 64
ROT = 32

epsilon = 1e-05
neg_big = -1e30
bf16 = jnp.bfloat16
f32 = jnp.float32


def passed_along(x, axis, by):
    peers = lax.axis_size(axis)
    pairs = [(i, i + by) for i in range(peers) if 0 <= i + by < peers]
    return lax.ppermute(x, axis, pairs)


def rotary_tables(positions, width):
    column = jnp.arange(width, dtype=jnp.int32) % HEAD_DIM
    pairs = (column // 2).astype(f32)
    freq = 10000.0 ** (-2.0 * pairs / ROT)
    angle = positions.astype(f32)[:, None] * freq[None, :]
    active = (column < ROT)[None, :]
    even = (column % 2 == 0)[None, :]
    cosine = jnp.where(active, jnp.cos(angle), 1.0)
    sine = jnp.where(active, jnp.sin(angle), 0.0)
    return cosine, jnp.where(even, -sine, 0.0), jnp.where(even, 0.0, sine)


def rotate(v, tables, sign):
    cosine, from_right, from_left = tables
    right = jnp.concatenate([v[..., 1:], v[..., :1]], -1)
    left = jnp.concatenate([v[..., -1:], v[..., :-1]], -1)
    return v * cosine + sign * (right * from_right + left * from_left)


def attention_kernel(x_ref, out_ref, xt, acc, sbuf, *, length, hd, tq, tk):
    xt[...] = x_ref[0].T
    scale = hd**-0.5
    nt = (((1,), (1,)), ((), ()))
    zero = jnp.zeros((hd, tq), bf16)

    def put(old, new, q0, join):
        if old is None:
            return new
        if q0 == 0:
            return join(old, new)
        return jnp.concatenate([old[:, :q0], join(old[:, q0:], new)], 1)

    add = lambda u, v: u + v
    for i in range(length // tq):
        first = i * tq
        qs = (xt[0:hd, first : first + tq].astype(f32) * scale).astype(bf16)
        at = xt[3 * hd : 4 * hd, first : first + tq].astype(f32)
        zq = jnp.concatenate([zero, qs], 0)
        qz = jnp.concatenate([qs, zero], 0)
        steps = [(k0, k0 + tk, 0) for k0 in range(0, first, tk)]
        steps += [(first + q0, first + q0 + tk // 2, q0) for q0 in range(0, tq, tk // 2)]
        top = None
        for k0, k1, q0 in steps:
            st = jnp.dot(x_ref[0, k0:k1, 0 : 2 * hd], zq[:, q0:], preferred_element_type=f32)
            if k0 >= first:
                kp = lax.broadcasted_iota(jnp.int32, st.shape, 0)
                qp = lax.broadcasted_iota(jnp.int32, st.shape, 1)
                st = jnp.where(kp <= qp, st, neg_big)
            sbuf[k0:k1, q0:] = st
            top = put(top, jnp.max(st, 0, keepdims=True), q0, jnp.maximum)
        tot = None
        ot = None
        for k0, k1, q0 in steps:
            e = jnp.exp(sbuf[k0:k1, q0:] - top[:, q0:])
            sbuf[k0:k1, q0:] = e
            tot = put(tot, jnp.sum(e, 0, keepdims=True), q0, add)
            ot = put(ot, jnp.dot(xt[2 * hd : 3 * hd, k0:k1], e.astype(bf16), preferred_element_type=f32), q0, add)
        r = 1.0 / tot
        ot = ot * r
        ar = (at * r).astype(bf16)
        spread = jnp.sum(ar.astype(f32) * ot, 0, keepdims=True)
        az = jnp.concatenate([ar, zero], 0)
        za = jnp.concatenate([zero, ar], 0)
        dqt = None
        for k0, k1, q0 in steps:
            dp = jnp.dot(x_ref[0, k0:k1, 2 * hd : 4 * hd], az[:, q0:], preferred_element_type=f32)
            e = sbuf[k0:k1, q0:]
            ds = (e * (dp - spread[:, q0:])).astype(bf16)
            dqt = put(dqt, jnp.dot(xt[hd : 2 * hd, k0:k1], ds, preferred_element_type=f32), q0, add)
            both = lax.dot_general(ds, qz[:, q0:], nt, preferred_element_type=f32) + lax.dot_general(
                e.astype(bf16), za[:, q0:], nt, preferred_element_type=f32
            )
            if k0 < first:
                both = acc[k0:k1, :] + both
            acc[k0:k1, :] = both
        both = jnp.concatenate([ot, dqt * scale], 0)
        out_ref[0, first : first + tq, 0 : 2 * hd] = both.T.astype(bf16)
    out_ref[0, :, 2 * hd : 4 * hd] = acc[...].astype(bf16)


def attention(x, after=()):
    n, length, width = x.shape
    hd = width // 4
    tq = 512 if length % 512 == 0 else 256
    spec = pl.BlockSpec((1, length, width), lambda i: (i, 0, 0))
    return call(
        partial(attention_kernel, length=length, hd=hd, tq=tq, tk=512),
        (n,),
        (x,),
        [spec],
        spec,
        shape_of(*x.shape),
        7,
        after,
        scratch=[pltpu.VMEM((width, length), bf16), pltpu.VMEM((length, 2 * hd), f32), pltpu.VMEM((length, tq), f32)],
        vmem=32,
        free_out=(0,),
    )


def gathered_kernel(shard_ref, *refs, parts, **sizes):
    x_ref = refs[parts + 1]
    rows = refs[0].shape[1]
    for k in range(parts):
        x_ref[0, pl.ds((shard_ref[0] ^ k) * rows, rows)] = refs[k][0]
    attention_kernel(x_ref, refs[parts], *refs[parts + 2 :], **sizes)


def attention_of(shard, same, other, after=()):
    _, rows, width = same[0].shape
    length, hd = 2 * rows * len(same), width // 4
    tq = 512 if length % 512 == 0 else 256
    specs = [pl.BlockSpec((1, rows, width), lambda i, _, side=side: (side, 0, 0)) for side in (0, 1)]
    return call(
        partial(gathered_kernel, parts=2 * len(same), length=length, hd=hd, tq=tq, tk=512),
        (1,),
        tuple(v for pair in zip(same, other) for v in pair),
        specs * len(same),
        pl.BlockSpec((1, length, width), lambda i, _: (0, 0, 0)),
        shape_of(1, length, width),
        7,
        after,
        (shard,),
        [
            pltpu.VMEM((1, length, width), bf16),
            pltpu.VMEM((width, length), bf16),
            pltpu.VMEM((length, 2 * hd), f32),
            pltpu.VMEM((length, tq), f32),
        ],
        vmem=32,
        free_out=(0,),
    )


def ring_attention(q, k, v, a):
    seq_count, row_count, inner_width = q.shape
    score_scale = HEAD_DIM ** (-0.5)
    shard_total = lax.axis_size("seq")
    my_shard = lax.axis_index("seq")
    heads_of = lambda x: x.reshape(seq_count, row_count, inner_width // HEAD_DIM, HEAD_DIM)
    flat_of = lambda x: x.reshape(seq_count, row_count, inner_width)
    qh, gh = heads_of(q), heads_of(a)
    local = jnp.arange(row_count, dtype=jnp.int32)
    own_mask = local[:, None] >= local[None, :]
    ein = partial(jnp.einsum, preferred_element_type=f32)

    def attend_block(state, key_block, value_block, visible):
        running_max, exp_total, weighted = state
        raw = ein("sthd,suhd->shtu", qh, key_block) * score_scale
        raw = jnp.where(visible[None, None], raw, neg_big)
        new_max = jnp.maximum(running_max, jnp.max(raw, -1))
        weights = jnp.where(visible[None, None], jnp.exp(raw - new_max[..., None]), 0.0)
        shrink = jnp.exp(running_max - new_max)
        exp_total = exp_total * shrink + jnp.sum(weights, -1)
        weighted = weighted * jnp.transpose(shrink, (0, 2, 1))[..., None] + ein(
            "shtu,suhd->sthd", weights.astype(bf16), value_block
        )
        return (new_max, exp_total, weighted)

    head_count = inner_width // HEAD_DIM
    state = (
        jnp.full((seq_count, head_count, row_count), neg_big, f32),
        jnp.zeros((seq_count, head_count, row_count), f32),
        jnp.zeros(qh.shape, f32),
    )
    state = attend_block(state, heads_of(k), heads_of(v), own_mask)
    empty_stack = jnp.zeros((max(shard_total - 1, 1),) + q.shape, bf16)

    def forward_step(step, carry):
        state, near_keys, near_values, key_stack, value_stack = carry
        near_keys, near_values = passed_along((near_keys, near_values), "seq", 1)
        visible = jnp.broadcast_to(my_shard >= step, (row_count, row_count))
        state = attend_block(state, heads_of(near_keys), heads_of(near_values), visible)
        key_stack = lax.dynamic_update_index_in_dim(key_stack, near_keys, step - 1, 0)
        value_stack = lax.dynamic_update_index_in_dim(value_stack, near_values, step - 1, 0)
        return (state, near_keys, near_values, key_stack, value_stack)

    state, _, _, key_stack, value_stack = lax.fori_loop(
        1, shard_total, forward_step, (state, k, v, empty_stack, empty_stack)
    )
    running_max, exp_total, weighted = state
    log_total = running_max + jnp.log(exp_total)
    attended = weighted / jnp.transpose(exp_total, (0, 2, 1))[..., None]
    spread = jnp.transpose(jnp.sum(gh.astype(f32) * attended, -1), (0, 2, 1))

    def grads(key_block, value_block, visible):
        raw = ein("sthd,suhd->shtu", qh, key_block) * score_scale
        probs = jnp.where(visible[None, None], jnp.exp(raw - log_total[..., None]), 0.0)
        grad_probs = ein("sthd,suhd->shtu", gh, value_block)
        slopes = (probs * (grad_probs - spread[..., None])).astype(bf16)
        query_grad = ein("shtu,suhd->sthd", slopes, key_block) * score_scale
        key_grad = ein("shtu,sthd->suhd", slopes, qh) * score_scale
        value_grad = ein("shtu,sthd->suhd", probs.astype(bf16), gh)
        return query_grad, key_grad, value_grad

    d_query, d_keys, d_values = grads(heads_of(k), heads_of(v), own_mask)

    def return_step(index, carry):
        query_grad_total, travelling = carry
        step = shard_total - 1 - index
        near_keys = lax.dynamic_index_in_dim(key_stack, step - 1, 0, keepdims=False)
        near_values = lax.dynamic_index_in_dim(value_stack, step - 1, 0, keepdims=False)
        visible = jnp.broadcast_to(my_shard >= step, (row_count, row_count))
        query_grad, key_grad, value_grad = grads(heads_of(near_keys), heads_of(near_values), visible)
        joined = jnp.concatenate([flat_of(key_grad), flat_of(value_grad)], -1)
        travelling = passed_along((travelling + joined).astype(bf16), "seq", -1).astype(f32)
        return (query_grad_total + query_grad, travelling)

    start = jnp.zeros((seq_count, row_count, 2 * inner_width), f32)
    d_query, travelling = lax.fori_loop(0, shard_total - 1, return_step, (d_query, start))
    d_keys = flat_of(d_keys) + travelling[..., :inner_width]
    d_values = flat_of(d_values) + travelling[..., inner_width:]
    return tuple(x.astype(bf16) for x in (flat_of(attended), flat_of(d_query), d_keys, d_values))


def by_ring(
    tokens, ln_gain, ln_bias, w_query, w_key, w_value, w_attn_out, w_in, b_in, w_mlp_out, b_out, cotangent
):
    x_low = tokens[0]
    cot = cotangent[0]
    seqs, rows, width = x_low.shape
    inner = w_query.shape[1]
    my_shard = lax.axis_index("seq")
    ein = partial(jnp.einsum, preferred_element_type=f32)
    positions = my_shard * rows + jnp.arange(rows, dtype=jnp.int32)
    tables = rotary_tables(positions, inner)
    x = x_low.astype(f32)
    centred = x - jnp.mean(x, -1, keepdims=True)
    inv_std = lax.rsqrt(jnp.mean(centred * centred, -1, keepdims=True) + epsilon)
    unit = centred * inv_std
    normed = (unit * ln_gain + ln_bias).astype(bf16)
    query = rotate(ein("std,de->ste", normed, w_query), tables, 1.0).astype(bf16)
    keys = rotate(ein("std,de->ste", normed, w_key), tables, 1.0).astype(bf16)
    values = ein("std,de->ste", normed, w_value).astype(bf16)
    d_attended = ein("std,ed->ste", cot, w_attn_out).astype(bf16)

    attended, d_query, d_keys, d_values = ring_attention(query, keys, values, d_attended)

    gate_in = ein("std,df->stf", normed, w_in) + b_in
    hidden, gelu_pull = jax.vjp(partial(jax.nn.gelu, approximate=True), gate_in)
    hidden = hidden.astype(bf16)
    d_hidden = ein("std,fd->stf", cot, w_mlp_out)
    d_gate = gelu_pull(d_hidden)[0].astype(bf16)
    d_b_in = jnp.sum(d_gate, (0, 1), dtype=f32)
    d_b_out = jnp.sum(cot, (0, 1), dtype=f32)
    d_w_mlp_out = ein("stf,std->fd", hidden, cot)
    d_w_in = ein("std,stf->df", normed, d_gate)
    mlp_part = ein("stf,fd->std", hidden, w_mlp_out)
    d_normed_mlp = ein("stf,df->std", d_gate, w_in)

    attn_part = ein("ste,ed->std", attended, w_attn_out)
    branches = lax.psum((attn_part + mlp_part).astype(bf16), "mlp").astype(f32)
    mixed = (x + branches + b_out).astype(bf16)
    d_w_attn_out = ein("ste,std->ed", attended, cot)
    d_query_pre = rotate(d_query.astype(f32), tables, -1.0).astype(bf16)
    d_key_pre = rotate(d_keys.astype(f32), tables, -1.0).astype(bf16)
    d_w_query = ein("std,ste->de", normed, d_query_pre)
    d_w_key = ein("std,ste->de", normed, d_key_pre)
    d_w_value = ein("std,ste->de", normed, d_values)
    d_normed_part = d_normed_mlp + ein("ste,de->std", d_query_pre, w_query)
    d_normed_part = d_normed_part + ein("ste,de->std", d_key_pre, w_key)
    d_normed_part = d_normed_part + ein("ste,de->std", d_values, w_value)
    d_normed = lax.psum(d_normed_part.astype(bf16), "mlp").astype(f32)
    d_gain = jnp.sum(d_normed * unit, (0, 1))
    d_bias = jnp.sum(d_normed, (0, 1))
    d_unit = d_normed * ln_gain
    d_inputs = inv_std * (
        d_unit - jnp.mean(d_unit, -1, keepdims=True) - unit * jnp.mean(d_unit * unit, -1, keepdims=True)
    )
    d_tokens = (cot.astype(f32) + d_inputs).astype(bf16)

    def total(v):
        return lax.psum(v.astype(bf16), "seq").astype(f32)

    return (
        mixed[None],
        d_tokens[None],
        total(d_gain),
        total(d_bias),
        total(d_w_query),
        total(d_w_key),
        total(d_w_value),
        total(d_w_attn_out),
        total(d_w_in),
        total(d_b_in),
        total(d_w_mlp_out),
        total(d_b_out),
    )


anywhere = pl.BlockSpec(memory_space=pl.ANY)


class Placed(list):
    def add(self, *arrays):
        self.extend(arrays)

    def pin(self, x):
        return pltpu.with_memory_space_constraint(x, pltpu.HBM) if any(x is y for y in self) else x


in_hbm = Placed()


def call(
    kernel, grid, ins, in_specs, out_specs, out_shape, us, after=(), scalars=(), scratch=(), alias=None, vmem=24, free_out=()
):
    used = len(scalars) + len(ins)

    def body(*refs):
        kernel(*refs[:used], *refs[used + len(after) :])

    one = not isinstance(out_shape, list)
    shapes = [out_shape] if one else out_shape
    shapes = [s if i in free_out else pltpu.HBM(s.shape, s.dtype) for i, s in enumerate(shapes)]
    results = pl.pallas_call(
        body,
        name=getattr(kernel, "func", kernel).__name__.strip("<>"),
        grid_spec=pltpu.PrefetchScalarGridSpec(
            num_scalar_prefetch=len(scalars),
            grid=grid,
            in_specs=list(in_specs) + [anywhere] * len(after),
            out_specs=out_specs,
            scratch_shapes=list(scratch),
        ),
        out_shape=shapes[0] if one else shapes,
        input_output_aliases={len(scalars) + k: v for k, v in (alias or {}).items()},
        compiler_params=pltpu.CompilerParams(vmem_limit_bytes=vmem * 2**20),
        cost_estimate=pl.CostEstimate(flops=int(us * 1e11), bytes_accessed=0, transcendentals=0),
    )(*scalars, *map(in_hbm.pin, ins), *map(in_hbm.pin, after))
    in_hbm.add(*[r for i, r in enumerate([results] if one else results) if i not in free_out])
    return results


def fence(x, *after):
    known = any(x is y for y in in_hbm)
    return call(
        lambda *refs: None,
        (1,),
        (x,),
        [anywhere],
        anywhere,
        shape_of(*x.shape, dtype=x.dtype),
        1,
        after,
        alias={0: 0},
        vmem=1,
        free_out=() if known else (0,),
    )


def dot(a, b):
    return jnp.dot(a, b, preferred_element_type=f32)


def dot_nt(a, b):
    return lax.dot_general(a, b, (((1,), (1,)), ((), ())), preferred_element_type=f32)


def dot_tn(a, b):
    return lax.dot_general(a, b, (((0,), (0,)), ((), ())), preferred_element_type=f32)


def whole(x):
    return pl.BlockSpec(x.shape, lambda *_: (0,) * x.ndim, pipeline_mode=pl.Buffered(1))


def mine(rows):
    return pl.BlockSpec((rows, 2 * HEAD_DIM), lambda i, at: (at[0], 0), pipeline_mode=pl.Buffered(1))


def shape_of(*shape, dtype=bf16):
    return jax.ShapeDtypeStruct(shape, dtype)


def unit_rows(x):
    average = jnp.mean(x, -1, keepdims=True)
    centred = x - average
    inv_std = lax.rsqrt(jnp.mean(centred * centred, -1, keepdims=True) + epsilon)
    return centred * inv_std, inv_std


def half_swap(low, high, lane, keep_low):
    if keep_low:
        return jnp.where(lane < HEAD_DIM, low, pltpu.roll(high, HEAD_DIM, 1))
    return jnp.where(lane < HEAD_DIM, pltpu.roll(low, HEAD_DIM, 1), high)


def rope_tile(v, cosine, from_right, from_left):
    width = v.shape[1]
    return v * cosine + pltpu.roll(v, width - 1, 1) * from_right + pltpu.roll(v, 1, 1) * from_left


def position_tables(total):
    column = np.arange(2 * HEAD_DIM) % HEAD_DIM
    freq = np.float32(10000.0) ** (np.float32(-2.0 / ROT) * (column // 2).astype(np.float32))
    angle = np.arange(total, dtype=np.float32)[:, None] * freq.astype(np.float32)[None, :]
    active = (column < ROT)[None, :]
    cosine = np.where(active, np.cos(angle.astype(np.float64)), 1.0).astype(np.float32)
    sine = np.where(active, np.sin(angle.astype(np.float64)), 0.0).astype(np.float32)
    return cosine, sine


def signed(cosine, sine):
    even = lax.broadcasted_iota(jnp.int32, sine.shape, 1) % 2 == 0
    return cosine, jnp.where(even, -sine, 0.0), jnp.where(even, 0.0, sine)


def pre_kernel(shard_ref, x_ref, g_ref, gain, bias, wq, wk, wv, wo, cosine, sine, *rest, partners):
    if partners:
        normed_ref, packed_ref = rest[-2 - partners], rest[-1]
        outs = rest[-1 - partners : -1]
    else:
        normed_ref, packed_ref = rest[-2:]
    unit, _ = unit_rows(x_ref[0].astype(f32))
    normed = (unit * gain[...] + bias[...]).astype(bf16)
    normed_ref[...] = normed
    q, k, v = dot(normed, wq[...]), dot(normed, wk[...]), dot(normed, wv[...])
    a = dot_nt(g_ref[0], wo[...])
    tables = signed(cosine[...], sine[...])
    lane = lax.broadcasted_iota(jnp.int32, tables[0].shape, 1)
    for tile in range(q.shape[1] // 128):
        cols = slice(tile * 128, (tile + 1) * 128)
        qt, kt = rope_tile(q[:, cols], *tables), rope_tile(k[:, cols], *tables)
        for side in (0, 1):
            head = tile * 2 + side
            packed_ref[head, :, 0:128] = half_swap(qt, kt, lane, side == 0).astype(bf16)
            packed_ref[head, :, 128:256] = half_swap(v[:, cols], a[:, cols], lane, side == 0).astype(bf16)
    for k in range(partners):
        for side in range(2):
            pair = shard_ref[0] ^ (2 * k + side)
            heads = packed_ref.shape[0]

            @pl.when(pair // heads == pl.program_id(0))
            def _():
                outs[k][side] = packed_ref[pair % heads]


def pre(c, count, shard, x, g, consts, tables, before, partners=0):
    seqs, rows, width = x.shape
    heads = consts[2].shape[1] // HEAD_DIM
    by_seq = pl.BlockSpec((1, rows, width), lambda i, _: (c * count + i, 0, 0))
    ins, specs = (x, g) + consts + tables, [by_seq, by_seq] + [whole(w) for w in consts] + [mine(rows)] * 2
    alias = {}
    if before is not None:
        alias = {len(ins): 0}
        ins, specs = ins + (before,), specs + [anywhere]
    blocks = pl.BlockSpec((heads, rows, 4 * HEAD_DIM), lambda i, _: (i, 0, 0))
    shapes = [shape_of(count * heads, rows, 4 * HEAD_DIM)]
    scratch = []
    if partners:
        shapes = [shape_of(2, rows, 4 * HEAD_DIM)] * partners
        scratch = [pltpu.VMEM((heads, rows, 4 * HEAD_DIM), bf16)]
        blocks = pl.BlockSpec((2, rows, 4 * HEAD_DIM), lambda i, _: (0, 0, 0))
    return call(
        partial(pre_kernel, partners=partners),
        (count,),
        ins,
        specs,
        [
            pl.BlockSpec((rows, width), lambda i, _: (c * count + i, 0)),
        ]
        + [blocks] * len(shapes),
        [shape_of(seqs * rows, width)] + shapes,
        3,
        scalars=(shard,),
        alias=alias,
        scratch=scratch,
        free_out=range(1, 1 + len(shapes)),
    )


def mlp_kernel(n_ref, g_ref, w_in, b_in, w_out, *rest):
    hidden_ref, dgate_ref, part_ref, dn_ref, db_in, db_out = rest[-6:]
    c0, c1 = 0.7978845608028654, 0.044715
    g = g_ref[...]
    gate = dot(n_ref[...], w_in[...]) + b_in[...]
    square = gate * gate
    tanh = jnp.tanh(c0 * gate * (1.0 + c1 * square))
    left = 0.5 * (1.0 + tanh)
    hidden = (gate * left).astype(bf16)
    slope = left + 0.5 * gate * (1.0 - tanh * tanh) * (c0 * (1.0 + 3.0 * c1 * square))
    dgate = (dot_nt(g, w_out[...]) * slope).astype(bf16)
    hidden_ref[...] = hidden
    dgate_ref[...] = dgate
    part_ref[...] = dot(hidden, w_out[...]).astype(bf16)
    dn_ref[...] = dot_nt(dgate, w_in[...]).astype(bf16)

    @pl.when(pl.program_id(0) == 0)
    def _():
        db_in[...] = jnp.zeros_like(db_in)
        db_out[...] = jnp.zeros_like(db_out)

    db_in[...] += jnp.sum(dgate.astype(f32), 0, keepdims=True)
    db_out[...] += jnp.sum(g.astype(f32), 0, keepdims=True)


def mlp(c, count, rows, normed, g, w_in, b_in, w_out, before, after):
    total, width = g.shape
    ff = w_in.shape[1]
    there = lambda w: pl.BlockSpec((rows, w), lambda i: (c * count + i, 0))
    here = lambda w: pl.BlockSpec((rows, w), lambda i: (i, 0))
    one = lambda w: pl.BlockSpec((1, w), lambda i: (0, 0))
    ins = (normed, g, w_in, b_in, w_out)
    specs = [there(width), there(width), whole(w_in), whole(b_in), whole(w_out)]
    alias = {}
    if before is not None:
        alias = {len(ins): 0, len(ins) + 1: 1}
        ins, specs = ins + tuple(before), specs + [anywhere] * 2
    return call(
        mlp_kernel,
        (count,),
        ins,
        specs,
        [there(ff), there(ff), here(width), here(width), one(ff), one(width)],
        [
            shape_of(total, ff),
            shape_of(total, ff),
            shape_of(count * rows, width),
            shape_of(count * rows, width),
            shape_of(1, ff, dtype=f32),
            shape_of(1, width, dtype=f32),
        ],
        5,
        after,
        alias=alias,
        vmem=32,
    )


def dense_grads_kernel(core_ref, n_ref, dgate_ref, hidden_ref, g_ref, give_ref, keep_ref):
    step, half = pl.program_id(0), pl.num_programs(0) // 2
    both = dot_tn(n_ref[...], dgate_ref[...]).astype(bf16), dot_tn(hidden_ref[...], g_ref[...]).astype(bf16)

    @pl.when(step < half)
    def _():
        give_ref[0], give_ref[1] = both

    @pl.when(step >= half)
    def _():
        keep_ref[0], keep_ref[1] = both


def halves(steps, rows, wide, slots):
    half = steps // 2

    def place(i, core):
        return jnp.where(i < half, (1 - core[0]) * half + i, core[0] * half + i - half)

    cols = lambda total: pl.BlockSpec((total, rows), lambda i, core: (0, place(i, core)))
    give = pl.BlockSpec((slots, rows, wide), lambda i, core: (0, jnp.minimum(i, half - 1), 0))
    keep = pl.BlockSpec((slots, rows, wide), lambda i, core: (0, jnp.maximum(i - half, 0), 0))
    return cols, [give, keep]


def dense_grads(core, normed, dgate, hidden, g, loose, steps=4):
    total, width = g.shape
    cols, outs = halves(steps, width // steps, width, 2)
    return call(
        dense_grads_kernel,
        (steps,),
        (normed, dgate, hidden, g),
        [cols(total), whole(dgate), cols(total), whole(g)],
        outs,
        [shape_of(2, width // 2, width)] * 2,
        6,
        scalars=(core,),
        after=loose,
    )


def post_kernel(place_ref, back_ref, x_ref, part_ref, dn_ref, b_out, wq, wk, wv, wo, cosine, sine, *rest):
    give_ref, keep_ref, flat_ref, dgain, dbias = rest[-5:]
    tables = signed(cosine[...], sine[...])
    lane = lax.broadcasted_iota(jnp.int32, tables[0].shape, 1)
    inner = wo.shape[0]
    for tile in range(inner // 128):
        even, odd = back_ref[2 * tile].astype(f32), back_ref[2 * tile + 1].astype(f32)
        lows = half_swap(even[:, 0:128], odd[:, 0:128], lane, True)
        dq = half_swap(even[:, 0:128], odd[:, 0:128], lane, False)
        dk = half_swap(even[:, 128:256], odd[:, 128:256], lane, True)
        dv = half_swap(even[:, 128:256], odd[:, 128:256], lane, False)
        dq = rope_tile(dq, tables[0], -tables[1], -tables[2])
        dk = rope_tile(dk, tables[0], -tables[1], -tables[2])
        for which, value in enumerate((lows, dq, dk, dv)):
            at = which * inner + tile * 128
            flat_ref[:, at : at + 128] = value.astype(bf16)
    x = x_ref[0].astype(f32)
    z = place_ref[1]
    first = (z == 0).astype(f32)
    mixed = dot(flat_ref[:, 0:inner], wo[...]) + part_ref[...].astype(f32) + first * (x + b_out[...])
    dn = dn_ref[...].astype(f32)
    for which, w in enumerate((wq, wk, wv)):
        at = (which + 1) * inner
        dn = dn + dot_nt(flat_ref[:, at : at + inner], w[...])
    unit, _ = unit_rows(x)
    odd = z % 2 == 1
    half = dn.shape[0] // 2
    for which, share in enumerate((dn, mixed)):
        top, bottom = share[:half].astype(bf16), share[half:].astype(bf16)
        give_ref[0, which] = jnp.where(odd, top, bottom)
        keep_ref[0, which] = jnp.where(odd, bottom, top)

    @pl.when(pl.program_id(0) == 0)
    def _():
        dgain[...] = jnp.zeros_like(dgain)
        dbias[...] = jnp.zeros_like(dbias)

    dgain[...] += jnp.sum(dn * unit, 0, keepdims=True)
    dbias[...] += jnp.sum(dn, 0, keepdims=True)


def post(c, count, place, back, x, part, dn, consts, tables, before, after):
    seqs, rows, width = x.shape
    inner = consts[1].shape[1]
    heads = inner // HEAD_DIM
    here = pl.BlockSpec((rows, width), lambda i, _: (i, 0))
    one = pl.BlockSpec((1, width), lambda i, _: (0, 0))
    ins = (back, x, part, dn) + consts + tables
    specs = [
        pl.BlockSpec((heads, rows, 4 * HEAD_DIM), lambda i, _: (i, 0, 0)),
        pl.BlockSpec((1, rows, width), lambda i, _: (c * count + i, 0, 0)),
        here,
        here,
    ]
    specs += [whole(w) for w in consts] + [mine(rows)] * 2
    alias = {}
    if before is not None:
        alias = {len(ins): 2}
        ins, specs = ins + (before,), specs + [anywhere]
    share_spec = pl.BlockSpec((1, 2, rows // 2, width), lambda i, place: (i ^ (place[1] // 2), 0, 0, 0))
    return call(
        post_kernel,
        (count,),
        ins,
        specs,
        [share_spec] * 2 + [pl.BlockSpec((rows, 4 * inner), lambda i, _: (c * count + i, 0)), one, one],
        [shape_of(count, 2, rows // 2, width)] * 2
        + [shape_of(seqs * rows, 4 * inner)]
        + [shape_of(1, width, dtype=f32)] * 2,
        4,
        after,
        (place,),
        alias=alias,
    )


def head_grads_kernel(core_ref, n_ref, g_ref, flat_ref, small_ref, give_ref, keep_ref, *, inner):
    step, half = pl.program_id(0), pl.num_programs(0) // 2
    out = dot_tn(g_ref[...], flat_ref[:, 0:inner])
    rest = dot_tn(n_ref[...], flat_ref[:, inner:])

    @pl.when(step < half)
    def _():
        give_ref[0, :, 0:inner] = out.astype(bf16)
        give_ref[0, :, inner:] = rest.astype(bf16)

    @pl.when(step >= half)
    def _():
        give_ref[0, 0 : small_ref.shape[0]] = small_ref[...]
        keep_ref[0, :, 0:inner] = out.astype(bf16)
        keep_ref[0, :, inner:] = rest.astype(bf16)


def head_grads(core, normed, g, flat, small, after, steps=4):
    total, width = g.shape
    wide = flat.shape[1]
    rows, half = width // steps, steps // 2
    cols, (_, keep) = halves(steps, rows, wide, 1)
    give = pl.BlockSpec((1, rows, wide), lambda i, core: (0, jnp.minimum(i, half), 0))
    return call(
        partial(head_grads_kernel, inner=wide // 4),
        (steps,),
        (normed, g, flat, small),
        [cols(total), cols(total), whole(flat), whole(small)],
        [give, keep],
        [shape_of(1, (half + 1) * rows, wide), shape_of(1, half * rows, wide)],
        4,
        after,
        (core,),
    )


def split_kernel(keep_ref, got_ref, *rest, small):
    out_ref, token_ref = rest[-2:]
    token_ref[...] = jnp.zeros_like(token_ref)
    rows = keep_ref.shape[1]
    out_ref[0, :, 0:rows] = (keep_ref[...].astype(f32) + got_ref[...].astype(f32)).astype(bf16)
    if small:
        own, got = rest[0], rest[1]
        out_ref[0, 0, rows:] = (own[...].astype(f32) + got[0].astype(f32)).astype(bf16)


def split(keep, got, small, chips, after):
    slots, total, wide = keep.shape
    rows = total // chips
    block = pl.BlockSpec((slots, rows, wide), lambda k: (0, k, 0))
    ins, specs, extra = (keep, got), [block, block], 0
    if small is not None:
        extra = small.shape[0]
        ins += (small, got)
        specs += [whole(small), pl.BlockSpec((1, extra, wide), lambda k: (0, total // extra, 0))]
    return call(
        partial(split_kernel, small=extra > 0),
        (chips,),
        ins,
        specs,
        [pl.BlockSpec((1, slots, rows + extra, wide), lambda k: (k, 0, 0, 0)), pl.BlockSpec((8, 128), lambda k: (0, 0))],
        [shape_of(chips, slots, rows + extra, wide), shape_of(8, 128, dtype=f32)],
        2,
        after,
        vmem=16,
    )


def parted_kernel(chip_ref, keep_ref, got_ref, *outs):
    outs[-1][...] = jnp.zeros_like(outs[-1])
    total = (keep_ref[...].astype(f32) + got_ref[...].astype(f32)).astype(bf16)
    for k, out in enumerate(outs[:-1]):

        @pl.when(pl.program_id(0) == k)
        def _():
            out[...] = total


def parted(chip, keep, got, chips, after):
    slots, rows, wide = keep.shape
    rows = rows // chips
    block = pl.BlockSpec((slots, rows, wide), lambda k, chip: (0, chip[0] ^ k, 0))
    one = pl.BlockSpec((slots, rows, wide), lambda k, chip: (0, 0, 0))
    return call(
        parted_kernel,
        (chips,),
        (keep, got),
        [block, block],
        [one] * chips + [pl.BlockSpec((8, 128), lambda k, chip: (0, 0))],
        [shape_of(slots, rows, wide)] * chips + [shape_of(8, 128, dtype=f32)],
        2,
        after,
        (chip,),
        vmem=16,
    )


def joined_kernel(*refs):
    parts, (out_ref, token_ref) = refs[:-2], refs[-2:]
    token_ref[...] = jnp.zeros_like(token_ref)
    total = parts[0][...].astype(f32)
    for part in parts[1:]:
        total = total + part[...].astype(f32)
    for k in range(out_ref.shape[0]):
        out_ref[k] = total.astype(bf16)


def joined(parts, after):
    slots, rows, wide = parts[0].shape
    block = pl.BlockSpec((1, rows, wide // 2), lambda i: (i // 2, 0, i % 2))
    return call(
        joined_kernel,
        (2 * slots,),
        tuple(parts),
        [block] * len(parts),
        [
            pl.BlockSpec((len(parts), 1, rows, wide // 2), lambda i: (0, i // 2, 0, i % 2)),
            pl.BlockSpec((8, 128), lambda i: (0, 0)),
        ],
        [shape_of(len(parts), slots, rows, wide), shape_of(8, 128, dtype=f32)],
        2,
        after,
        vmem=16,
    )


def total_kernel(parts_ref, out_ref, token_ref):
    token_ref[...] = jnp.zeros_like(token_ref)
    total = parts_ref[0].astype(f32)
    for k in range(1, parts_ref.shape[0]):
        total = total + parts_ref[k].astype(f32)
    for k in range(out_ref.shape[0]):
        out_ref[k] = total.astype(bf16)


def total(parts, copies, loose):
    chips, slots, rows, wide = parts.shape
    steps = 2 * slots
    block = lambda n: pl.BlockSpec((n, 1, rows, wide // 2), lambda i: (0, i // 2, 0, i % 2))
    return call(
        total_kernel,
        (steps,),
        (parts,),
        [block(chips)],
        [block(copies), pl.BlockSpec((8, 128), lambda i: (0, 0))],
        [shape_of(copies, slots, rows, wide), shape_of(8, 128, dtype=f32)],
        2,
        vmem=16,
        after=loose,
    )


def widened(at_ref, own_ref, other_ref, stage, in_sems, take):
    chips = own_ref.shape[0]
    loads = [
        pltpu.make_async_copy((own_ref, other_ref)[i // chips].at[i % chips], stage.at[i], in_sems.at[i])
        for i in range(2 * chips)
    ]
    for load in loads:
        load.start()
    stores = []
    for i, load in enumerate(loads):
        load.wait()
        spot = (at_ref[0] ^ (i // chips)) * chips + (at_ref[1] ^ (i % chips))
        for store in take(i, spot):
            store.start()
            stores.append(store)
    for store in stores:
        store.wait()


def dense_outs_kernel(at_ref, own_ref, other_ref, out_in, out_out, stage, wide_stage, in_sems, out_sems):
    rows = stage.shape[2]

    def take(i, spot):
        for which, out in enumerate((out_in, out_out)):
            wide_stage[i, which] = stage[i, which].astype(f32)
            here = out.at[pl.ds(spot * rows, rows)]
            yield pltpu.make_async_copy(wide_stage.at[i, which], here, out_sems.at[i, which])

    widened(at_ref, own_ref, other_ref, stage, in_sems, take)


def head_outs_kernel(at_ref, own_ref, other_ref, out_t, out_q, out_k, out_v, stage, turned, wide_stage, in_sems, out_sems):
    rows, inner = wide_stage.shape[2:]

    def take(i, spot):
        here = pl.ds(spot * rows, rows)
        turned[i] = stage[i, 0, 0:rows, 0:inner].astype(f32).T
        yield pltpu.make_async_copy(turned.at[i], out_t.at[:, here], out_sems.at[i, 0])
        for which, out in enumerate((out_q, out_k, out_v)):
            cols = slice((which + 1) * inner, (which + 2) * inner)
            wide_stage[i, which] = stage[i, 0, 0:rows, cols].astype(f32)
            yield pltpu.make_async_copy(wide_stage.at[i, which], out.at[here], out_sems.at[i, which + 1])

    widened(at_ref, own_ref, other_ref, stage, in_sems, take)


def dense_outs(at, own, other, width, after):
    chips, slots, rows, wide = own.shape
    dma = pltpu.SemaphoreType.DMA
    return call(
        dense_outs_kernel,
        (1,),
        (own, other),
        [anywhere] * 2,
        [anywhere] * 2,
        [shape_of(width, wide, dtype=f32)] * 2,
        4,
        after,
        (at,),
        [
            pltpu.VMEM((2 * chips, slots, rows, wide), bf16),
            pltpu.VMEM((2 * chips, slots, rows, wide), f32),
            dma((2 * chips,)),
            dma((2 * chips, slots)),
        ],
        vmem=20,
    )


def head_outs(at, own, other, width, after):
    chips, slots, tall, wide = own.shape
    rows, inner = width // (2 * chips), wide // 4
    dma = pltpu.SemaphoreType.DMA
    return call(
        head_outs_kernel,
        (1,),
        (own, other),
        [anywhere] * 2,
        [anywhere] * 4,
        [shape_of(inner, width, dtype=f32)] + [shape_of(width, inner, dtype=f32)] * 3,
        3,
        after,
        (at,),
        [
            pltpu.VMEM((2 * chips, slots, tall, wide), bf16),
            pltpu.VMEM((2 * chips, inner, rows), f32),
            pltpu.VMEM((2 * chips, 3, rows, inner), f32),
            dma((2 * chips,)),
            dma((2 * chips, 4)),
        ],
        vmem=16,
    )


def input_grad(x, g, dn, gain):
    unit, inv_std = unit_rows(x.astype(f32))
    du = dn.astype(f32) * gain
    d = inv_std * (du - jnp.mean(du, -1, keepdims=True) - unit * jnp.mean(du * unit, -1, keepdims=True))
    return (g.astype(f32) + d).astype(bf16)


def pair_sum_kernel(keep_ref, got_ref, own_ref, other_ref):
    for at, ref in enumerate((own_ref, other_ref)):

        @pl.when(pl.program_id(0) == at)
        def _():
            ref[...] = (keep_ref[0].astype(f32) + got_ref[0].astype(f32)).astype(bf16)


def pair_sum(keep, got, after):
    _, _, rows, width = keep.shape
    block = pl.BlockSpec((1, 2, rows, width), lambda i: (i, 0, 0, 0))
    out = pl.BlockSpec((2, rows, width), lambda i: (0, 0, 0))
    return call(
        pair_sum_kernel, (2,), (keep, got), [block, block], [out, out], [shape_of(2, rows, width)] * 2, 1, after, vmem=12
    )


def own_quarter_kernel(place_ref, x_ref, g_ref, own_ref, got_ref, gain, *outs):
    total = own_ref[...].astype(f32) + got_ref[...].astype(f32)
    tokens = input_grad(x_ref[0], g_ref[0], total[0], gain[...])
    mixed = total[1].astype(bf16)
    for ref in outs:
        ref[0] = tokens
        ref[1] = mixed


def own_quarter(place, start, x, g, own, got, gain, copies, loose):
    _, rows, width = own.shape
    per = x.shape[1] // rows
    block = pl.BlockSpec((1, rows, width), lambda i, place: (start + place[1] // per, place[1] % per, 0))
    return call(
        own_quarter_kernel,
        (1,),
        (x, g, own, got, gain),
        [block, block, whole(own), whole(got), whole(gain)],
        [pl.BlockSpec(own.shape, lambda i, _: (0, 0, 0))] * copies,
        [shape_of(*own.shape)] * copies,
        2,
        scalars=(place,),
        vmem=12,
        after=loose,
    )


def placed_kernel(place_ref, *refs, pieces, start):
    tokens_ref, mixed_ref, stage, in_sems, out_sems = refs[-5:]
    rows = stage.shape[2]
    per = tokens_ref.shape[1] // rows
    loads = [pltpu.make_async_copy(ref, stage.at[at], in_sems.at[at]) for at, ref in enumerate(refs[:pieces])]
    for load in loads:
        load.start()
    stores = []
    for at, load in enumerate(loads):
        load.wait()
        quarter = place_ref[1] ^ at
        spot = start + quarter // per, pl.ds((quarter % per) * rows, rows)
        for which, out in enumerate((tokens_ref, mixed_ref)):
            stores.append(pltpu.make_async_copy(stage.at[at, which], out.at[spot], out_sems.at[at, which]))
            stores[-1].start()
    for store in stores:
        store.wait()


def placed(place, shape, start, pieces, before, after):
    ins, alias, count = tuple(pieces), {}, len(pieces)
    if before is not None:
        alias = {count: 0, count + 1: 1}
        ins += tuple(before)
    dma = pltpu.SemaphoreType.DMA
    return call(
        partial(placed_kernel, pieces=count, start=start),
        (1,),
        ins,
        [anywhere] * len(ins),
        [anywhere, anywhere],
        [shape_of(*shape)] * 2,
        2,
        after,
        (place,),
        [pltpu.VMEM((count,) + pieces[0].shape, bf16), dma((count,)), dma((count, 2))],
        alias,
        vmem=6,
    )


def exchanged(x, bits):
    return lax.ppermute(x, "seq", [(i, i ^ bits) for i in range(lax.axis_size("seq"))])


def by_pairs(
    tokens, ln_gain, ln_bias, w_query, w_key, w_value, w_attn_out, w_in, b_in, w_mlp_out, b_out, cotangent
):
    x, cot = tokens[0], cotangent[0]
    seqs, rows, width = x.shape
    inner = w_query.shape[1]
    ff = w_in.shape[1]
    heads = inner // HEAD_DIM
    shards = lax.axis_size("seq")
    count = shards // heads
    in_hbm.clear()
    in_hbm.add(x, cot, w_query, w_key, w_value, w_attn_out, w_in, w_mlp_out)
    row = lambda v: v.reshape(1, -1)
    gain, bias, b_in, b_out = row(ln_gain), row(ln_bias), row(b_in), row(b_out)
    in_hbm.add(gain, bias, b_in, b_out)
    flat_cot = cot.reshape(-1, width)
    in_hbm.add(flat_cot)
    shard = lax.axis_index("seq").astype(jnp.int32)
    core, chip, chips = (shard % 2).reshape(1), (shard // 2).reshape(1), shards // 2
    z = lax.axis_index("mlp").astype(jnp.int32)
    place = jnp.stack([shard, z])
    tables = tuple(map(jnp.asarray, position_tables(shards * rows)))
    in_hbm.add(*tables)
    weights = (w_query, w_key, w_value, w_attn_out)
    pre_consts = (gain, bias) + weights
    post_consts = (b_out,) + weights

    def attend(sent, after):
        done = attention(sent.reshape(1, shards * rows, 4 * HEAD_DIM), after)
        return done.reshape(shards, rows, 4 * HEAD_DIM)

    def traded(v):
        return lax.all_to_all(v, "seq", 0, 0, tiled=True)

    def over_line(v, bits):
        return lax.ppermute(v, "mlp", [(i, i ^ bits) for i in range(4)])

    dense_args = (flat_cot, w_in, b_in, w_mlp_out)
    normed, packed_a = pre(0, count, place, x, cot, pre_consts, tables, None)
    sent_a = traded(packed_a)
    normed, *packed_b = pre(1, count, place, x, cot, pre_consts, tables, normed, chips)
    hidden, dgate, part_a, dn_a, db_in_a, db_out_a = mlp(0, count, rows, normed, *dense_args, None, (normed,))
    done_a = attend(sent_a, (db_in_a,))
    back_a = traded(done_a)
    hidden, dgate, part_b, dn_b, db_in_b, db_out_b = mlp(1, count, rows, normed, *dense_args, (hidden, dgate), (done_a,))
    packed_b = [fence(v, db_in_b) for v in packed_b]
    same = [packed_b[0]] + [exchanged(packed_b[k], 2 * k) for k in (1, 2, 3)]
    beside = exchanged(packed_b[0], 1)
    give_a, keep_a, flat, gain_a, bias_a = post(
        0, count, place, back_a, x, part_a, dn_a, post_consts, tables, None, (db_in_b,)
    )
    same = [same[0]] + [fence(v, gain_a) for v in same[1:]]
    got_a = over_line(give_a, 1)
    other = [beside] + [exchanged(v, 1) for v in same[1:]]
    done_b = attention_of(shard.reshape(1), same, other, (gain_a,))
    done_b = done_b.reshape(shards, rows, 4 * HEAD_DIM)
    back_b = traded(done_b)
    give_e, keep_e = dense_grads(core, normed, dgate, hidden, flat_cot, (done_b,))
    got_e = exchanged(give_e, 1)
    own_a, other_a = pair_sum(keep_a, got_a, (keep_e,))
    got_a = over_line(other_a, 2)
    give_b, keep_b, flat, gain_b, bias_b = post(
        1, count, place, back_b, x, part_b, dn_b, post_consts, tables, flat, (own_a,)
    )

    def over_chips(v):
        same_core = [list(range(side, shards, 2)) for side in (0, 1)]
        return lax.all_to_all(v, "seq", 0, 0, axis_index_groups=same_core, tiled=True)

    *dense, token = parted(chip, keep_e, got_e, chips, (gain_b,))
    dense = [dense[0]] + [exchanged(dense[k], 2 * k) for k in range(1, chips)]
    small = jnp.concatenate([gain_a + gain_b, bias_a + bias_b, db_in_a + db_in_b, db_out_a + db_out_b], 0)
    small = jnp.concatenate([small, jnp.zeros((12, width), f32)], 0).astype(bf16)
    give_l, keep_l = head_grads(core, normed, flat_cot, flat, small, (token,))
    got_l = exchanged(give_l, 1)
    done_a, more_a, again_a = own_quarter(place, 0, x, cot, own_a, got_a, gain, 3, (keep_l,))
    got_l = fence(got_l, more_a)
    head, token = split(keep_l, got_l, small, chips, (more_a,))
    head = over_chips(head)
    far_a = over_line(done_a, 2)
    got_b = over_line(give_b, 1)
    own_b, other_b = pair_sum(keep_b, got_b, (token,))
    near_a = over_line(fence(again_a, own_b), 1)
    got_b = over_line(other_b, 2)
    dense[1] = fence(dense[1], own_b)
    dense[2] = fence(dense[2], dense[1])
    dense, token = joined(dense, (dense[2],))
    head, token = total(head, chips, (token,))
    dense = over_chips(fence(dense, token))
    far_a = fence(far_a, token)
    beside_a = over_line(far_a, 1)
    done_b, more_b = own_quarter(place, count, x, cot, own_b, got_b, gain, 2, (far_a,))
    near_b = over_line(done_b, 1)
    far_b = over_line(more_b, 2)
    small = head[0, 0, -small.shape[0] :].astype(f32)
    dense = fence(dense, done_b)
    vectors = fence(small[:2], dense)
    head = over_chips(fence(head, dense))
    dense_other = exchanged(dense, 1)
    near_a = fence(near_a, dense)
    vectors_got = over_line(vectors, 1)
    beside_a = fence(beside_a, near_a)
    dense_other = fence(dense_other, beside_a)
    far_b = fence(far_b, dense_other)
    beside_b = over_line(far_b, 1)
    d_tokens, mixed = placed(place, x.shape, 0, (more_a, near_a, far_a, beside_a), None, (far_b,))
    d_in, d_out = dense_outs(jnp.concatenate([core, jnp.zeros_like(core)]), dense, dense_other, width, (d_tokens,))
    vectors = vectors + fence(vectors_got, d_out)
    vectors_got = over_line(vectors, 2)
    head = fence(head, d_out)
    head_other = exchanged(head, 1)
    head_other = fence(head_other, d_out)
    d_attn_out, d_query, d_key, d_value = head_outs(
        jnp.concatenate([core, jnp.zeros_like(core)]), head, head_other, width, (d_out,)
    )
    vectors = vectors + fence(vectors_got, d_value)
    near_b = fence(near_b, vectors)
    beside_b = fence(beside_b, near_b)
    d_tokens, mixed = placed(place, x.shape, count, (more_b, near_b, far_b, beside_b), (d_tokens, mixed), (beside_b,))
    return (
        mixed.reshape(tokens.shape),
        d_tokens[None],
        vectors[0],
        vectors[1],
        d_query,
        d_key,
        d_value,
        d_attn_out,
        d_in,
        small[2],
        d_out,
        small[3],
    )


def per_device(
    tokens, ln_gain, ln_bias, w_query, w_key, w_value, w_attn_out, w_in, b_in, w_mlp_out, b_out, cotangent
):
    _, seqs, rows, width = tokens.shape
    inner = w_query.shape[1]
    heads = inner // HEAD_DIM
    shards = lax.axis_size("seq")
    fits = shards == 8 and lax.axis_size("mlp") == 4 and seqs * heads == 2 * shards and shards % heads == 0
    fits = fits and inner % 128 == 0 and rows % 256 == 0 and width % 1024 == 0 and w_in.shape[1] == width
    fits = fits and 4 * inner == width
    plan = by_pairs if fits else by_ring
    return plan(
        tokens, ln_gain, ln_bias, w_query, w_key, w_value, w_attn_out, w_in, b_in, w_mlp_out, b_out, cotangent
    )


def solution(mesh):
    rows, whole = P("seq", None, None, None), P()
    cols, down = P(None, "mlp"), P("mlp", None)
    return jax.shard_map(
        per_device,
        mesh=mesh,
        in_specs=(rows, whole, whole, cols, cols, cols, down, cols, P("mlp"), down, whole, rows),
        out_specs=(rows, rows, whole, whole, cols, cols, cols, down, cols, P("mlp"), down, whole),
        check_vma=False,
    )
```
